256 devices in a mesh: blocks: 64 (over z, y, core), views: 4 (over x).
Axes of the slice: x: 4, y: 4, z: 8, core: 2. Of those that a mesh axis runs over, the one named last changes fastest.
Arguments:
- params: float32 [59, 131072], P(None, 'blocks'), as said below
- moment1: float32 [59, 131072], P(None, 'blocks'), may hold values from -0.046875 to 0.046875
- moment2: float32 [59, 131072], P(None, 'blocks'), may hold values from 1e-09 to 0.001
- dual: float32 [59, 65536], P(None, 'blocks'), may hold values from -4 to 4
- z_copy: float32 [59, 65536], P(None, 'blocks'), may hold values from -6 to 6
- z_table: float32 [59, 65536], P(None, 'blocks'), may hold values from -6 to 6
- boundary_rows: int32 [65536], P('blocks'), may hold values from 0 to 2047
- owner_block: int32 [65536, 1], P('blocks'), may hold values from 0 to 63; in each aligned block of 1024 rows (0 to 1023, 1024 to 2047, ...) at most 64 rows name the same one
- owner_slot: int32 [65536], P('blocks'), may hold values from 0 to 1023
- tile_lists: int32 [4096, 32], P(('blocks', 'views')), may hold values from 0 to 2047
- tile_counts: int32 [4096], P(('blocks', 'views')), may hold values from 8 to 32, as said below
- cameras: float32 [256, 24], P(('blocks', 'views'))
- target: float32 [3, 1048576], P(None, ('blocks', 'views')), may hold values from 0 to 1
Outputs:
- new_params: float32 [59, 131072], P(None, 'blocks')
- new_moment1: float32 [59, 131072], P(None, 'blocks')
- new_moment2: float32 [59, 131072], P(None, 'blocks')
- z_new: float32 [59, 65536], P(None, 'blocks')
- dual_new: float32 [59, 65536], P(None, 'blocks')
The draws below stay inside these ranges and needn't reach their ends.
Inputs may be any that keep to these rules, and one draw needn't show every extreme that they name: `tile_lists`: rows of the Gaussian lists from slot tile_counts on are padding. `tile_counts`: every device has a tile with all 32 slots live. `owner_block`: among the 1024 copies of one block at most 64 name the same owner, and some owner gets exactly 64. `params`: the quaternion's first entry is 1 or more.
All inputs are finite; a program needn't handle non-finite values.
Results may differ from the reference program's by a relative error of at most 0.0003.
Values sent between devices are 32-bit elements; how exact they have to be, the bound alone decides.
A program may use at most 64 MiB of HBM per device.

```python
import math
import jax
import jax.numpy as jnp
import numpy as np
from jax import lax

NPAR = 59
G_DEV = 2048
B_DEV = 1024
Z_DEV = 1024
TILES_DEV = 16
K = 32
V_DEV = 1
CAP = 64
G_TOT = 131072
B_TOT = 65536
Z_TOT = 65536
TILES_TOT = 4096
CAMS_TOT = 256
PIX_TOT = 1048576
N_BLOCKS = 64
N_VIEWS = 4


def draw_params(key, part):
    key = jax.random.fold_in(key, 1)
    keys = jax.random.split(key, 7)
    centre = jax.random.normal(keys[0], (3, G_TOT), jnp.float32) * 0.6
    coeffs = jax.random.normal(keys[6], (48, G_TOT), jnp.float32) * 0.3
    logs = jax.random.uniform(keys[1], (3, G_TOT), jnp.float32, -1.6, -0.4)
    head = jax.random.uniform(keys[2], (1, G_TOT), jnp.float32, 1.0, 2.0)
    rest = jax.random.normal(keys[3], (3, G_TOT), jnp.float32) * 0.5
    opacity = jax.random.normal(keys[4], (1, G_TOT), jnp.float32) * 2.0 - 1.5
    return jnp.concatenate([centre, logs, head, rest, opacity, coeffs], axis=0)


def draw_tile_counts(key, part):
    key = jax.random.fold_in(key, 2)
    counts = jax.random.randint(key, (TILES_TOT,), K // 4, K + 1)
    return counts.at[::TILES_DEV].set(K)


def draw_cameras(key, part):
    key = jax.random.fold_in(key, 3)
    keys = jax.random.split(key, 3)
    proj = jax.random.normal(keys[0], (CAMS_TOT, 6), jnp.float32) * 0.6
    shift = jax.random.uniform(keys[1], (CAMS_TOT, 2), jnp.float32, -0.3, 0.3)
    basis = jax.random.normal(keys[2], (CAMS_TOT, 16), jnp.float32) * 0.5
    return jnp.concatenate([proj, shift, basis], axis=1)


def plant(array, rng, low, largest):
    index_at = [jax.random.randint(jax.random.fold_in(rng, axis), (), 0, length) for axis, length in enumerate(array.shape)]
    main_axis = array.shape.index(max(array.shape))
    neighbour = index_at[:main_axis] + [(index_at[main_axis] + 1) % array.shape[main_axis]] + index_at[main_axis + 1:]
    return array.at[tuple(index_at)].set(low).at[tuple(neighbour)].set(largest)


def shard_levels(own_key, dims, cuts, low, largest):
    level, own = 1.0, jax.random.fold_in(own_key, 6)
    for dim, parts in cuts:
        heights = jnp.exp(jax.random.uniform(jax.random.fold_in(own, dim), (parts,), jnp.float32, low / len(cuts), largest / len(cuts)))
        level = level * jnp.repeat(heights, dims[dim] // parts).reshape([-1 if axis == dim else 1 for axis in range(len(dims))])
    return level


def routed_block(rng, own, number, rows, amount, top, reach, slope):
    sequence = jax.random.permutation(rng, amount)
    crowded, ordinary = load_shares(amount, rows * top, reach, slope, True), load_shares(amount, rows * top, reach, slope, False)
    places = jnp.arange(amount)

    def named(lengths, offset_by):
        used = int((lengths > 0).sum())
        fixed = max(1, used // 4)
        moved = fixed + (places - fixed + offset_by * (used - fixed)) % max(1, amount - fixed)
        return jnp.zeros((amount,), jnp.int32).at[sequence[jnp.where(places < fixed, places, moved)]].set(jnp.asarray(lengths, jnp.int32))

    lengths = jnp.where(number % 4 == 0, named(crowded, number // 4), named(ordinary, number - number // 4 - 1))
    mixed = jax.random.permutation(jax.random.fold_in(own, 3), amount)
    giver, receiver = mixed[0:amount // 2 * 2:2], mixed[1:amount // 2 * 2:2]
    margin = jnp.minimum(lengths[giver] - 1, reach - lengths[receiver]) // 2
    margin = jnp.where((giver == sequence[0]) | (receiver == sequence[0]) | (lengths[receiver] == 0), 0, jnp.maximum(margin, 0))
    moved = jax.random.randint(jax.random.fold_in(own, 4), (amount // 2,), 0, 1 << 20) % (margin + 1)
    lengths = lengths.at[giver].add(-moved).at[receiver].add(moved)
    items = jnp.searchsorted(jnp.cumsum(lengths), jnp.arange(rows * top), side="right").astype(jnp.int32)
    listing = items.reshape(top, rows).T
    listing = listing[jax.random.permutation(jax.random.fold_in(own, 1), rows)]
    offset_by = jax.random.randint(jax.random.fold_in(own, 2), (rows, 1), 0, top)
    return jnp.take_along_axis(listing, (jnp.arange(top)[None, :] + offset_by) % top, axis=1)


def load_shares(count, total, bound, lean, full):
    loads = [(1 << 20) // math.isqrt(grade ** lean) + 1 for grade in range(1, count + 1)]
    largest = bound if full else min(bound, max(-(-total // count), total * loads[0] // sum(loads)))
    least = 1 if total - largest >= count - 1 else 0
    holding, spare = [largest] + [least] * (count - 1), total - largest - least * (count - 1)
    while spare > 0:
        free = [i for i in range(1, count) if holding[i] < largest] or [i for i in range(1, count) if holding[i] < bound]
        whole, left = sum([loads[i] for i in free]), spare
        for i in free:
            extra = min(bound - holding[i], max(1, left * loads[i] // whole), spare)
            holding[i] = holding[i] + extra
            spare = spare - extra
    return np.array(holding)


def bell_draw(own_key, extent, spread, bound, pieces=(), kind=jnp.bfloat16):
    result = jax.random.normal(own_key, extent, jnp.float32) * spread
    if len(pieces) > 0:
        result = shard_levels(own_key, extent, pieces, -0.22, 0.18) * result
    return jnp.clip(result, min=-bound, max=bound).astype(kind)


def setup_inputs(seed: int = 0) -> dict:
    streams_of = jax.random.split(jax.random.key(seed), 14)
    params = draw_params(jax.random.fold_in(streams_of[13], 71), 0)
    moment1 = bell_draw(streams_of[1], (NPAR, G_TOT), 0.003, 0.046875, ((1, 64),), jnp.float32)
    moment2 = jnp.clip(jnp.exp(math.log(0.001) - 13.815511 * jax.random.uniform(streams_of[2], (NPAR, G_TOT), jnp.float32) ** shard_levels(streams_of[2], (NPAR, G_TOT), ((1, 64),), -0.2, 0.2)), 9.999999717180685e-10, 0.001)
    dual = bell_draw(streams_of[3], (NPAR, B_TOT), 0.3, 4.0, ((1, 64),), jnp.float32)
    z_copy = bell_draw(streams_of[4], (NPAR, B_TOT), 1.0, 6.0, ((1, 64),), jnp.float32)
    z_table = bell_draw(streams_of[5], (NPAR, Z_TOT), 1.0, 6.0, ((1, 64),), jnp.float32)
    boundary_rows = plant(jax.random.randint(streams_of[6], (B_TOT,), 0, G_DEV), jax.random.fold_in(streams_of[6], 1), 0, G_DEV - 1).astype(jnp.int32)
    owner_block_keys = jax.random.split(jax.random.fold_in(streams_of[7], 1), B_TOT // B_DEV)
    owner_block_turns = jax.random.permutation(jax.random.fold_in(streams_of[7], 3), B_TOT // B_DEV)
    owner_block = jax.vmap(lambda own, number: routed_block(jax.random.fold_in(streams_of[7], 2), own, number, B_DEV, N_BLOCKS, 1, CAP, 2))(owner_block_keys, owner_block_turns).reshape((B_TOT, 1))
    owner_slot = plant(jax.random.randint(streams_of[8], (B_TOT,), 0, Z_DEV), jax.random.fold_in(streams_of[8], 1), 0, Z_DEV - 1).astype(jnp.int32)
    tile_lists = plant(jax.random.randint(streams_of[9], (TILES_TOT, K), 0, G_DEV), jax.random.fold_in(streams_of[9], 1), 0, G_DEV - 1).astype(jnp.int32)
    tile_counts = draw_tile_counts(jax.random.fold_in(streams_of[13], 71), 0)
    cameras = draw_cameras(jax.random.fold_in(streams_of[13], 71), 0)
    target = jnp.clip(1.0 * jax.random.uniform(streams_of[12], (3, PIX_TOT), jnp.float32) ** shard_levels(streams_of[12], (3, PIX_TOT), ((1, 256),), -0.2, 0.2), 0.0, 1.0)
    return dict(params=params, moment1=moment1, moment2=moment2, dual=dual, z_copy=z_copy, z_table=z_table, boundary_rows=boundary_rows, owner_block=owner_block, owner_slot=owner_slot, tile_lists=tile_lists, tile_counts=tile_counts, cameras=cameras, target=target)


RHO = 1.0
LEARN = 0.05
BETA_ONE = 0.9
BETA_TWO = 0.999
EPSILON = 1e-08

def render_loss(params, lists, counts, cams, target):
    hp = lax.Precision.HIGHEST
    gcount = params.shape[1]
    tiles, depth = lists.shape
    nview = cams.shape[0]
    centre = params[0:3]
    scales = jnp.exp(params[3:6])
    quat = params[6:10]
    quat = quat / jnp.sqrt(lax.optimization_barrier(jnp.sum(quat * quat, axis=0)))
    qw, qx, qy, qz = (quat[0], quat[1], quat[2], quat[3])
    rot = jnp.stack([1 - 2 * (qy * qy + qz * qz), 2 * (qx * qy - qw * qz), 2 * (qx * qz + qw * qy), 2 * (qx * qy + qw * qz), 1 - 2 * (qx * qx + qz * qz), 2 * (qy * qz - qw * qx), 2 * (qx * qz - qw * qy), 2 * (qy * qz + qw * qx), 1 - 2 * (qx * qx + qy * qy)]).reshape(3, 3, gcount)
    scaled = rot * scales[None, :, :]
    proj = cams[:, 0:6].reshape(nview, 2, 3)
    mixed = jnp.einsum('vij,jkg->vikg', proj, scaled, precision=hp)
    cov = jnp.einsum('vikg,vjkg->vijg', mixed, mixed, precision=hp)
    first = cov[:, 0, 0] + 0.01
    cross = cov[:, 0, 1]
    second = cov[:, 1, 1] + 0.01
    det = first * second - cross * cross
    centre_u = jnp.einsum('vj,jg->vg', proj[:, 0, :], centre, precision=hp) + cams[:, 6:7]
    centre_w = jnp.einsum('vj,jg->vg', proj[:, 1, :], centre, precision=hp) + cams[:, 7:8]
    coeffs = params[11:59].reshape(3, 16, gcount)
    colour = jnp.einsum('vk,ckg->vcg', cams[:, 8:24], coeffs, precision=hp) + 0.5
    opacity = jnp.broadcast_to(jax.nn.sigmoid(params[10])[None, :], (nview, gcount))
    feats = jnp.stack([centre_u, centre_w, second / det, -cross / det, first / det, opacity, colour[:, 0], colour[:, 1], colour[:, 2]]).reshape(9, nview * gcount)
    tile = jnp.arange(tiles, dtype=jnp.int32)
    lookup = (tile // 16)[:, None] * gcount + lists
    picked = jnp.take(feats, lookup, axis=1)
    pixel = jnp.arange(256, dtype=jnp.int32)
    within = tile % 16
    xpos = (within % 4 * 16)[:, None] + (pixel % 16)[None, :]
    ypos = (within // 4 * 16)[:, None] + (pixel // 16)[None, :]
    coord_u = (xpos.astype(jnp.float32) + 0.5) / 32.0 - 1.0
    coord_w = (ypos.astype(jnp.float32) + 0.5) / 32.0 - 1.0
    delta_u = coord_u[:, None, :] - picked[0][:, :, None]
    delta_w = coord_w[:, None, :] - picked[1][:, :, None]
    quad = picked[2][:, :, None] * delta_u * delta_u + 2.0 * picked[3][:, :, None] * delta_u * delta_w + picked[4][:, :, None] * delta_w * delta_w
    live = (jnp.arange(depth, dtype=jnp.int32)[None, :] < counts[:, None]).astype(jnp.float32)
    alpha = jnp.minimum(picked[5][:, :, None] * jnp.exp(-0.5 * quad), 0.99) * live[:, :, None]
    passed = jnp.cumprod(1.0 - alpha, axis=1)
    before = jnp.concatenate([jnp.ones_like(passed[:, :1]), passed[:, :-1]], axis=1)
    weight = alpha * before
    image = jnp.einsum('tkp,ctk->ctp', weight, picked[6:9], precision=hp)
    diff = image - target.reshape(3, tiles, 256)
    return 0.5 * jnp.sum(diff * diff)

def adam(value, first, second, grad):
    mnew = BETA_ONE * first + (1.0 - BETA_ONE) * grad
    vnew = BETA_TWO * second + (1.0 - BETA_TWO) * grad * grad
    mhat = mnew / (1.0 - BETA_ONE ** 10)
    vhat = vnew / (1.0 - BETA_TWO ** 10)
    return (value - LEARN * mhat / (jnp.sqrt(vhat) + EPSILON), mnew, vnew)

def reference(params, moment1, moment2, dual, z_copy, z_table, boundary_rows, owner_block, owner_slot, tile_lists, tile_counts, cameras, target):
    nblk = N_BLOCKS
    per_block = params.reshape(59, nblk, G_DEV).transpose(1, 0, 2)
    lists = tile_lists.reshape(nblk, TILES_DEV * N_VIEWS, K)
    counts = tile_counts.reshape(nblk, TILES_DEV * N_VIEWS)
    cams = cameras.reshape(nblk, V_DEV * N_VIEWS, 24)
    targets = target.reshape(3, nblk, TILES_DEV * N_VIEWS * 256).transpose(1, 0, 2)

    def one_block(items):
        return jax.grad(render_loss)(items[0], items[1], items[2], items[3], items[4])
    grads = lax.map(one_block, (per_block, lists, counts, cams, targets))
    grad = grads.transpose(1, 0, 2).reshape(59, nblk * G_DEV)
    owner_of = jnp.arange(B_TOT, dtype=jnp.int32) // B_DEV
    column = owner_of * G_DEV + boundary_rows
    penalty = RHO * (params[:, column] - z_copy + dual)
    grad = grad.at[:, column].add(penalty)
    new_params, new_moment1, new_moment2 = adam(params, moment1, moment2, grad)
    x_copy = new_params[:, column]
    keyrow = owner_block[:, 0] * Z_DEV + owner_slot
    total = jax.ops.segment_sum((x_copy + dual).T, keyrow, num_segments=nblk * Z_DEV).T
    number = jax.ops.segment_sum(jnp.ones((B_TOT,), jnp.float32), keyrow, num_segments=nblk * Z_DEV)
    z_new = (z_table + total) / (1.0 + number)[None, :]
    dual_new = dual + x_copy - z_new[:, keyrow]
    return (new_params, new_moment1, new_moment2, z_new, dual_new)
```

```python
import functools

import jax
import jax.numpy as jnp
from jax import lax
from jax.experimental import pallas as pl
from jax.experimental.pallas import tpu as pltpu
from jax.sharding import PartitionSpec as P

LEARN = 0.05
BETA_ONE = 0.9
BETA_TWO = 0.999
EPSILON = 1e-08

NPAR = 59
GAUSS = 2048
COPIES = 1024
ROWS = 1024
TILES = 16
DEPTH = 32
PAIRS = TILES * DEPTH
PIXELS = 256
NBLK = 64
NVIEW = 4
CAP = 64
SHARE = 15
WIDE = PAIRS + 128
JOINT = NVIEW * PAIRS + COPIES

F32 = jnp.float32
BF16 = jnp.bfloat16
I32 = jnp.int32
MESH = pl.DeviceIdType.MESH
NT = (((1,), (1,)), ((), ()))


def lane_gather(source, index, groups):
    low = index & 127
    high = index >> 7
    found = [jnp.take_along_axis(part, low, axis=1) for part in source[0]]
    for g in range(1, groups):
        here = high == g
        for n, part in enumerate(source[g]):
            found[n] = jnp.where(here, jnp.take_along_axis(part, low, axis=1), found[n])
    return found


def wide(row):
    return jnp.broadcast_to(row, (8, row.shape[1]))


def split(value):
    high = value.astype(BF16)
    return high, (value - high.astype(F32)).astype(BF16)


def share_of(ref, view):
    parts = [ref[SHARE * v : SHARE * v + 16, :] for v in range(NVIEW)]
    result = parts[3]
    for v in range(3):
        result = jnp.where(view == v, parts[v], result)
    return result


def render_kernel(cam, params, listed, target, out, table, sheet, goal, e_all, t_all, parts):
    table[0:11, :] = params[0:11, :]
    table[14:16, :] = jnp.zeros((2, GAUSS), F32)
    for c in range(3):
        colour = cam[0, 8] * params[11 + 16 * c : 12 + 16 * c, :]
        for k in range(1, 16):
            row = 11 + 16 * c + k
            colour += cam[0, 8 + k] * params[row : row + 1, :]
        table[11 + c : 12 + c, :] = colour + 0.5
    for c in range(3):
        for t in range(TILES):
            goal[16 * c + t : 16 * c + t + 1, :] = target[c : c + 1, PIXELS * t : PIXELS * (t + 1)]

    coded = listed[...]
    live = jnp.where(coded < GAUSS, 1.0, 0.0)
    index = coded & (GAUSS - 1)
    picked = []
    for j in range(PAIRS // 128):
        lanes = wide(index[:, 128 * j : 128 * (j + 1)])
        source = [
            [table[8 * n : 8 * n + 8, 128 * g : 128 * (g + 1)] for n in range(2)]
            for g in range(GAUSS // 128)
        ]
        picked.append(jnp.concatenate(lane_gather(source, lanes, GAUSS // 128), axis=0))
    picked = jnp.concatenate(picked, axis=1)

    def take(row):
        return picked[row : row + 1, :]

    jac = [[cam[0, 3 * i + j] for j in range(3)] for i in range(2)]
    centre = [take(j) for j in range(3)]
    scale = [jnp.exp(take(3 + k)) for k in range(3)]
    quat = [take(6 + k) for k in range(4)]
    norm = 1.0 / jnp.sqrt(quat[0] * quat[0] + quat[1] * quat[1] + quat[2] * quat[2] + quat[3] * quat[3])
    qw, qx, qy, qz = [q * norm for q in quat]
    rot = [
        [1 - 2 * (qy * qy + qz * qz), 2 * (qx * qy - qw * qz), 2 * (qx * qz + qw * qy)],
        [2 * (qx * qy + qw * qz), 1 - 2 * (qx * qx + qz * qz), 2 * (qy * qz - qw * qx)],
        [2 * (qx * qz - qw * qy), 2 * (qy * qz + qw * qx), 1 - 2 * (qx * qx + qy * qy)],
    ]
    mixed = [
        [(jac[i][0] * rot[0][k] + jac[i][1] * rot[1][k] + jac[i][2] * rot[2][k]) * scale[k] for k in range(3)]
        for i in range(2)
    ]

    def inner(a, b):
        return a[0] * b[0] + a[1] * b[1] + a[2] * b[2]

    first = inner(mixed[0], mixed[0]) + 0.01
    second = inner(mixed[1], mixed[1]) + 0.01
    cross = inner(mixed[0], mixed[1])
    det = first * second - cross * cross
    con0, con1, con2 = second / det, -cross / det, first / det
    cu = inner(jac[0], centre) + cam[0, 6]
    cw = inner(jac[1], centre) + cam[0, 7]
    opacity = 1.0 / (1.0 + jnp.exp(-take(10)))
    shown = opacity * live

    rows = [cu, cw, con0, 2.0 * con1, con2, shown, take(11), take(12), take(13)]
    rows = jnp.concatenate(rows + [jnp.zeros((7, PAIRS), F32)], axis=0)
    sheet[...] = rows.T

    tile = lax.broadcasted_iota(I32, (TILES, PIXELS), 0)
    pixel = lax.broadcasted_iota(I32, (TILES, PIXELS), 1)
    pos_u = (((tile & 3) * 16 + (pixel & 15)).astype(F32) + 0.5) / 32.0 - 1.0
    pos_w = (((tile >> 2) * 16 + (pixel >> 4)).astype(F32) + 0.5) / 32.0 - 1.0

    def column(s, f):
        return jnp.broadcast_to(sheet[16 * s : 16 * s + 16, f : f + 1], (TILES, PIXELS))

    image = [jnp.zeros((TILES, PIXELS), F32)] * 3
    passed = jnp.ones((TILES, PIXELS), F32)
    for s in range(DEPTH):
        du = pos_u - column(s, 0)
        dw = pos_w - column(s, 1)
        quad = (column(s, 2) * du + column(s, 3) * dw) * du + column(s, 4) * dw * dw
        bell = jnp.exp(-0.5 * quad)
        alpha = jnp.minimum(column(s, 5) * bell, 0.99)
        weight = alpha * passed
        for c in range(3):
            image[c] = image[c] + column(s, 6 + c) * weight
        e_all[16 * s : 16 * s + 16, :] = bell
        t_all[16 * s : 16 * s + 16, :] = passed
        passed = passed - weight

    diff = [image[c] - goal[16 * c : 16 * c + 16, :] for c in range(3)]
    behind = jnp.zeros((TILES, PIXELS), F32)
    for s in range(DEPTH - 1, -1, -1):
        bell = e_all[16 * s : 16 * s + 16, :]
        before = t_all[16 * s : 16 * s + 16, :]
        raw = column(s, 5) * bell
        alpha = jnp.minimum(raw, 0.99)
        glow = diff[0] * column(s, 6) + diff[1] * column(s, 7) + diff[2] * column(s, 8)
        slope = before * (glow - behind)
        slope = jnp.where(raw < 0.99, slope, jnp.where(raw == 0.99, 0.5 * slope, 0.0))
        behind = behind + alpha * (glow - behind)
        weight = alpha * before
        sums = [-0.5 * raw * slope, bell * slope] + [diff[c] * weight for c in range(3)]
        for n, value in enumerate(sums):
            high, low = split(value)
            parts[2 * n, 16 * s : 16 * s + 16, :] = high
            parts[2 * n + 1, 16 * s : 16 * s + 16, :] = low

    which = lax.broadcasted_iota(I32, (16, PIXELS), 0)
    place = lax.broadcasted_iota(I32, (16, PIXELS), 1)
    in_u = ((place & 15).astype(F32) - 7.5) / 32.0
    in_w = ((place >> 4).astype(F32) - 7.5) / 32.0
    basis = jnp.where(which == 0, 1.0, 0.0)
    basis = jnp.where(which == 1, in_u, basis)
    basis = jnp.where(which == 2, in_w, basis)
    basis = jnp.where(which == 3, in_u * in_u, basis)
    basis = jnp.where(which == 4, in_u * in_w, basis)
    basis = jnp.where(which == 5, in_w * in_w, basis)
    basis = basis.astype(BF16)

    def over_pixels(n):
        return lax.dot_general(basis, parts[2 * n], NT, preferred_element_type=F32) + lax.dot_general(
            basis, parts[2 * n + 1], NT, preferred_element_type=F32
        )

    moments = over_pixels(0)
    m1, mu, mw, muu, muw, mww = [moments[n : n + 1, :] for n in range(6)]
    g_opacity = over_pixels(1)[0:1, :] * live
    g_colour = [over_pixels(2 + c)[0:1, :] for c in range(3)]
    at = lax.broadcasted_iota(I32, (1, PAIRS), 1) & 15
    off_u = cu - (((at & 3) * 16 + 8).astype(F32) / 32.0 - 1.0)
    off_w = cw - (((at >> 2) * 16 + 8).astype(F32) / 32.0 - 1.0)
    s_u = mu - off_u * m1
    s_w = mw - off_w * m1
    g_con0 = muu - off_u * (mu + s_u)
    g_con1 = 2.0 * (muw - off_u * mw - off_w * s_u)
    g_con2 = mww - off_w * (mw + s_w)
    g_cu = -2.0 * (con0 * s_u + con1 * s_w)
    g_cw = -2.0 * (con1 * s_u + con2 * s_w)

    g_first = -(con0 * con0 * g_con0 + con0 * con1 * g_con1 + con1 * con1 * g_con2)
    g_second = -(con1 * con1 * g_con0 + con1 * con2 * g_con1 + con2 * con2 * g_con2)
    g_cross = -(2.0 * con0 * con1 * g_con0 + (con0 * con2 + con1 * con1) * g_con1 + 2.0 * con1 * con2 * g_con2)
    g_mixed = [
        [2.0 * g_first * mixed[0][k] + g_cross * mixed[1][k] for k in range(3)],
        [2.0 * g_second * mixed[1][k] + g_cross * mixed[0][k] for k in range(3)],
    ]
    g_scale = [g_mixed[0][k] * mixed[0][k] + g_mixed[1][k] * mixed[1][k] for k in range(3)]
    r = [
        [(jac[0][j] * g_mixed[0][k] + jac[1][j] * g_mixed[1][k]) * scale[k] for k in range(3)] for j in range(3)
    ]
    h_w = 2 * (qz * (r[1][0] - r[0][1]) + qy * (r[0][2] - r[2][0]) + qx * (r[2][1] - r[1][2]))
    h_x = 2 * (
        qy * (r[0][1] + r[1][0]) + qz * (r[0][2] + r[2][0]) + qw * (r[2][1] - r[1][2]) - 2 * qx * (r[1][1] + r[2][2])
    )
    h_y = 2 * (
        qx * (r[0][1] + r[1][0]) + qz * (r[1][2] + r[2][1]) + qw * (r[0][2] - r[2][0]) - 2 * qy * (r[0][0] + r[2][2])
    )
    h_z = 2 * (
        qx * (r[0][2] + r[2][0]) + qy * (r[1][2] + r[2][1]) + qw * (r[1][0] - r[0][1]) - 2 * qz * (r[0][0] + r[1][1])
    )
    along = qw * h_w + qx * h_x + qy * h_y + qz * h_z
    g_quat = [(h - q * along) * norm for h, q in ((h_w, qw), (h_x, qx), (h_y, qy), (h_z, qz))]
    g_centre = [jac[0][j] * g_cu + jac[1][j] * g_cw for j in range(3)]
    g_logit = g_opacity * opacity * (1.0 - opacity)
    sent = g_centre + g_scale + g_quat + [g_logit] + g_colour + [index.astype(F32), jnp.zeros((1, PAIRS), F32)]
    out[:, 0:PAIRS] = jnp.concatenate(sent, axis=0)
    spot = lax.broadcasted_iota(I32, (16, 128), 0)
    colbasis = jnp.zeros((16, 128), F32)
    for k in range(16):
        colbasis = jnp.where(spot == k, cam[0, 8 + k], colbasis)
    out[:, PAIRS:WIDE] = colbasis


def views_kernel(mine, out, send_sem, recv_sem):
    view = lax.axis_index("views")
    barrier = pltpu.get_barrier_semaphore()
    for k in range(1, NVIEW):
        pl.semaphore_signal(barrier, inc=1, device_id={"views": (view + k) % NVIEW}, device_id_type=MESH)
    pl.semaphore_wait(barrier, NVIEW - 1)
    copies = []
    for k in range(1, NVIEW):
        copy = pltpu.make_async_remote_copy(
            src_ref=mine,
            dst_ref=out.at[view],
            send_sem=send_sem.at[k - 1],
            recv_sem=recv_sem.at[k - 1],
            device_id={"views": (view + k) % NVIEW},
            device_id_type=MESH,
        )
        copy.start()
        copies.append(copy)
    out[view] = mine[...]
    for copy in copies:
        copy.wait()


def update_kernel(
    gathered, params, moment1, moment2, dual, z_copy, rows, owner, slot,
    new_params, new_moment1, new_moment2, send, holds, place,
    left, masked, onehot, padded, padded_dual, source, names,
):
    view = lax.axis_index("views")
    left[59:64, :] = jnp.zeros((5, JOINT), F32)
    for v in range(NVIEW):
        lanes = slice(PAIRS * v, PAIRS * (v + 1))
        left[0:11, lanes] = gathered[v, 0:11, 0:PAIRS]
        colbasis = gathered[v, :, PAIRS : PAIRS + 1]
        for c in range(3):
            left[11 + 16 * c : 27 + 16 * c, lanes] = colbasis * gathered[v, 11 + c : 12 + c, 0:PAIRS]
    lanes = slice(NVIEW * PAIRS, JOINT)
    left[0:NPAR, lanes] = dual[...] - z_copy[...]
    left[NPAR : NPAR + 1, lanes] = jnp.ones((1, COPIES), F32)
    boundary = rows[...]
    joint = jnp.concatenate([gathered[v, 14:15, 0:PAIRS].astype(I32) for v in range(NVIEW)] + [boundary], axis=1)
    high, low = split(left[...])
    group = joint >> 8
    for h in range(8):
        mask = jnp.where(jnp.broadcast_to(group, (16, JOINT)) == h, 1.0, 0.0).astype(BF16)
        for n in range(4):
            masked[128 * h + 16 * n : 128 * h + 16 * n + 16, :] = high[16 * n : 16 * n + 16, :] * mask
            masked[128 * h + 64 + 16 * n : 128 * h + 80 + 16 * n, :] = low[16 * n : 16 * n + 16, :] * mask
    inside = joint & 255
    hot = lax.broadcasted_iota(I32, (256, JOINT), 0) == inside
    onehot[...] = jnp.where(hot, 1.0, 0.0).astype(BF16)
    total = lax.dot_general(masked[...], onehot[...], NT, preferred_element_type=F32)

    padded[NPAR:64, :] = jnp.zeros((64 - NPAR, GAUSS), F32)
    for h in range(8):
        both = total[128 * h : 128 * h + 64, :] + total[128 * h + 64 : 128 * h + 128, :]
        lanes = slice(256 * h, 256 * (h + 1))
        value = params[:, lanes]
        grad = both[0:NPAR] + both[NPAR : NPAR + 1] * value
        first = BETA_ONE * moment1[:, lanes] + (1.0 - BETA_ONE) * grad
        second = BETA_TWO * moment2[:, lanes] + (1.0 - BETA_TWO) * grad * grad
        mhat = first * (1.0 / (1.0 - BETA_ONE**10))
        vhat = second * (1.0 / (1.0 - BETA_TWO**10))
        value = value - LEARN * mhat / (jnp.sqrt(vhat) + EPSILON)
        new_moment1[:, lanes] = first
        new_moment2[:, lanes] = second
        new_params[:, lanes] = value
        padded[0:NPAR, lanes] = value
    padded_dual[0:NPAR, :] = dual[...]
    padded_dual[NPAR:64, :] = jnp.zeros((64 - NPAR, COPIES), F32)

    owned = lax.broadcasted_iota(I32, (NBLK, COPIES), 0) == owner[...]
    owned = jnp.where(owned, 1.0, 0.0)
    upper = lax.broadcasted_iota(I32, (128, 128), 0) < lax.broadcasted_iota(I32, (128, 128), 1)
    upper = jnp.where(upper, 1.0, 0.0).astype(BF16)
    ranks = []
    carry = jnp.zeros((NBLK, 1), F32)
    for j in range(COPIES // 128):
        part = owned[:, 128 * j : 128 * (j + 1)]
        ahead = jnp.dot(part.astype(BF16), upper, preferred_element_type=F32) + carry
        ranks.append(jnp.sum(part * ahead, axis=0, keepdims=True))
        carry = carry + jnp.sum(part, axis=1, keepdims=True)
    rank = jnp.concatenate(ranks, axis=1).astype(I32)
    place[...] = owner[...] * CAP + rank
    ident = lax.broadcasted_iota(I32, (1, COPIES), 1)
    ranked = (lax.broadcasted_iota(I32, (128, COPIES), 0) & (CAP - 1)) == rank
    coarse = jnp.where(ranked, (ident >> 5).astype(F32), 0.0).astype(BF16)
    fine = jnp.where(ranked, ((ident & 31) + 1).astype(F32), 0.0).astype(BF16)
    owned = owned.astype(BF16)
    names[...] = (
        32.0 * lax.dot_general(owned, coarse, NT, preferred_element_type=F32)
        + lax.dot_general(owned, fine, NT, preferred_element_type=F32)
    ).astype(I32)

    mine = share_of(padded, view)
    xs = []
    for j in range(COPIES // 128):
        parts = [
            [mine[8 * n : 8 * n + 8, 128 * g : 128 * (g + 1)] for n in range(2)] for g in range(GAUSS // 128)
        ]
        xs.append(jnp.concatenate(lane_gather(parts, wide(boundary[:, 128 * j : 128 * (j + 1)]), GAUSS // 128), axis=0))
    source[...] = jnp.concatenate(xs, axis=1) + share_of(padded_dual, view)
    source[15:16, :] = (slot[...] + 1).astype(F32)
    holds[...] = source[...]

    lane = lax.broadcasted_iota(I32, (8, 128), 1)
    for j in range(NBLK // 2):
        name = jnp.where(lane < CAP, wide(names[2 * j : 2 * j + 1, :]), wide(names[2 * j + 1 : 2 * j + 2, :]))
        parts = [
            [source[8 * n : 8 * n + 8, 128 * g : 128 * (g + 1)] for n in range(2)] for g in range(COPIES // 128)
        ]
        top, bottom = lane_gather(parts, jnp.maximum(name - 1, 0), COPIES // 128)
        top = jnp.where(name > 0, top, 0.0)
        bottom = jnp.where(name > 0, bottom, 0.0)
        send[2 * j] = jnp.where(lane < CAP, top, pltpu.roll(bottom, CAP, 1))
        send[2 * j + 1] = jnp.where(lane < CAP, pltpu.roll(top, CAP, 1), bottom)


def to_blocks(outgoing, incoming, send_sem, recv_sem, block):
    def one(k, _):
        other = (block + k) % NBLK
        pltpu.make_async_remote_copy(
            src_ref=outgoing.at[other],
            dst_ref=incoming.at[block],
            send_sem=send_sem,
            recv_sem=recv_sem,
            device_id={"blocks": other},
            device_id_type=MESH,
        ).start()
        return 0

    lax.fori_loop(1, NBLK, one, 0)
    incoming[block] = outgoing[block]


def wait_blocks(outgoing, incoming, send_sem, recv_sem, block):
    whole = pltpu.make_async_remote_copy(
        src_ref=outgoing.at[pl.ds(0, NBLK - 1)],
        dst_ref=incoming.at[pl.ds(0, NBLK - 1)],
        send_sem=send_sem,
        recv_sem=recv_sem,
        device_id={"blocks": block},
        device_id_type=MESH,
    )
    whole.wait_send()
    whole.wait_recv()


def to_views(pieces, send_sem, recv_sem, view):
    copies = []
    for k in range(1, NVIEW):
        copy = pltpu.make_async_remote_copy(
            src_ref=pieces.at[view],
            dst_ref=pieces.at[view],
            send_sem=send_sem.at[k - 1],
            recv_sem=recv_sem.at[k - 1],
            device_id={"views": (view + k) % NVIEW},
            device_id_type=MESH,
        )
        copy.start()
        copies.append(copy)
    return copies


def unpack(chunks, j):
    lane = lax.broadcasted_iota(I32, (8, 128), 1)
    even, odd = chunks[2 * j], chunks[2 * j + 1]
    top = jnp.where(lane < CAP, even, pltpu.roll(odd, CAP, 1))
    bottom = jnp.where(lane < CAP, pltpu.roll(even, CAP, 1), odd)
    return top, bottom


def consensus_kernel(
    send, z_table, holds, place,
    z_new, dual_new,
    got, answers, returned, z_parts, d_parts, padded, items, masked, onehot,
    s_send, r_send, s_back, r_back, s_z, r_z, s_d, r_d,
):
    block = lax.axis_index("blocks")
    view = lax.axis_index("views")
    barrier = pltpu.get_barrier_semaphore()

    def greet(k, _):
        pl.semaphore_signal(barrier, inc=1, device_id={"blocks": (block + k) % NBLK}, device_id_type=MESH)
        return 0

    lax.fori_loop(1, NBLK, greet, 0)
    for k in range(1, NVIEW):
        pl.semaphore_signal(barrier, inc=1, device_id={"views": (view + k) % NVIEW}, device_id_type=MESH)
    pl.semaphore_wait(barrier, NBLK - 1 + NVIEW - 1)
    to_blocks(send, got, s_send, r_send, block)
    padded[0:NPAR, :] = z_table[...]
    padded[NPAR:64, :] = jnp.zeros((64 - NPAR, ROWS), F32)
    wait_blocks(send, got, s_send, r_send, block)

    for j in range(NBLK // 2):
        top, bottom = unpack(got, j)
        items[0:8, 128 * j : 128 * (j + 1)] = top
        items[8:16, 128 * j : 128 * (j + 1)] = bottom
    label = items[15:16, :].astype(I32)
    index = jnp.maximum(label - 1, 0)
    present = label > 0
    last = lax.broadcasted_iota(I32, (16, NBLK * CAP), 0) == 15
    high, low = split(jnp.where(last, 1.0, items[...]))
    group = jnp.where(present, index >> 8, 4)
    for h in range(4):
        mask = jnp.where(jnp.broadcast_to(group, (16, NBLK * CAP)) == h, 1.0, 0.0).astype(BF16)
        masked[32 * h : 32 * h + 16, :] = high * mask
        masked[32 * h + 16 : 32 * h + 32, :] = low * mask
    hot = lax.broadcasted_iota(I32, (256, NBLK * CAP), 0) == (index & 255)
    onehot[...] = jnp.where(hot, 1.0, 0.0).astype(BF16)
    total = lax.dot_general(masked[...], onehot[...], NT, preferred_element_type=F32)
    mine = share_of(padded, view)
    fresh = []
    for h in range(4):
        both = total[32 * h : 32 * h + 16, :] + total[32 * h + 16 : 32 * h + 32, :]
        fresh.append((mine[:, 256 * h : 256 * (h + 1)] + both) / (1.0 + both[15:16, :]))
    fresh = jnp.concatenate(fresh, axis=1)
    z_parts[view] = fresh
    z_copies = to_views(z_parts, s_z, r_z, view)

    lane = lax.broadcasted_iota(I32, (8, 128), 1)
    parts = [[fresh[8 * n : 8 * n + 8, 128 * g : 128 * (g + 1)] for n in range(2)] for g in range(ROWS // 128)]
    for j in range(NBLK // 2):
        top, bottom = lane_gather(parts, wide(index[:, 128 * j : 128 * (j + 1)]), ROWS // 128)
        answers[2 * j] = jnp.where(lane < CAP, top, pltpu.roll(bottom, CAP, 1))
        answers[2 * j + 1] = jnp.where(lane < CAP, pltpu.roll(top, CAP, 1), bottom)
    to_blocks(answers, returned, s_back, r_back, block)
    wait_blocks(answers, returned, s_back, r_back, block)

    for j in range(NBLK // 2):
        top, bottom = unpack(returned, j)
        items[0:8, 128 * j : 128 * (j + 1)] = top
        items[8:16, 128 * j : 128 * (j + 1)] = bottom
    fetched = []
    for j in range(COPIES // 128):
        parts = [
            [items[8 * n : 8 * n + 8, 128 * g : 128 * (g + 1)] for n in range(2)] for g in range(NBLK // 2)
        ]
        fetched.append(
            jnp.concatenate(lane_gather(parts, wide(place[:, 128 * j : 128 * (j + 1)]), NBLK // 2), axis=0)
        )
    d_parts[view] = holds[...] - jnp.concatenate(fetched, axis=1)
    d_copies = to_views(d_parts, s_d, r_d, view)
    for copy in z_copies:
        copy.wait()
    for v in range(NVIEW):
        count = min(SHARE, NPAR - SHARE * v)
        z_new[SHARE * v : SHARE * v + count, :] = z_parts[v, 0:count, :]
    for copy in d_copies:
        copy.wait()
    for v in range(NVIEW):
        count = min(SHARE, NPAR - SHARE * v)
        dual_new[SHARE * v : SHARE * v + count, :] = d_parts[v, 0:count, :]


def vmem():
    return pl.BlockSpec(memory_space=pltpu.VMEM)


def local(
    params, moment1, moment2, dual, z_copy, z_table, boundary_rows, owner_block, owner_slot,
    tile_lists, tile_counts, cameras, target,
):
    spots = jnp.arange(DEPTH, dtype=I32)[None, :]
    listed = jnp.where(spots < tile_counts[:, None], tile_lists, tile_lists + GAUSS).T.reshape(1, PAIRS)
    limit = 48 * 1024 * 1024
    shape = jax.ShapeDtypeStruct
    mine = pl.pallas_call(
        render_kernel,
        out_shape=shape((16, WIDE), F32),
        in_specs=[pl.BlockSpec(memory_space=pltpu.SMEM), vmem(), vmem(), vmem()],
        out_specs=vmem(),
        scratch_shapes=[
            pltpu.VMEM((16, GAUSS), F32),
            pltpu.VMEM((PAIRS, 16), F32),
            pltpu.VMEM((48, PIXELS), F32),
            pltpu.VMEM((PAIRS, PIXELS), F32),
            pltpu.VMEM((PAIRS, PIXELS), F32),
            pltpu.VMEM((10, PAIRS, PIXELS), BF16),
        ],
        compiler_params=pltpu.CompilerParams(vmem_limit_bytes=limit),
        name="render",
    )(cameras, params, listed, target)
    gathered = pl.pallas_call(
        views_kernel,
        out_shape=shape((NVIEW, 16, WIDE), F32),
        in_specs=[vmem()],
        out_specs=vmem(),
        scratch_shapes=[pltpu.SemaphoreType.DMA((3,)), pltpu.SemaphoreType.DMA((3,))],
        compiler_params=pltpu.CompilerParams(collective_id=0, has_side_effects=True),
        name="exchange_views",
    )(mine)
    new_params, new_moment1, new_moment2, send, holds, place = pl.pallas_call(
        update_kernel,
        out_shape=(
            shape((NPAR, GAUSS), F32),
            shape((NPAR, GAUSS), F32),
            shape((NPAR, GAUSS), F32),
            shape((NBLK, 8, 128), F32),
            shape((16, COPIES), F32),
            shape((1, COPIES), I32),
        ),
        in_specs=[vmem()] * 9,
        out_specs=(vmem(),) * 6,
        scratch_shapes=[
            pltpu.VMEM((64, JOINT), F32),
            pltpu.VMEM((1024, JOINT), BF16),
            pltpu.VMEM((256, JOINT), BF16),
            pltpu.VMEM((64, GAUSS), F32),
            pltpu.VMEM((64, COPIES), F32),
            pltpu.VMEM((16, COPIES), F32),
            pltpu.VMEM((NBLK, 128), I32),
        ],
        compiler_params=pltpu.CompilerParams(vmem_limit_bytes=limit),
        name="update",
    )(
        gathered, params, moment1, moment2, dual, z_copy,
        boundary_rows.reshape(1, COPIES), owner_block.reshape(1, COPIES), owner_slot.reshape(1, COPIES),
    )
    z_new, dual_new = pl.pallas_call(
        consensus_kernel,
        out_shape=(shape((NPAR, ROWS), F32), shape((NPAR, COPIES), F32)),
        in_specs=[vmem()] * 4,
        out_specs=(vmem(),) * 2,
        scratch_shapes=[
            pltpu.VMEM((NBLK, 8, 128), F32),
            pltpu.VMEM((NBLK, 8, 128), F32),
            pltpu.VMEM((NBLK, 8, 128), F32),
            pltpu.VMEM((NVIEW, 16, ROWS), F32),
            pltpu.VMEM((NVIEW, 16, COPIES), F32),
            pltpu.VMEM((64, ROWS), F32),
            pltpu.VMEM((16, NBLK * CAP), F32),
            pltpu.VMEM((128, NBLK * CAP), BF16),
            pltpu.VMEM((256, NBLK * CAP), BF16),
            pltpu.SemaphoreType.DMA,
            pltpu.SemaphoreType.DMA,
            pltpu.SemaphoreType.DMA,
            pltpu.SemaphoreType.DMA,
            pltpu.SemaphoreType.DMA((3,)),
            pltpu.SemaphoreType.DMA((3,)),
            pltpu.SemaphoreType.DMA((3,)),
            pltpu.SemaphoreType.DMA((3,)),
        ],
        compiler_params=pltpu.CompilerParams(collective_id=1, has_side_effects=True, vmem_limit_bytes=limit),
        name="consensus",
    )(send, z_table, holds, place)
    return (new_params, new_moment1, new_moment2, z_new, dual_new)


def solution(mesh):
    whole, both = P(None, "blocks"), ("blocks", "views")
    placed = (whole,) * 6 + (P("blocks"), P("blocks", None), P("blocks"))
    placed += (P(both, None), P(both), P(both, None), P(None, both))
    return jax.shard_map(local, mesh=mesh, in_specs=placed, out_specs=(whole,) * 5, check_vma=False)
```

```python
import functools

import jax
import jax.numpy as jnp
from jax import lax
from jax.experimental import pallas as pl
from jax.experimental.pallas import tpu as pltpu
from jax.sharding import PartitionSpec as P

LEARN = 0.05
BETA_ONE = 0.9
BETA_TWO = 0.999
EPSILON = 1e-08

NPAR = 59
GAUSS = 2048
COPIES = 1024
ROWS = 1024
TILES = 16
DEPTH = 32
PAIRS = TILES * DEPTH
PIXELS = 256
NBLK = 64
NVIEW = 4
CAP = 64
SHARE = 15
WIDE = PAIRS + 128
JOINT = NVIEW * PAIRS + COPIES
UNROLL = 4

F32 = jnp.float32
BF16 = jnp.bfloat16
I32 = jnp.int32
MESH = pl.DeviceIdType.MESH
NT = (((1,), (1,)), ((), ()))


def lane_gather(source, index, groups):
    low = index & 127
    high = index >> 7
    found = [jnp.take_along_axis(part, low, axis=1) for part in source[0]]
    for g in range(1, groups):
        here = high == g
        for n, part in enumerate(source[g]):
            found[n] = jnp.where(here, jnp.take_along_axis(part, low, axis=1), found[n])
    return found


def wide(row):
    return jnp.broadcast_to(row, (8, row.shape[1]))


def split(value):
    high = value.astype(BF16)
    return high, (value - high.astype(F32)).astype(BF16)


def share_of(ref, view):
    parts = [ref[SHARE * v : SHARE * v + 16, :] for v in range(NVIEW - 1)]
    rest = ref[SHARE * 3 : NPAR, :]
    result = jnp.concatenate([rest, jnp.zeros((16 - rest.shape[0], rest.shape[1]), rest.dtype)], axis=0)
    for v in range(3):
        result = jnp.where(view == v, parts[v], result)
    return result


def render(cam, params, lists, counts, target, table, sheet, goal, e_all, t_all, parts):
    table[0:11, :] = params[0:11, :]
    table[14:16, :] = jnp.zeros((2, GAUSS), F32)
    for c in range(3):
        colour = cam[0, 8] * params[11 + 16 * c : 12 + 16 * c, :]
        for k in range(1, 16):
            row = 11 + 16 * c + k
            colour += cam[0, 8 + k] * params[row : row + 1, :]
        table[11 + c : 12 + c, :] = colour + 0.5
    for c in range(3):
        for t in range(TILES):
            goal[16 * c + t : 16 * c + t + 1, :] = target[c : c + 1, PIXELS * t : PIXELS * (t + 1)]

    turned = lists[...].astype(F32).T
    slots = lax.broadcasted_iota(I32, (DEPTH, TILES), 0)
    turned = jnp.where(slots < counts[...], turned, turned + GAUSS)
    turned = jnp.concatenate([turned, jnp.zeros((DEPTH, 128 - TILES), F32)], axis=1)
    turns = [turned] + [pltpu.roll(turned, TILES * m, 1) for m in range(1, 8)]
    lane = lax.broadcasted_iota(I32, (1, 128), 1)
    pieces = []
    for j in range(PAIRS // 128):
        row = turns[0][8 * j : 8 * j + 1, :]
        for m in range(1, 8):
            row = jnp.where(lane >> 4 == m, turns[m][8 * j + m : 8 * j + m + 1, :], row)
        pieces.append(row)
    coded = jnp.concatenate(pieces, axis=1).astype(I32)
    live = jnp.where(coded < GAUSS, 1.0, 0.0)
    index = coded & (GAUSS - 1)
    picked = []
    for j in range(PAIRS // 128):
        lanes = wide(index[:, 128 * j : 128 * (j + 1)])
        source = [
            [table[8 * n : 8 * n + 8, 128 * g : 128 * (g + 1)] for n in range(2)]
            for g in range(GAUSS // 128)
        ]
        picked.append(jnp.concatenate(lane_gather(source, lanes, GAUSS // 128), axis=0))
    picked = jnp.concatenate(picked, axis=1)

    def take(row):
        return picked[row : row + 1, :]

    jac = [[cam[0, 3 * i + j] for j in range(3)] for i in range(2)]
    centre = [take(j) for j in range(3)]
    scale = [jnp.exp(take(3 + k)) for k in range(3)]
    quat = [take(6 + k) for k in range(4)]
    norm = 1.0 / jnp.sqrt(quat[0] * quat[0] + quat[1] * quat[1] + quat[2] * quat[2] + quat[3] * quat[3])
    qw, qx, qy, qz = [q * norm for q in quat]
    rot = [
        [1 - 2 * (qy * qy + qz * qz), 2 * (qx * qy - qw * qz), 2 * (qx * qz + qw * qy)],
        [2 * (qx * qy + qw * qz), 1 - 2 * (qx * qx + qz * qz), 2 * (qy * qz - qw * qx)],
        [2 * (qx * qz - qw * qy), 2 * (qy * qz + qw * qx), 1 - 2 * (qx * qx + qy * qy)],
    ]
    mixed = [
        [(jac[i][0] * rot[0][k] + jac[i][1] * rot[1][k] + jac[i][2] * rot[2][k]) * scale[k] for k in range(3)]
        for i in range(2)
    ]

    def inner(a, b):
        return a[0] * b[0] + a[1] * b[1] + a[2] * b[2]

    first = inner(mixed[0], mixed[0]) + 0.01
    second = inner(mixed[1], mixed[1]) + 0.01
    cross = inner(mixed[0], mixed[1])
    det = first * second - cross * cross
    con0, con1, con2 = second / det, -cross / det, first / det
    cu = inner(jac[0], centre) + cam[0, 6]
    cw = inner(jac[1], centre) + cam[0, 7]
    opacity = 1.0 / (1.0 + jnp.exp(-take(10)))
    shown = opacity * live

    rows = [cu, cw, con0, 2.0 * con1, con2, shown, take(11), take(12), take(13)]
    rows = jnp.concatenate(rows + [jnp.zeros((7, PAIRS), F32)], axis=0)
    sheet[...] = rows.T

    tile = lax.broadcasted_iota(I32, (TILES, PIXELS), 0)
    pixel = lax.broadcasted_iota(I32, (TILES, PIXELS), 1)
    pos_u = (((tile & 3) * 16 + (pixel & 15)).astype(F32) + 0.5) / 32.0 - 1.0
    pos_w = (((tile >> 2) * 16 + (pixel >> 4)).astype(F32) + 0.5) / 32.0 - 1.0

    def at_slot(s):
        return pl.ds(pl.multiple_of(TILES * s, TILES), TILES)

    def column(s, f):
        return jnp.broadcast_to(sheet[at_slot(s), f : f + 1], (TILES, PIXELS))

    def forward(step, state):
        image, passed = list(state[0:3]), state[3]
        for s in [UNROLL * step + n for n in range(UNROLL)]:
            du = pos_u - column(s, 0)
            dw = pos_w - column(s, 1)
            quad = (column(s, 2) * du + column(s, 3) * dw) * du + column(s, 4) * dw * dw
            bell = jnp.exp(-0.5 * quad)
            alpha = jnp.minimum(column(s, 5) * bell, 0.99)
            weight = alpha * passed
            for c in range(3):
                image[c] = image[c] + column(s, 6 + c) * weight
            e_all[at_slot(s), :] = bell
            t_all[at_slot(s), :] = passed
            passed = passed - weight
        return (*image, passed)

    zero = jnp.zeros((TILES, PIXELS), F32)
    image = lax.fori_loop(0, DEPTH // UNROLL, forward, (zero, zero, zero, zero + 1.0))
    diff = [image[c] - goal[16 * c : 16 * c + 16, :] for c in range(3)]

    def backward(step, behind):
        for s in [DEPTH - 1 - UNROLL * step - n for n in range(UNROLL)]:
            bell = e_all[at_slot(s), :]
            before = t_all[at_slot(s), :]
            raw = column(s, 5) * bell
            alpha = jnp.minimum(raw, 0.99)
            glow = diff[0] * column(s, 6) + diff[1] * column(s, 7) + diff[2] * column(s, 8)
            slope = before * (glow - behind)
            slope = jnp.where(raw < 0.99, slope, jnp.where(raw == 0.99, 0.5 * slope, 0.0))
            behind = behind + alpha * (glow - behind)
            weight = alpha * before
            sums = [-0.5 * raw * slope, bell * slope] + [diff[c] * weight for c in range(3)]
            for n, value in enumerate(sums):
                high, low = split(value)
                parts[2 * n, at_slot(s), :] = high
                parts[2 * n + 1, at_slot(s), :] = low
        return behind

    lax.fori_loop(0, DEPTH // UNROLL, backward, zero)

    which = lax.broadcasted_iota(I32, (16, PIXELS), 0)
    place = lax.broadcasted_iota(I32, (16, PIXELS), 1)
    in_u = ((place & 15).astype(F32) - 7.5) / 32.0
    in_w = ((place >> 4).astype(F32) - 7.5) / 32.0
    basis = jnp.where(which == 0, 1.0, 0.0)
    basis = jnp.where(which == 1, in_u, basis)
    basis = jnp.where(which == 2, in_w, basis)
    basis = jnp.where(which == 3, in_u * in_u, basis)
    basis = jnp.where(which == 4, in_u * in_w, basis)
    basis = jnp.where(which == 5, in_w * in_w, basis)
    basis = basis.astype(BF16)

    def over_pixels(n):
        return lax.dot_general(basis, parts[2 * n], NT, preferred_element_type=F32) + lax.dot_general(
            basis, parts[2 * n + 1], NT, preferred_element_type=F32
        )

    moments = over_pixels(0)
    m1, mu, mw, muu, muw, mww = [moments[n : n + 1, :] for n in range(6)]
    g_opacity = over_pixels(1)[0:1, :] * live
    g_colour = [over_pixels(2 + c)[0:1, :] for c in range(3)]
    at = lax.broadcasted_iota(I32, (1, PAIRS), 1) & 15
    off_u = cu - (((at & 3) * 16 + 8).astype(F32) / 32.0 - 1.0)
    off_w = cw - (((at >> 2) * 16 + 8).astype(F32) / 32.0 - 1.0)
    s_u = mu - off_u * m1
    s_w = mw - off_w * m1
    g_con0 = muu - off_u * (mu + s_u)
    g_con1 = 2.0 * (muw - off_u * mw - off_w * s_u)
    g_con2 = mww - off_w * (mw + s_w)
    g_cu = -2.0 * (con0 * s_u + con1 * s_w)
    g_cw = -2.0 * (con1 * s_u + con2 * s_w)

    g_first = -(con0 * con0 * g_con0 + con0 * con1 * g_con1 + con1 * con1 * g_con2)
    g_second = -(con1 * con1 * g_con0 + con1 * con2 * g_con1 + con2 * con2 * g_con2)
    g_cross = -(2.0 * con0 * con1 * g_con0 + (con0 * con2 + con1 * con1) * g_con1 + 2.0 * con1 * con2 * g_con2)
    g_mixed = [
        [2.0 * g_first * mixed[0][k] + g_cross * mixed[1][k] for k in range(3)],
        [2.0 * g_second * mixed[1][k] + g_cross * mixed[0][k] for k in range(3)],
    ]
    g_scale = [g_mixed[0][k] * mixed[0][k] + g_mixed[1][k] * mixed[1][k] for k in range(3)]
    r = [
        [(jac[0][j] * g_mixed[0][k] + jac[1][j] * g_mixed[1][k]) * scale[k] for k in range(3)] for j in range(3)
    ]
    h_w = 2 * (qz * (r[1][0] - r[0][1]) + qy * (r[0][2] - r[2][0]) + qx * (r[2][1] - r[1][2]))
    h_x = 2 * (
        qy * (r[0][1] + r[1][0]) + qz * (r[0][2] + r[2][0]) + qw * (r[2][1] - r[1][2]) - 2 * qx * (r[1][1] + r[2][2])
    )
    h_y = 2 * (
        qx * (r[0][1] + r[1][0]) + qz * (r[1][2] + r[2][1]) + qw * (r[0][2] - r[2][0]) - 2 * qy * (r[0][0] + r[2][2])
    )
    h_z = 2 * (
        qx * (r[0][2] + r[2][0]) + qy * (r[1][2] + r[2][1]) + qw * (r[1][0] - r[0][1]) - 2 * qz * (r[0][0] + r[1][1])
    )
    along = qw * h_w + qx * h_x + qy * h_y + qz * h_z
    g_quat = [(h - q * along) * norm for h, q in ((h_w, qw), (h_x, qx), (h_y, qy), (h_z, qz))]
    g_centre = [jac[0][j] * g_cu + jac[1][j] * g_cw for j in range(3)]
    g_logit = g_opacity * opacity * (1.0 - opacity)
    sent = g_centre + g_scale + g_quat + [g_logit] + g_colour + [index.astype(F32), jnp.zeros((1, PAIRS), F32)]
    spot = lax.broadcasted_iota(I32, (16, 128), 0)
    colbasis = jnp.zeros((16, 128), F32)
    for k in range(16):
        colbasis = jnp.where(spot == k, cam[0, 8 + k], colbasis)
    return jnp.concatenate(sent, axis=0), colbasis


def to_blocks(outgoing, incoming, send_sem, recv_sem, block):
    def one(k, _):
        other = (block + k) % NBLK
        pltpu.make_async_remote_copy(
            src_ref=outgoing.at[other],
            dst_ref=incoming.at[block],
            send_sem=send_sem,
            recv_sem=recv_sem,
            device_id={"blocks": other},
            device_id_type=MESH,
        ).start()
        return 0

    lax.fori_loop(1, NBLK, one, 0)
    incoming[block] = outgoing[block]


def wait_blocks(outgoing, incoming, send_sem, recv_sem, block):
    whole = pltpu.make_async_remote_copy(
        src_ref=outgoing.at[pl.ds(0, NBLK - 1)],
        dst_ref=incoming.at[pl.ds(0, NBLK - 1)],
        send_sem=send_sem,
        recv_sem=recv_sem,
        device_id={"blocks": block},
        device_id_type=MESH,
    )
    whole.wait_send()
    whole.wait_recv()


def to_views(pieces, send_sem, recv_sem, view):
    copies = []
    for k in range(1, NVIEW):
        copy = pltpu.make_async_remote_copy(
            src_ref=pieces.at[view],
            dst_ref=pieces.at[view],
            send_sem=send_sem.at[k - 1],
            recv_sem=recv_sem.at[k - 1],
            device_id={"views": (view + k) % NVIEW},
            device_id_type=MESH,
        )
        copy.start()
        copies.append(copy)
    return copies


def unpack(chunks, j):
    lane = lax.broadcasted_iota(I32, (8, 128), 1)
    even, odd = chunks[2 * j], chunks[2 * j + 1]
    top = jnp.where(lane < CAP, even, pltpu.roll(odd, CAP, 1))
    bottom = jnp.where(lane < CAP, pltpu.roll(even, CAP, 1), odd)
    return top, bottom


def pack(top, bottom, chunks, j):
    lane = lax.broadcasted_iota(I32, (8, 128), 1)
    chunks[2 * j] = jnp.where(lane < CAP, top, pltpu.roll(bottom, CAP, 1))
    chunks[2 * j + 1] = jnp.where(lane < CAP, pltpu.roll(top, CAP, 1), bottom)


def row_blocks(value, groups):
    return [[value[8 * n : 8 * n + 8, 128 * g : 128 * (g + 1)] for n in range(2)] for g in range(groups)]


def adam(value, first, second, grad):
    first = BETA_ONE * first + (1.0 - BETA_ONE) * grad
    second = BETA_TWO * second + (1.0 - BETA_TWO) * grad * grad
    mhat = first * (1.0 / (1.0 - BETA_ONE**10))
    vhat = second * (1.0 / (1.0 - BETA_TWO**10))
    return value - LEARN * mhat / (jnp.sqrt(vhat) + EPSILON), first, second


def round_kernel(
    cam, params_in, moment1_in, moment2_in, dual_in, z_copy_in, z_table_in, rows_in, owner_in, slot_in,
    lists_in, counts_in, target_in,
    params_out, moment1_out, moment2_out, z_out, dual_out,
    params, moment1, moment2, dual, z_copy, z_table, rows, owner, slot, lists, counts, target,
    table, sheet, goal, e_all, t_all, parts, gathered,
    left, masks, masked, onehot, source, names, place,
    send, got, answers, returned, z_parts, d_parts, items, item_masked, item_hot, z_new, dual_new,
    in_sem, out_sem, s_mine, r_mine, s_send, r_send, s_back, r_back, s_z, r_z, s_d, r_d,
):
    block = lax.axis_index("blocks")
    view = lax.axis_index("views")

    pairs = [
        (lists_in, lists), (counts_in, counts), (params_in, params), (target_in, target),
        (rows_in, rows), (owner_in, owner), (slot_in, slot), (dual_in, dual), (z_copy_in, z_copy),
        (moment1_in, moment1), (moment2_in, moment2), (z_table_in, z_table),
    ]
    arriving = [pltpu.make_async_copy(there, here, in_sem.at[n]) for n, (there, here) in enumerate(pairs)]
    for copy in arriving:
        copy.start()
    barrier = pltpu.get_barrier_semaphore()

    def greet(k, _):
        pl.semaphore_signal(barrier, inc=1, device_id={"blocks": (block + k) % NBLK}, device_id_type=MESH)
        return 0

    lax.fori_loop(1, NBLK, greet, 0)
    for k in range(1, NVIEW):
        pl.semaphore_signal(barrier, inc=1, device_id={"views": (view + k) % NVIEW}, device_id_type=MESH)

    for copy in arriving[0:4]:
        copy.wait()
    slots_part, basis_part = render(
        cam, params, lists, counts, target, table, sheet, goal, e_all, t_all, parts
    )
    gathered[view, :, 0:PAIRS] = slots_part
    gathered[view, :, PAIRS:WIDE] = basis_part
    pl.semaphore_wait(barrier, NBLK - 1 + NVIEW - 1)
    view_copies = to_views(gathered, s_mine, r_mine, view)

    for copy in arriving[4:]:
        copy.wait()
    owned = lax.broadcasted_iota(I32, (NBLK, COPIES), 0) == owner[...]
    owned = jnp.where(owned, 1.0, 0.0)
    upper = lax.broadcasted_iota(I32, (128, 128), 0) < lax.broadcasted_iota(I32, (128, 128), 1)
    upper = jnp.where(upper, 1.0, 0.0).astype(BF16)
    ranks = []
    carry = jnp.zeros((NBLK, 1), F32)
    for j in range(COPIES // 128):
        part = owned[:, 128 * j : 128 * (j + 1)]
        ahead = jnp.dot(part.astype(BF16), upper, preferred_element_type=F32) + carry
        ranks.append(jnp.sum(part * ahead, axis=0, keepdims=True))
        carry = carry + jnp.sum(part, axis=1, keepdims=True)
    rank = jnp.concatenate(ranks, axis=1).astype(I32)
    place[...] = owner[...] * CAP + rank
    ident = lax.broadcasted_iota(I32, (1, COPIES), 1)
    ranked = (lax.broadcasted_iota(I32, (128, COPIES), 0) & (CAP - 1)) == rank
    coarse = jnp.where(ranked, (ident >> 5).astype(F32), 0.0).astype(BF16)
    fine = jnp.where(ranked, ((ident & 31) + 1).astype(F32), 0.0).astype(BF16)
    owned = owned.astype(BF16)
    names[...] = (
        32.0 * lax.dot_general(owned, coarse, NT, preferred_element_type=F32)
        + lax.dot_general(owned, fine, NT, preferred_element_type=F32)
    ).astype(I32)

    boundary = rows[...]
    lanes = slice(NVIEW * PAIRS, JOINT)
    left[NPAR:64, :] = jnp.zeros((64 - NPAR, JOINT), F32)
    left[0:NPAR, lanes] = dual[...] - z_copy[...]
    left[NPAR : NPAR + 1, lanes] = jnp.ones((1, COPIES), F32)

    def prepare(index, lanes):
        width = index.shape[1]
        group = jnp.broadcast_to(index >> 8, (16, width))
        for h in range(8):
            masks[16 * h : 16 * h + 16, lanes] = jnp.where(group == h, 1.0, 0.0).astype(BF16)
        hot = lax.broadcasted_iota(I32, (256, width), 0) == (index & 255)
        onehot[:, lanes] = jnp.where(hot, 1.0, 0.0).astype(BF16)

    prepare(boundary, lanes)

    for copy in view_copies:
        copy.wait()
    for v in range(NVIEW):
        lanes = slice(PAIRS * v, PAIRS * (v + 1))
        left[0:11, lanes] = gathered[v, 0:11, 0:PAIRS]
        colbasis = gathered[v, :, PAIRS : PAIRS + 1]
        for c in range(3):
            left[11 + 16 * c : 27 + 16 * c, lanes] = colbasis * gathered[v, 11 + c : 12 + c, 0:PAIRS]
        prepare(gathered[v, 14:15, 0:PAIRS].astype(I32), lanes)

    spot = lax.broadcasted_iota(I32, (16, JOINT), 0)
    high, low = split(jnp.where(spot == 15, left[NPAR : NPAR + 1, :], share_of(left, view)))
    for h in range(8):
        mask = masks[16 * h : 16 * h + 16, :]
        masked[32 * h : 32 * h + 16, :] = high * mask
        masked[32 * h + 16 : 32 * h + 32, :] = low * mask
    total = lax.dot_general(masked[0:256, :], onehot[...], NT, preferred_element_type=F32)
    value, first, second = share_of(params, view), share_of(moment1, view), share_of(moment2, view)
    moved = []
    for h in range(8):
        both = total[32 * h : 32 * h + 16, :] + total[32 * h + 16 : 32 * h + 32, :]
        lanes = slice(256 * h, 256 * (h + 1))
        grad = both + both[15:16, :] * value[:, lanes]
        moved.append(adam(value[:, lanes], first[:, lanes], second[:, lanes], grad)[0])
    moved = row_blocks(jnp.concatenate(moved, axis=1), GAUSS // 128)
    fetched = []
    for j in range(COPIES // 128):
        found = lane_gather(moved, wide(boundary[:, 128 * j : 128 * (j + 1)]), GAUSS // 128)
        fetched.append(jnp.concatenate(found, axis=0))
    spot = lax.broadcasted_iota(I32, (16, COPIES), 0)
    sums = jnp.concatenate(fetched, axis=1) + share_of(dual, view)
    source[...] = jnp.where(spot == 15, (slot[...] + 1).astype(F32), sums)
    lane = lax.broadcasted_iota(I32, (8, 128), 1)
    blocks_of = row_blocks(source, COPIES // 128)
    for j in range(NBLK // 2):
        name = jnp.where(lane < CAP, wide(names[2 * j : 2 * j + 1, :]), wide(names[2 * j + 1 : 2 * j + 2, :]))
        top, bottom = lane_gather(blocks_of, jnp.maximum(name - 1, 0), COPIES // 128)
        pack(jnp.where(name > 0, top, 0.0), jnp.where(name > 0, bottom, 0.0), send, j)
    to_blocks(send, got, s_send, r_send, block)

    high, low = split(left[...])
    for h in range(8):
        mask = masks[16 * h : 16 * h + 16, :]
        for n in range(4):
            masked[128 * h + 16 * n : 128 * h + 16 * n + 16, :] = high[16 * n : 16 * n + 16, :] * mask
            masked[128 * h + 64 + 16 * n : 128 * h + 80 + 16 * n, :] = low[16 * n : 16 * n + 16, :] * mask
    total = lax.dot_general(masked[...], onehot[...], NT, preferred_element_type=F32)
    for h in range(8):
        both = total[128 * h : 128 * h + 64, :] + total[128 * h + 64 : 128 * h + 128, :]
        lanes = slice(256 * h, 256 * (h + 1))
        value = params[:, lanes]
        grad = both[0:NPAR] + both[NPAR : NPAR + 1] * value
        params[:, lanes], moment1[:, lanes], moment2[:, lanes] = adam(
            value, moment1[:, lanes], moment2[:, lanes], grad
        )
    leaving = [
        pltpu.make_async_copy(here, there, out_sem.at[n])
        for n, (here, there) in enumerate(
            [(params, params_out), (moment1, moment1_out), (moment2, moment2_out), (z_new, z_out), (dual_new, dual_out)]
        )
    ]
    for copy in leaving[0:3]:
        copy.start()
    mine = share_of(z_table, view)
    wait_blocks(send, got, s_send, r_send, block)

    for j in range(NBLK // 2):
        top, bottom = unpack(got, j)
        items[0:8, 128 * j : 128 * (j + 1)] = top
        items[8:16, 128 * j : 128 * (j + 1)] = bottom
    label = items[15:16, :].astype(I32)
    index = jnp.maximum(label - 1, 0)
    last = lax.broadcasted_iota(I32, (16, NBLK * CAP), 0) == 15
    high, low = split(jnp.where(last, 1.0, items[...]))
    group = jnp.broadcast_to(jnp.where(label > 0, index >> 8, 4), (16, NBLK * CAP))
    for h in range(4):
        mask = jnp.where(group == h, 1.0, 0.0).astype(BF16)
        item_masked[32 * h : 32 * h + 16, :] = high * mask
        item_masked[32 * h + 16 : 32 * h + 32, :] = low * mask
    hot = lax.broadcasted_iota(I32, (256, NBLK * CAP), 0) == (index & 255)
    item_hot[...] = jnp.where(hot, 1.0, 0.0).astype(BF16)
    total = lax.dot_general(item_masked[...], item_hot[...], NT, preferred_element_type=F32)
    fresh = []
    for h in range(4):
        both = total[32 * h : 32 * h + 16, :] + total[32 * h + 16 : 32 * h + 32, :]
        fresh.append((mine[:, 256 * h : 256 * (h + 1)] + both) / (1.0 + both[15:16, :]))
    fresh = jnp.concatenate(fresh, axis=1)
    z_parts[view] = fresh
    answer = row_blocks(fresh, ROWS // 128)
    for j in range(NBLK // 2):
        top, bottom = lane_gather(answer, wide(index[:, 128 * j : 128 * (j + 1)]), ROWS // 128)
        pack(top, bottom, answers, j)
    to_blocks(answers, returned, s_back, r_back, block)
    z_copies = to_views(z_parts, s_z, r_z, view)
    for copy in z_copies:
        copy.wait()
    for v in range(NVIEW):
        count = min(SHARE, NPAR - SHARE * v)
        z_new[SHARE * v : SHARE * v + count, :] = z_parts[v, 0:count, :]
    leaving[3].start()
    wait_blocks(answers, returned, s_back, r_back, block)

    for j in range(NBLK // 2):
        top, bottom = unpack(returned, j)
        items[0:8, 128 * j : 128 * (j + 1)] = top
        items[8:16, 128 * j : 128 * (j + 1)] = bottom
    fetched = []
    answer = row_blocks(items, NBLK // 2)
    for j in range(COPIES // 128):
        found = lane_gather(answer, wide(place[:, 128 * j : 128 * (j + 1)]), NBLK // 2)
        fetched.append(jnp.concatenate(found, axis=0))
    d_parts[view] = source[...] - jnp.concatenate(fetched, axis=1)
    d_copies = to_views(d_parts, s_d, r_d, view)
    for copy in d_copies:
        copy.wait()
    for v in range(NVIEW):
        count = min(SHARE, NPAR - SHARE * v)
        dual_new[SHARE * v : SHARE * v + count, :] = d_parts[v, 0:count, :]
    leaving[4].start()
    for copy in leaving:
        copy.wait()


def finish_kernel(*refs):
    sources, targets, staged, in_sem, out_sem = refs[0:5], refs[5:10], refs[10:15], refs[15], refs[16]
    steps = []
    for n, ref in enumerate(sources):
        for piece in range(ref.shape[1] // ROWS):
            lanes = pl.ds(ROWS * piece, ROWS)
            at = len(steps)
            steps.append(
                (
                    pltpu.make_async_copy(ref.at[:, lanes], staged[n].at[:, lanes], in_sem.at[at]),
                    pltpu.make_async_copy(staged[n].at[:, lanes], targets[n].at[:, lanes], out_sem.at[at]),
                )
            )
    for arrive, _ in steps:
        arrive.start()
    for arrive, leave in steps:
        arrive.wait()
        leave.start()
    for _, leave in steps:
        leave.wait()


def anywhere():
    return pl.BlockSpec(memory_space=pl.ANY)


def local(
    params, moment1, moment2, dual, z_copy, z_table, boundary_rows, owner_block, owner_slot,
    tile_lists, tile_counts, cameras, target,
):
    shape = jax.ShapeDtypeStruct
    outs = (shape((NPAR, GAUSS), F32),) * 3 + (shape((NPAR, ROWS), F32), shape((NPAR, COPIES), F32))

    def f32(*dims):
        return pltpu.VMEM(dims, F32)

    def bf16(*dims):
        return pltpu.VMEM(dims, BF16)

    def i32(*dims):
        return pltpu.VMEM(dims, I32)

    chunks = f32(NBLK, 8, 128)
    dma = pltpu.SemaphoreType.DMA
    results = pl.pallas_call(
        round_kernel,
        out_shape=outs,
        in_specs=[pl.BlockSpec(memory_space=pltpu.SMEM)] + [anywhere()] * 12,
        out_specs=(anywhere(),) * 5,
        scratch_shapes=[
            f32(NPAR, GAUSS), f32(NPAR, GAUSS), f32(NPAR, GAUSS),
            f32(NPAR, COPIES), f32(NPAR, COPIES), f32(NPAR, ROWS),
            i32(1, COPIES), i32(1, COPIES), i32(1, COPIES), i32(TILES, DEPTH), i32(1, TILES), f32(3, TILES * PIXELS),
            f32(16, GAUSS), f32(PAIRS, 16), f32(48, PIXELS), f32(PAIRS, PIXELS), f32(PAIRS, PIXELS),
            bf16(10, PAIRS, PIXELS), f32(NVIEW, 16, WIDE),
            f32(64, JOINT), bf16(128, JOINT), bf16(1024, JOINT), bf16(256, JOINT),
            f32(16, COPIES), i32(NBLK, 128), i32(1, COPIES),
            chunks, chunks, chunks, chunks, f32(NVIEW, 16, ROWS), f32(NVIEW, 16, COPIES),
            f32(16, NBLK * CAP), bf16(128, NBLK * CAP), bf16(256, NBLK * CAP), f32(NPAR, ROWS), f32(NPAR, COPIES),
            dma((12,)), dma((5,)), dma((3,)), dma((3,)), dma, dma, dma, dma, dma((3,)), dma((3,)), dma((3,)), dma((3,)),
        ],
        compiler_params=pltpu.CompilerParams(
            collective_id=0, has_side_effects=True, vmem_limit_bytes=56 * 1024 * 1024
        ),
        name="round",
    )(
        cameras, params, moment1, moment2, dual, z_copy, z_table,
        boundary_rows.reshape(1, COPIES), owner_block.reshape(1, COPIES), owner_slot.reshape(1, COPIES),
        tile_lists, tile_counts.reshape(1, TILES), target,
    )
    return pl.pallas_call(
        finish_kernel,
        out_shape=outs,
        in_specs=[anywhere()] * 5,
        out_specs=(anywhere(),) * 5,
        scratch_shapes=[f32(*out.shape) for out in outs] + [dma((8,)), dma((8,))],
        compiler_params=pltpu.CompilerParams(vmem_limit_bytes=56 * 1024 * 1024),
        name="finish",
    )(*results)


def solution(mesh):
    whole, both = P(None, "blocks"), ("blocks", "views")
    placed = (whole,) * 6 + (P("blocks"), P("blocks", None), P("blocks"))
    placed += (P(both, None), P(both), P(both, None), P(None, both))
    return jax.shard_map(local, mesh=mesh, in_specs=placed, out_specs=(whole,) * 5, check_vma=False)
```

```python
import functools

import jax
import jax.numpy as jnp
from jax import lax
from jax.experimental import pallas as pl
from jax.experimental.pallas import tpu as pltpu
from jax.sharding import PartitionSpec as P

LEARN = 0.05
BETA_ONE = 0.9
BETA_TWO = 0.999
EPSILON = 1e-08

NPAR = 59
GAUSS = 2048
COPIES = 1024
ROWS = 1024
TILES = 16
DEPTH = 32
PAIRS = TILES * DEPTH
PIXELS = 256
NBLK = 64
NVIEW = 4
CAP = 64
SHARE = 15
JOINT = NVIEW * PAIRS + COPIES
UNROLL = 4

F32 = jnp.float32
BF16 = jnp.bfloat16
I32 = jnp.int32
MESH = pl.DeviceIdType.MESH
NT = (((1,), (1,)), ((), ()))


def lane_gather(source, index):
    low = index & 127
    high = index >> 7
    found = jnp.take_along_axis(source[0], low, axis=1)
    for g in range(1, len(source)):
        found = jnp.where(high == g, jnp.take_along_axis(source[g], low, axis=1), found)
    return found


def groups_of(value, rows):
    return [value[rows : rows + 8, 128 * g : 128 * (g + 1)] for g in range(value.shape[1] // 128)]


def fetch(value, rows, index):
    source = groups_of(value, rows)
    found = [lane_gather(source, wide(index[:, 128 * j : 128 * (j + 1)])) for j in range(index.shape[1] // 128)]
    return jnp.concatenate(found, axis=1)


def wide(row):
    return jnp.broadcast_to(row, (8, row.shape[1]))


def split(value):
    high = value.astype(BF16)
    return high, (value - high.astype(F32)).astype(BF16)


def share_of(ref, view):
    parts = []
    for v in range(NVIEW):
        end = min(SHARE * v + SHARE, NPAR)
        rows = [ref[SHARE * v : SHARE * v + 7, :], jnp.zeros((1, ref.shape[1]), F32), ref[SHARE * v + 7 : end, :]]
        if end < SHARE * v + SHARE:
            rows.append(jnp.zeros((SHARE * v + SHARE - end, ref.shape[1]), F32))
        parts.append(jnp.concatenate(rows, axis=0))
    result = parts[3]
    for v in range(3):
        result = jnp.where(view == v, parts[v], result)
    return result


def assemble(target, part, v, wave):
    start = SHARE * v + 7 * wave
    count = min(7 + wave, NPAR - start)
    target[start : start + count, :] = part[0:count, :]


def render(cam, params, lists, counts, target, table, sheet, goal, e_all, t_all, parts):
    table[0:11, :] = params[0:11, :]
    table[14:16, :] = jnp.zeros((2, GAUSS), F32)
    for c in range(3):
        colour = cam[0, 8] * params[11 + 16 * c : 12 + 16 * c, :]
        for k in range(1, 16):
            row = 11 + 16 * c + k
            colour += cam[0, 8 + k] * params[row : row + 1, :]
        table[11 + c : 12 + c, :] = colour + 0.5
    for c in range(3):
        for t in range(TILES):
            goal[16 * c + t : 16 * c + t + 1, :] = target[c : c + 1, PIXELS * t : PIXELS * (t + 1)]

    turned = lists[...].astype(F32).T
    slots = lax.broadcasted_iota(I32, (DEPTH, TILES), 0)
    turned = jnp.where(slots < counts[...], turned, turned + GAUSS)
    turned = jnp.concatenate([turned, jnp.zeros((DEPTH, 128 - TILES), F32)], axis=1)
    turns = [turned] + [pltpu.roll(turned, TILES * m, 1) for m in range(1, 8)]
    lane = lax.broadcasted_iota(I32, (1, 128), 1)
    pieces = []
    for j in range(PAIRS // 128):
        row = turns[0][8 * j : 8 * j + 1, :]
        for m in range(1, 8):
            row = jnp.where(lane >> 4 == m, turns[m][8 * j + m : 8 * j + m + 1, :], row)
        pieces.append(row)
    coded = jnp.concatenate(pieces, axis=1).astype(I32)
    live = jnp.where(coded < GAUSS, 1.0, 0.0)
    index = coded & (GAUSS - 1)
    picked = []
    for j in range(PAIRS // 128):
        lanes = wide(index[:, 128 * j : 128 * (j + 1)])
        picked.append(jnp.concatenate([lane_gather(groups_of(table, 8 * n), lanes) for n in range(2)], axis=0))
    picked = jnp.concatenate(picked, axis=1)

    def take(row):
        return picked[row : row + 1, :]

    jac = [[cam[0, 3 * i + j] for j in range(3)] for i in range(2)]
    centre = [take(j) for j in range(3)]
    scale = [jnp.exp(take(3 + k)) for k in range(3)]
    quat = [take(6 + k) for k in range(4)]
    norm = 1.0 / jnp.sqrt(quat[0] * quat[0] + quat[1] * quat[1] + quat[2] * quat[2] + quat[3] * quat[3])
    qw, qx, qy, qz = [q * norm for q in quat]
    rot = [
        [1 - 2 * (qy * qy + qz * qz), 2 * (qx * qy - qw * qz), 2 * (qx * qz + qw * qy)],
        [2 * (qx * qy + qw * qz), 1 - 2 * (qx * qx + qz * qz), 2 * (qy * qz - qw * qx)],
        [2 * (qx * qz - qw * qy), 2 * (qy * qz + qw * qx), 1 - 2 * (qx * qx + qy * qy)],
    ]
    mixed = [
        [(jac[i][0] * rot[0][k] + jac[i][1] * rot[1][k] + jac[i][2] * rot[2][k]) * scale[k] for k in range(3)]
        for i in range(2)
    ]

    def inner(a, b):
        return a[0] * b[0] + a[1] * b[1] + a[2] * b[2]

    first = inner(mixed[0], mixed[0]) + 0.01
    second = inner(mixed[1], mixed[1]) + 0.01
    cross = inner(mixed[0], mixed[1])
    det = first * second - cross * cross
    con0, con1, con2 = second / det, -cross / det, first / det
    cu = inner(jac[0], centre) + cam[0, 6]
    cw = inner(jac[1], centre) + cam[0, 7]
    opacity = 1.0 / (1.0 + jnp.exp(-take(10)))
    shown = opacity * live

    rows = [cu, cw, con0, 2.0 * con1, con2, shown, take(11), take(12), take(13)]
    rows = jnp.concatenate(rows + [jnp.zeros((7, PAIRS), F32)], axis=0)
    sheet[...] = rows.T

    tile = lax.broadcasted_iota(I32, (TILES, PIXELS), 0)
    pixel = lax.broadcasted_iota(I32, (TILES, PIXELS), 1)
    pos_u = (((tile & 3) * 16 + (pixel & 15)).astype(F32) + 0.5) / 32.0 - 1.0
    pos_w = (((tile >> 2) * 16 + (pixel >> 4)).astype(F32) + 0.5) / 32.0 - 1.0

    def at_slot(s):
        return pl.ds(pl.multiple_of(TILES * s, TILES), TILES)

    def column(s, f):
        return jnp.broadcast_to(sheet[at_slot(s), f : f + 1], (TILES, PIXELS))

    def forward(step, state):
        image, passed = list(state[0:3]), state[3]
        for s in [UNROLL * step + n for n in range(UNROLL)]:
            du = pos_u - column(s, 0)
            dw = pos_w - column(s, 1)
            quad = (column(s, 2) * du + column(s, 3) * dw) * du + column(s, 4) * dw * dw
            bell = jnp.exp(-0.5 * quad)
            alpha = jnp.minimum(column(s, 5) * bell, 0.99)
            weight = alpha * passed
            for c in range(3):
                image[c] = image[c] + column(s, 6 + c) * weight
            e_all[at_slot(s), :] = bell
            t_all[at_slot(s), :] = passed
            passed = passed - weight
        return (*image, passed)

    zero = jnp.zeros((TILES, PIXELS), F32)
    image = lax.fori_loop(0, DEPTH // UNROLL, forward, (zero, zero, zero, zero + 1.0))
    diff = [image[c] - goal[16 * c : 16 * c + 16, :] for c in range(3)]

    def backward(step, behind):
        for s in [DEPTH - 1 - UNROLL * step - n for n in range(UNROLL)]:
            bell = e_all[at_slot(s), :]
            before = t_all[at_slot(s), :]
            raw = column(s, 5) * bell
            alpha = jnp.minimum(raw, 0.99)
            glow = diff[0] * column(s, 6) + diff[1] * column(s, 7) + diff[2] * column(s, 8)
            slope = before * (glow - behind)
            slope = jnp.where(raw < 0.99, slope, jnp.where(raw == 0.99, 0.5 * slope, 0.0))
            behind = behind + alpha * (glow - behind)
            weight = alpha * before
            sums = [-0.5 * raw * slope, bell * slope] + [diff[c] * weight for c in range(3)]
            for n, value in enumerate(sums):
                high, low = split(value)
                parts[2 * n, at_slot(s), :] = high
                parts[2 * n + 1, at_slot(s), :] = low
        return behind

    lax.fori_loop(0, DEPTH // UNROLL, backward, zero)

    which = lax.broadcasted_iota(I32, (16, PIXELS), 0)
    place = lax.broadcasted_iota(I32, (16, PIXELS), 1)
    in_u = ((place & 15).astype(F32) - 7.5) / 32.0
    in_w = ((place >> 4).astype(F32) - 7.5) / 32.0
    basis = jnp.where(which == 0, 1.0, 0.0)
    basis = jnp.where(which == 1, in_u, basis)
    basis = jnp.where(which == 2, in_w, basis)
    basis = jnp.where(which == 3, in_u * in_u, basis)
    basis = jnp.where(which == 4, in_u * in_w, basis)
    basis = jnp.where(which == 5, in_w * in_w, basis)
    basis = basis.astype(BF16)

    def over_pixels(n):
        return lax.dot_general(basis, parts[2 * n], NT, preferred_element_type=F32) + lax.dot_general(
            basis, parts[2 * n + 1], NT, preferred_element_type=F32
        )

    moments = over_pixels(0)
    m1, mu, mw, muu, muw, mww = [moments[n : n + 1, :] for n in range(6)]
    g_opacity = over_pixels(1)[0:1, :] * live
    g_colour = [over_pixels(2 + c)[0:1, :] for c in range(3)]
    at = lax.broadcasted_iota(I32, (1, PAIRS), 1) & 15
    off_u = cu - (((at & 3) * 16 + 8).astype(F32) / 32.0 - 1.0)
    off_w = cw - (((at >> 2) * 16 + 8).astype(F32) / 32.0 - 1.0)
    s_u = mu - off_u * m1
    s_w = mw - off_w * m1
    g_con0 = muu - off_u * (mu + s_u)
    g_con1 = 2.0 * (muw - off_u * mw - off_w * s_u)
    g_con2 = mww - off_w * (mw + s_w)
    g_cu = -2.0 * (con0 * s_u + con1 * s_w)
    g_cw = -2.0 * (con1 * s_u + con2 * s_w)

    g_first = -(con0 * con0 * g_con0 + con0 * con1 * g_con1 + con1 * con1 * g_con2)
    g_second = -(con1 * con1 * g_con0 + con1 * con2 * g_con1 + con2 * con2 * g_con2)
    g_cross = -(2.0 * con0 * con1 * g_con0 + (con0 * con2 + con1 * con1) * g_con1 + 2.0 * con1 * con2 * g_con2)
    g_mixed = [
        [2.0 * g_first * mixed[0][k] + g_cross * mixed[1][k] for k in range(3)],
        [2.0 * g_second * mixed[1][k] + g_cross * mixed[0][k] for k in range(3)],
    ]
    g_scale = [g_mixed[0][k] * mixed[0][k] + g_mixed[1][k] * mixed[1][k] for k in range(3)]
    r = [
        [(jac[0][j] * g_mixed[0][k] + jac[1][j] * g_mixed[1][k]) * scale[k] for k in range(3)] for j in range(3)
    ]
    h_w = 2 * (qz * (r[1][0] - r[0][1]) + qy * (r[0][2] - r[2][0]) + qx * (r[2][1] - r[1][2]))
    h_x = 2 * (
        qy * (r[0][1] + r[1][0]) + qz * (r[0][2] + r[2][0]) + qw * (r[2][1] - r[1][2]) - 2 * qx * (r[1][1] + r[2][2])
    )
    h_y = 2 * (
        qx * (r[0][1] + r[1][0]) + qz * (r[1][2] + r[2][1]) + qw * (r[0][2] - r[2][0]) - 2 * qy * (r[0][0] + r[2][2])
    )
    h_z = 2 * (
        qx * (r[0][2] + r[2][0]) + qy * (r[1][2] + r[2][1]) + qw * (r[1][0] - r[0][1]) - 2 * qz * (r[0][0] + r[1][1])
    )
    along = qw * h_w + qx * h_x + qy * h_y + qz * h_z
    g_quat = [(h - q * along) * norm for h, q in ((h_w, qw), (h_x, qx), (h_y, qy), (h_z, qz))]
    g_centre = [jac[0][j] * g_cu + jac[1][j] * g_cw for j in range(3)]
    g_logit = g_opacity * opacity * (1.0 - opacity)
    along_row = lax.broadcasted_iota(I32, (1, PAIRS), 1)
    colbasis = jnp.zeros((1, PAIRS), F32)
    for k in range(16):
        colbasis = jnp.where(along_row == k, cam[0, 8 + k], colbasis)
    sent = g_centre + g_scale + g_quat + [g_logit] + g_colour + [index.astype(F32), colbasis]
    return jnp.concatenate(sent, axis=0)


def to_blocks(outgoing, incoming, send_sem, recv_sem, block, wave):
    def one(k, _):
        other = (block + k) % NBLK
        pltpu.make_async_remote_copy(
            src_ref=outgoing.at[wave, other],
            dst_ref=incoming.at[wave, block],
            send_sem=send_sem.at[wave],
            recv_sem=recv_sem.at[wave],
            device_id={"blocks": other},
            device_id_type=MESH,
        ).start()
        return 0

    lax.fori_loop(1, NBLK, one, 0)
    incoming[wave, block] = outgoing[wave, block]


def wait_blocks(outgoing, incoming, send_sem, recv_sem, block, wave):
    whole = pltpu.make_async_remote_copy(
        src_ref=outgoing.at[wave, pl.ds(0, NBLK - 1)],
        dst_ref=incoming.at[wave, pl.ds(0, NBLK - 1)],
        send_sem=send_sem.at[wave],
        recv_sem=recv_sem.at[wave],
        device_id={"blocks": block},
        device_id_type=MESH,
    )
    whole.wait_send()
    whole.wait_recv()


def to_views(piece, send_sem, recv_sem, view):
    copies = []
    for k in range(1, NVIEW):
        copy = pltpu.make_async_remote_copy(
            src_ref=piece,
            dst_ref=piece,
            send_sem=send_sem.at[k - 1],
            recv_sem=recv_sem.at[k - 1],
            device_id={"views": (view + k) % NVIEW},
            device_id_type=MESH,
        )
        copy.start()
        copies.append(copy)
    return copies


def refold(value):
    left = lax.broadcasted_iota(I32, (8, 128), 1) < CAP
    upper = lax.broadcasted_iota(I32, (8, 128), 0) < 4
    return jnp.where(left == upper, value, pltpu.roll(pltpu.roll(value, CAP, 1), 4, 0))


def pack(value, chunks, wave, j):
    folded = refold(value)
    chunks[wave, 2 * j] = folded[0:4]
    chunks[wave, 2 * j + 1] = folded[4:8]


def unpack(chunks, wave, j):
    return refold(jnp.concatenate([chunks[wave, 2 * j], chunks[wave, 2 * j + 1]], axis=0))


def adam(value, first, second, grad):
    first = BETA_ONE * first + (1.0 - BETA_ONE) * grad
    second = BETA_TWO * second + (1.0 - BETA_TWO) * grad * grad
    mhat = first * (1.0 / (1.0 - BETA_ONE**10))
    vhat = second * (1.0 / (1.0 - BETA_TWO**10))
    return value - LEARN * mhat / (jnp.sqrt(vhat) + EPSILON), first, second


def round_kernel(
    cam, params_in, moment1_in, moment2_in, dual_in, z_copy_in, z_table_in, rows_in, owner_in, slot_in,
    lists_in, counts_in, target_in,
    params_out, moment1_out, moment2_out, z_out, dual_out,
    params, moment1, moment2, dual, z_copy, z_table, rows, owner, slot, lists, counts, target,
    table, sheet, goal, e_all, t_all, parts, gathered,
    left, masks, masked, pen_masked, onehot, source, names, place, s_value, s_first, s_second, s_dual, s_table,
    send, got, answers, returned, z_parts, d_parts, items, item_masks, item_masked, item_hot, z_new, dual_new,
    in_sem, out_sem, s_mine, r_mine, s_send, r_send, s_back, r_back, s_z, r_z, s_d, r_d,
):
    block = lax.axis_index("blocks")
    view = lax.axis_index("views")

    pairs = [
        (lists_in, lists), (counts_in, counts), (params_in, params), (target_in, target),
        (rows_in, rows), (owner_in, owner), (slot_in, slot), (dual_in, dual), (z_copy_in, z_copy),
        (moment1_in, moment1), (moment2_in, moment2), (z_table_in, z_table),
    ]
    arriving = [pltpu.make_async_copy(there, here, in_sem.at[n]) for n, (there, here) in enumerate(pairs)]
    for copy in arriving:
        copy.start()
    barrier = pltpu.get_barrier_semaphore()

    def greet(k, _):
        pl.semaphore_signal(barrier, inc=1, device_id={"blocks": (block + k) % NBLK}, device_id_type=MESH)
        return 0

    lax.fori_loop(1, NBLK, greet, 0)
    for k in range(1, NVIEW):
        pl.semaphore_signal(barrier, inc=1, device_id={"views": (view + k) % NVIEW}, device_id_type=MESH)

    for copy in arriving[0:4]:
        copy.wait()
    gathered[view] = render(cam, params, lists, counts, target, table, sheet, goal, e_all, t_all, parts)
    pl.semaphore_wait(barrier, NBLK - 1 + NVIEW - 1)
    view_copies = to_views(gathered.at[view], s_mine, r_mine, view)

    for copy in arriving[4:]:
        copy.wait()
    owned = lax.broadcasted_iota(I32, (NBLK, COPIES), 0) == owner[...]
    owned = jnp.where(owned, 1.0, 0.0)
    upper = lax.broadcasted_iota(I32, (128, 128), 0) < lax.broadcasted_iota(I32, (128, 128), 1)
    upper = jnp.where(upper, 1.0, 0.0).astype(BF16)
    ranks = []
    carry = jnp.zeros((NBLK, 1), F32)
    for j in range(COPIES // 128):
        part = owned[:, 128 * j : 128 * (j + 1)]
        ahead = jnp.dot(part.astype(BF16), upper, preferred_element_type=F32) + carry
        ranks.append(jnp.sum(part * ahead, axis=0, keepdims=True))
        carry = carry + jnp.sum(part, axis=1, keepdims=True)
    rank = jnp.concatenate(ranks, axis=1).astype(I32)
    place[...] = owner[...] * CAP + rank
    ident = lax.broadcasted_iota(I32, (1, COPIES), 1)
    ranked = (lax.broadcasted_iota(I32, (128, COPIES), 0) & (CAP - 1)) == rank
    coarse = jnp.where(ranked, (ident >> 5).astype(F32), 0.0).astype(BF16)
    fine = jnp.where(ranked, ((ident & 31) + 1).astype(F32), 0.0).astype(BF16)
    owned = owned.astype(BF16)
    names[...] = (
        32.0 * lax.dot_general(owned, coarse, NT, preferred_element_type=F32)
        + lax.dot_general(owned, fine, NT, preferred_element_type=F32)
    ).astype(I32)

    boundary = rows[...]
    lanes = slice(NVIEW * PAIRS, JOINT)
    left[NPAR:64, :] = jnp.zeros((64 - NPAR, JOINT), F32)
    left[0:NPAR, lanes] = dual[...] - z_copy[...]
    left[NPAR : NPAR + 1, lanes] = jnp.ones((1, COPIES), F32)

    def prepare(index, lanes):
        width = index.shape[1]
        group = jnp.broadcast_to(index >> 8, (16, width))
        for h in range(8):
            masks[16 * h : 16 * h + 16, lanes] = jnp.where(group == h, 1.0, 0.0).astype(BF16)
        hot = lax.broadcasted_iota(I32, (256, width), 0) == (index & 255)
        onehot[:, lanes] = jnp.where(hot, 1.0, 0.0).astype(BF16)

    prepare(boundary, lanes)

    s_value[...] = share_of(params, view)
    s_first[...] = share_of(moment1, view)
    s_second[...] = share_of(moment2, view)
    s_dual[...] = share_of(dual, view)
    s_table[...] = share_of(z_table, view)

    def share_masked(target, value, at):
        high, low = split(value)
        for h in range(8):
            mask = masks[16 * h : 16 * h + 16, at]
            target[32 * h : 32 * h + 16, :] = high * mask
            target[32 * h + 16 : 32 * h + 32, :] = low * mask

    spot = lax.broadcasted_iota(I32, (16, COPIES), 0)
    share_masked(pen_masked, jnp.where(spot == 7, 1.0, share_of(left.at[:, lanes], view)), lanes)
    pen_total = lax.dot_general(pen_masked[...], onehot[:, lanes], NT, preferred_element_type=F32)

    for copy in view_copies:
        copy.wait()
    diagonal = lax.broadcasted_iota(I32, (16, 128), 0) == lax.broadcasted_iota(I32, (16, 128), 1)
    for v in range(NVIEW):
        lanes = slice(PAIRS * v, PAIRS * (v + 1))
        left[0:11, lanes] = gathered[v, 0:11, :]
        colbasis = jnp.sum(jnp.where(diagonal, gathered[v, 15:16, 0:128], 0.0), axis=1, keepdims=True)
        for c in range(3):
            left[11 + 16 * c : 27 + 16 * c, lanes] = colbasis * gathered[v, 11 + c : 12 + c, :]
        prepare(gathered[v, 14:15, :].astype(I32), lanes)

    lanes = slice(0, NVIEW * PAIRS)
    view_masked = masked.at[0:256, lanes]
    share_masked(view_masked, share_of(left.at[:, lanes], view), lanes)
    total = pen_total + lax.dot_general(view_masked[...], onehot[:, lanes], NT, preferred_element_type=F32)
    moved = []
    for h in range(8):
        both = total[32 * h : 32 * h + 16, :] + total[32 * h + 16 : 32 * h + 32, :]
        lanes = slice(256 * h, 256 * (h + 1))
        value = s_value[:, lanes]
        grad = both + both[7:8, :] * value
        moved.append(adam(value, s_first[:, lanes], s_second[:, lanes], grad)[0])
    moved = jnp.concatenate(moved, axis=1)
    lane = lax.broadcasted_iota(I32, (8, 128), 1)
    spot = lax.broadcasted_iota(I32, (8, COPIES), 0)
    for wave in range(2):
        at = slice(8 * wave, 8 * wave + 8)
        sums = fetch(moved, 8 * wave, boundary) + s_dual[at, :]
        if wave == 0:
            sums = jnp.where(spot == 7, (slot[...] + 1).astype(F32), sums)
        source[at, :] = sums
        blocks_of = groups_of(source, 8 * wave)
        for j in range(NBLK // 2):
            name = jnp.where(lane < CAP, wide(names[2 * j : 2 * j + 1, :]), wide(names[2 * j + 1 : 2 * j + 2, :]))
            found = lane_gather(blocks_of, jnp.maximum(name - 1, 0))
            pack(jnp.where(name > 0, found, 0.0), send, wave, j)
        to_blocks(send, got, s_send, r_send, block, wave)

    high, low = split(left[...])
    for h in range(8):
        mask = masks[16 * h : 16 * h + 16, :]
        for n in range(4):
            masked[128 * h + 16 * n : 128 * h + 16 * n + 16, :] = high[16 * n : 16 * n + 16, :] * mask
            masked[128 * h + 64 + 16 * n : 128 * h + 80 + 16 * n, :] = low[16 * n : 16 * n + 16, :] * mask
    total = lax.dot_general(masked[...], onehot[...], NT, preferred_element_type=F32)
    for h in range(8):
        both = total[128 * h : 128 * h + 64, :] + total[128 * h + 64 : 128 * h + 128, :]
        lanes = slice(256 * h, 256 * (h + 1))
        value = params[:, lanes]
        grad = both[0:NPAR] + both[NPAR : NPAR + 1] * value
        params[:, lanes], moment1[:, lanes], moment2[:, lanes] = adam(
            value, moment1[:, lanes], moment2[:, lanes], grad
        )
    leaving = [
        pltpu.make_async_copy(here, there, out_sem.at[n])
        for n, (here, there) in enumerate(
            [(params, params_out), (moment1, moment1_out), (moment2, moment2_out), (z_new, z_out), (dual_new, dual_out)]
        )
    ]
    for copy in leaving[0:3]:
        copy.start()
    last = lax.broadcasted_iota(I32, (8, NBLK * CAP), 0) == 7
    for wave in range(2):
        at = slice(8 * wave, 8 * wave + 8)
        wait_blocks(send, got, s_send, r_send, block, wave)
        for j in range(NBLK // 2):
            items[at, 128 * j : 128 * (j + 1)] = unpack(got, wave, j)
        value = items[at, :]
        if wave == 0:
            label = items[7:8, :].astype(I32)
            index = jnp.maximum(label - 1, 0)
            group = jnp.broadcast_to(jnp.where(label > 0, index >> 8, 4), (16, NBLK * CAP))
            for h in range(4):
                item_masks[16 * h : 16 * h + 16, :] = jnp.where(group == h, 1.0, 0.0).astype(BF16)
            hot = lax.broadcasted_iota(I32, (256, NBLK * CAP), 0) == (index & 255)
            item_hot[...] = jnp.where(hot, 1.0, 0.0).astype(BF16)
            value = jnp.where(last, 1.0, value)
        high = value.astype(BF16).astype(F32)
        both = jnp.concatenate([high, value - high], axis=0).astype(BF16)
        for h in range(4):
            item_masked[16 * h : 16 * h + 16, :] = both * item_masks[16 * h : 16 * h + 16, :]
        total = lax.dot_general(item_masked[...], item_hot[...], NT, preferred_element_type=F32)
        total = jnp.concatenate([total[16 * h : 16 * h + 8, :] + total[16 * h + 8 : 16 * h + 16, :] for h in range(4)], axis=1)
        if wave == 0:
            number = 1.0 + total[7:8, :]
        fresh = (s_table[at, :] + total) / number
        z_parts[view, at, :] = fresh
        answer = groups_of(fresh, 0)
        for j in range(NBLK // 2):
            pack(lane_gather(answer, wide(index[:, 128 * j : 128 * (j + 1)])), answers, wave, j)
        to_blocks(answers, returned, s_back, r_back, block, wave)
    z_copies = to_views(z_parts.at[view], s_z, r_z, view)

    d_copies = []
    for wave in range(2):
        at = slice(8 * wave, 8 * wave + 8)
        wait_blocks(answers, returned, s_back, r_back, block, wave)
        for j in range(NBLK // 2):
            items[at, 128 * j : 128 * (j + 1)] = unpack(returned, wave, j)
        d_parts[wave, view] = source[at, :] - fetch(items, 8 * wave, place)
        d_copies.append(to_views(d_parts.at[wave, view], s_d.at[wave], r_d.at[wave], view))
        if wave == 0:
            for copy in z_copies:
                copy.wait()
            for v in range(NVIEW):
                for part in range(2):
                    assemble(z_new, z_parts.at[v, 8 * part : 8 * part + 8], v, part)
            leaving[3].start()
    for wave in range(2):
        for copy in d_copies[wave]:
            copy.wait()
        for v in range(NVIEW):
            assemble(dual_new, d_parts.at[wave, v], v, wave)
    leaving[4].start()
    for copy in leaving:
        copy.wait()


def finish_kernel(*refs):
    sources, targets, staged, in_sem, out_sem = refs[0:5], refs[5:10], refs[10:15], refs[15], refs[16]
    steps = []
    for n, ref in enumerate(sources):
        for piece in range(ref.shape[1] // ROWS):
            lanes = pl.ds(ROWS * piece, ROWS)
            at = len(steps)
            steps.append(
                (
                    pltpu.make_async_copy(ref.at[:, lanes], staged[n].at[:, lanes], in_sem.at[at]),
                    pltpu.make_async_copy(staged[n].at[:, lanes], targets[n].at[:, lanes], out_sem.at[at]),
                )
            )
    for arrive, _ in steps:
        arrive.start()
    for arrive, leave in steps:
        arrive.wait()
        leave.start()
    for _, leave in steps:
        leave.wait()


def anywhere():
    return pl.BlockSpec(memory_space=pl.ANY)


def local(
    params, moment1, moment2, dual, z_copy, z_table, boundary_rows, owner_block, owner_slot,
    tile_lists, tile_counts, cameras, target,
):
    shape = jax.ShapeDtypeStruct
    outs = (shape((NPAR, GAUSS), F32),) * 3 + (shape((NPAR, ROWS), F32), shape((NPAR, COPIES), F32))

    def f32(*dims):
        return pltpu.VMEM(dims, F32)

    def bf16(*dims):
        return pltpu.VMEM(dims, BF16)

    def i32(*dims):
        return pltpu.VMEM(dims, I32)

    chunks = f32(2, NBLK, 4, 128)
    dma = pltpu.SemaphoreType.DMA
    results = pl.pallas_call(
        round_kernel,
        out_shape=outs,
        in_specs=[pl.BlockSpec(memory_space=pltpu.SMEM)] + [anywhere()] * 12,
        out_specs=(anywhere(),) * 5,
        scratch_shapes=[
            f32(NPAR, GAUSS), f32(NPAR, GAUSS), f32(NPAR, GAUSS),
            f32(NPAR, COPIES), f32(NPAR, COPIES), f32(NPAR, ROWS),
            i32(1, COPIES), i32(1, COPIES), i32(1, COPIES), i32(TILES, DEPTH), i32(1, TILES), f32(3, TILES * PIXELS),
            f32(16, GAUSS), f32(PAIRS, 16), f32(48, PIXELS), f32(PAIRS, PIXELS), f32(PAIRS, PIXELS),
            bf16(10, PAIRS, PIXELS), f32(NVIEW, 16, PAIRS),
            f32(64, JOINT), bf16(128, JOINT), bf16(1024, JOINT), bf16(256, COPIES), bf16(256, JOINT),
            f32(16, COPIES), i32(NBLK, 128), i32(1, COPIES),
            f32(16, GAUSS), f32(16, GAUSS), f32(16, GAUSS), f32(16, COPIES), f32(16, ROWS),
            chunks, chunks, chunks, chunks, f32(NVIEW, 16, ROWS), f32(2, NVIEW, 8, COPIES),
            f32(16, NBLK * CAP), bf16(64, NBLK * CAP), bf16(64, NBLK * CAP), bf16(256, NBLK * CAP), f32(NPAR, ROWS), f32(NPAR, COPIES),
            dma((12,)), dma((5,)), dma((3,)), dma((3,)), dma((2,)), dma((2,)), dma((2,)), dma((2,)),
            dma((3,)), dma((3,)), dma((2, 3)), dma((2, 3)),
        ],
        compiler_params=pltpu.CompilerParams(
            collective_id=0, has_side_effects=True, vmem_limit_bytes=56 * 1024 * 1024
        ),
        name="round",
    )(
        cameras, params, moment1, moment2, dual, z_copy, z_table,
        boundary_rows.reshape(1, COPIES), owner_block.reshape(1, COPIES), owner_slot.reshape(1, COPIES),
        tile_lists, tile_counts.reshape(1, TILES), target,
    )
    return pl.pallas_call(
        finish_kernel,
        out_shape=outs,
        in_specs=[anywhere()] * 5,
        out_specs=(anywhere(),) * 5,
        scratch_shapes=[f32(*out.shape) for out in outs] + [dma((8,)), dma((8,))],
        compiler_params=pltpu.CompilerParams(vmem_limit_bytes=56 * 1024 * 1024),
        name="finish",
    )(*results)


def solution(mesh):
    whole, both = P(None, "blocks"), ("blocks", "views")
    placed = (whole,) * 6 + (P("blocks"), P("blocks", None), P("blocks"))
    placed += (P(both, None), P(both), P(both, None), P(None, both))
    return jax.shard_map(local, mesh=mesh, in_specs=placed, out_specs=(whole,) * 5, check_vma=False)
```

```python
import functools

import jax
import jax.numpy as jnp
from jax import lax
from jax.experimental import pallas as pl
from jax.experimental.pallas import tpu as pltpu
from jax.sharding import PartitionSpec as P

LEARN = 0.05
BETA_ONE = 0.9
BETA_TWO = 0.999
EPSILON = 1e-08

NPAR = 59
GAUSS = 2048
COPIES = 1024
ROWS = 1024
TILES = 16
DEPTH = 32
PAIRS = TILES * DEPTH
PIXELS = 256
NBLK = 64
PLANE = 8
NVIEW = 4
CAP = 64
SHARE = 15
JOINT = NVIEW * PAIRS + COPIES
UNROLL = 32

F32 = jnp.float32
BF16 = jnp.bfloat16
I32 = jnp.int32
MESH = pl.DeviceIdType.MESH
NT = (((1,), (1,)), ((), ()))


def lane_gather(source, index):
    low = index & 127
    high = index >> 7
    found = jnp.take_along_axis(source[0], low, axis=1)
    for g in range(1, len(source)):
        found = jnp.where(high == g, jnp.take_along_axis(source[g], low, axis=1), found)
    return found


def groups_of(value, rows):
    return [value[rows : rows + 8, 128 * g : 128 * (g + 1)] for g in range(value.shape[1] // 128)]


def fetch(value, rows, index):
    source = groups_of(value, rows)
    found = [lane_gather(source, wide(index[:, 128 * j : 128 * (j + 1)])) for j in range(index.shape[1] // 128)]
    return jnp.concatenate(found, axis=1)


def wide(row):
    return jnp.broadcast_to(row, (8, row.shape[1]))


def split(value):
    high = value.astype(BF16)
    return high, (value - high.astype(F32)).astype(BF16)


def share_of(ref, view):
    parts = []
    for v in range(NVIEW):
        end = min(SHARE * v + SHARE, NPAR)
        rows = [ref[SHARE * v : SHARE * v + 7, :], jnp.zeros((1, ref.shape[1]), F32), ref[SHARE * v + 7 : end, :]]
        if end < SHARE * v + SHARE:
            rows.append(jnp.zeros((SHARE * v + SHARE - end, ref.shape[1]), F32))
        parts.append(jnp.concatenate(rows, axis=0))
    result = parts[3]
    for v in range(3):
        result = jnp.where(view == v, parts[v], result)
    return result


def assemble(target, part, v, wave):
    start = SHARE * v + 7 * wave
    count = min(7 + wave, NPAR - start)
    target[start : start + count, :] = part[0:count, :]


def render(cam, params, lists, counts, target, table, sheet, goal, e_all, t_all, parts):
    table[0:11, :] = params[0:11, :]
    table[14:16, :] = jnp.zeros((2, GAUSS), F32)
    for c in range(3):
        colour = cam[0, 8] * params[11 + 16 * c : 12 + 16 * c, :]
        for k in range(1, 16):
            row = 11 + 16 * c + k
            colour += cam[0, 8 + k] * params[row : row + 1, :]
        table[11 + c : 12 + c, :] = colour + 0.5
    for c in range(3):
        for t in range(TILES):
            goal[16 * c + t : 16 * c + t + 1, :] = target[c : c + 1, PIXELS * t : PIXELS * (t + 1)]

    turned = lists[...].astype(F32).T
    slots = lax.broadcasted_iota(I32, (DEPTH, TILES), 0)
    turned = jnp.where(slots < counts[...], turned, turned + GAUSS)
    turned = jnp.concatenate([turned, jnp.zeros((DEPTH, 128 - TILES), F32)], axis=1)
    turns = [turned] + [pltpu.roll(turned, TILES * m, 1) for m in range(1, 8)]
    lane = lax.broadcasted_iota(I32, (1, 128), 1)
    pieces = []
    for j in range(PAIRS // 128):
        row = turns[0][8 * j : 8 * j + 1, :]
        for m in range(1, 8):
            row = jnp.where(lane >> 4 == m, turns[m][8 * j + m : 8 * j + m + 1, :], row)
        pieces.append(row)
    coded = jnp.concatenate(pieces, axis=1).astype(I32)
    live = jnp.where(coded < GAUSS, 1.0, 0.0)
    index = coded & (GAUSS - 1)
    picked = []
    for j in range(PAIRS // 128):
        lanes = wide(index[:, 128 * j : 128 * (j + 1)])
        picked.append(jnp.concatenate([lane_gather(groups_of(table, 8 * n), lanes) for n in range(2)], axis=0))
    picked = jnp.concatenate(picked, axis=1)

    def take(row):
        return picked[row : row + 1, :]

    jac = [[cam[0, 3 * i + j] for j in range(3)] for i in range(2)]
    centre = [take(j) for j in range(3)]
    scale = [jnp.exp(take(3 + k)) for k in range(3)]
    quat = [take(6 + k) for k in range(4)]
    norm = 1.0 / jnp.sqrt(quat[0] * quat[0] + quat[1] * quat[1] + quat[2] * quat[2] + quat[3] * quat[3])
    qw, qx, qy, qz = [q * norm for q in quat]
    rot = [
        [1 - 2 * (qy * qy + qz * qz), 2 * (qx * qy - qw * qz), 2 * (qx * qz + qw * qy)],
        [2 * (qx * qy + qw * qz), 1 - 2 * (qx * qx + qz * qz), 2 * (qy * qz - qw * qx)],
        [2 * (qx * qz - qw * qy), 2 * (qy * qz + qw * qx), 1 - 2 * (qx * qx + qy * qy)],
    ]
    mixed = [
        [(jac[i][0] * rot[0][k] + jac[i][1] * rot[1][k] + jac[i][2] * rot[2][k]) * scale[k] for k in range(3)]
        for i in range(2)
    ]

    def inner(a, b):
        return a[0] * b[0] + a[1] * b[1] + a[2] * b[2]

    first = inner(mixed[0], mixed[0]) + 0.01
    second = inner(mixed[1], mixed[1]) + 0.01
    cross = inner(mixed[0], mixed[1])
    det = first * second - cross * cross
    con0, con1, con2 = second / det, -cross / det, first / det
    cu = inner(jac[0], centre) + cam[0, 6]
    cw = inner(jac[1], centre) + cam[0, 7]
    opacity = 1.0 / (1.0 + jnp.exp(-take(10)))
    shown = opacity * live

    rows = [cu, cw, con0, 2.0 * con1, con2, shown, take(11), take(12), take(13)]
    rows = jnp.concatenate(rows + [jnp.zeros((7, PAIRS), F32)], axis=0)
    sheet[...] = rows.T

    tile = lax.broadcasted_iota(I32, (TILES, PIXELS), 0)
    pixel = lax.broadcasted_iota(I32, (TILES, PIXELS), 1)
    pos_u = (((tile & 3) * 16 + (pixel & 15)).astype(F32) + 0.5) / 32.0 - 1.0
    pos_w = (((tile >> 2) * 16 + (pixel >> 4)).astype(F32) + 0.5) / 32.0 - 1.0

    def at_slot(s):
        return pl.ds(pl.multiple_of(TILES * s, TILES), TILES)

    def column(s, f):
        return jnp.broadcast_to(sheet[at_slot(s), f : f + 1], (TILES, PIXELS))

    def forward(step, state):
        image, passed = list(state[0:3]), state[3]
        for s in [UNROLL * step + n for n in range(UNROLL)]:
            du = pos_u - column(s, 0)
            dw = pos_w - column(s, 1)
            quad = (column(s, 2) * du + column(s, 3) * dw) * du + column(s, 4) * dw * dw
            bell = jnp.exp(-0.5 * quad)
            alpha = jnp.minimum(column(s, 5) * bell, 0.99)
            weight = alpha * passed
            for c in range(3):
                image[c] = image[c] + column(s, 6 + c) * weight
            e_all[at_slot(s), :] = bell
            t_all[at_slot(s), :] = passed
            passed = passed - weight
        return (*image, passed)

    zero = jnp.zeros((TILES, PIXELS), F32)
    image = lax.fori_loop(0, DEPTH // UNROLL, forward, (zero, zero, zero, zero + 1.0))
    diff = [image[c] - goal[16 * c : 16 * c + 16, :] for c in range(3)]

    def backward(step, behind):
        for s in [DEPTH - 1 - UNROLL * step - n for n in range(UNROLL)]:
            bell = e_all[at_slot(s), :]
            before = t_all[at_slot(s), :]
            raw = column(s, 5) * bell
            alpha = jnp.minimum(raw, 0.99)
            glow = diff[0] * column(s, 6) + diff[1] * column(s, 7) + diff[2] * column(s, 8)
            slope = before * (glow - behind)
            slope = jnp.where(raw < 0.99, slope, jnp.where(raw == 0.99, 0.5 * slope, 0.0))
            behind = behind + alpha * (glow - behind)
            weight = alpha * before
            sums = [-0.5 * raw * slope, bell * slope] + [diff[c] * weight for c in range(3)]
            for n, value in enumerate(sums):
                high, low = split(value)
                parts[2 * n, at_slot(s), :] = high
                parts[2 * n + 1, at_slot(s), :] = low
        return behind

    lax.fori_loop(0, DEPTH // UNROLL, backward, zero)

    which = lax.broadcasted_iota(I32, (16, PIXELS), 0)
    place = lax.broadcasted_iota(I32, (16, PIXELS), 1)
    in_u = ((place & 15).astype(F32) - 7.5) / 32.0
    in_w = ((place >> 4).astype(F32) - 7.5) / 32.0
    basis = jnp.where(which == 0, 1.0, 0.0)
    basis = jnp.where(which == 1, in_u, basis)
    basis = jnp.where(which == 2, in_w, basis)
    basis = jnp.where(which == 3, in_u * in_u, basis)
    basis = jnp.where(which == 4, in_u * in_w, basis)
    basis = jnp.where(which == 5, in_w * in_w, basis)
    basis = basis.astype(BF16)

    def over_pixels(n):
        return lax.dot_general(basis, parts[2 * n], NT, preferred_element_type=F32) + lax.dot_general(
            basis, parts[2 * n + 1], NT, preferred_element_type=F32
        )

    moments = over_pixels(0)
    m1, mu, mw, muu, muw, mww = [moments[n : n + 1, :] for n in range(6)]
    g_opacity = over_pixels(1)[0:1, :] * live
    g_colour = [over_pixels(2 + c)[0:1, :] for c in range(3)]
    at = lax.broadcasted_iota(I32, (1, PAIRS), 1) & 15
    off_u = cu - (((at & 3) * 16 + 8).astype(F32) / 32.0 - 1.0)
    off_w = cw - (((at >> 2) * 16 + 8).astype(F32) / 32.0 - 1.0)
    s_u = mu - off_u * m1
    s_w = mw - off_w * m1
    g_con0 = muu - off_u * (mu + s_u)
    g_con1 = 2.0 * (muw - off_u * mw - off_w * s_u)
    g_con2 = mww - off_w * (mw + s_w)
    g_cu = -2.0 * (con0 * s_u + con1 * s_w)
    g_cw = -2.0 * (con1 * s_u + con2 * s_w)

    g_first = -(con0 * con0 * g_con0 + con0 * con1 * g_con1 + con1 * con1 * g_con2)
    g_second = -(con1 * con1 * g_con0 + con1 * con2 * g_con1 + con2 * con2 * g_con2)
    g_cross = -(2.0 * con0 * con1 * g_con0 + (con0 * con2 + con1 * con1) * g_con1 + 2.0 * con1 * con2 * g_con2)
    g_mixed = [
        [2.0 * g_first * mixed[0][k] + g_cross * mixed[1][k] for k in range(3)],
        [2.0 * g_second * mixed[1][k] + g_cross * mixed[0][k] for k in range(3)],
    ]
    g_scale = [g_mixed[0][k] * mixed[0][k] + g_mixed[1][k] * mixed[1][k] for k in range(3)]
    r = [
        [(jac[0][j] * g_mixed[0][k] + jac[1][j] * g_mixed[1][k]) * scale[k] for k in range(3)] for j in range(3)
    ]
    h_w = 2 * (qz * (r[1][0] - r[0][1]) + qy * (r[0][2] - r[2][0]) + qx * (r[2][1] - r[1][2]))
    h_x = 2 * (
        qy * (r[0][1] + r[1][0]) + qz * (r[0][2] + r[2][0]) + qw * (r[2][1] - r[1][2]) - 2 * qx * (r[1][1] + r[2][2])
    )
    h_y = 2 * (
        qx * (r[0][1] + r[1][0]) + qz * (r[1][2] + r[2][1]) + qw * (r[0][2] - r[2][0]) - 2 * qy * (r[0][0] + r[2][2])
    )
    h_z = 2 * (
        qx * (r[0][2] + r[2][0]) + qy * (r[1][2] + r[2][1]) + qw * (r[1][0] - r[0][1]) - 2 * qz * (r[0][0] + r[1][1])
    )
    along = qw * h_w + qx * h_x + qy * h_y + qz * h_z
    g_quat = [(h - q * along) * norm for h, q in ((h_w, qw), (h_x, qx), (h_y, qy), (h_z, qz))]
    g_centre = [jac[0][j] * g_cu + jac[1][j] * g_cw for j in range(3)]
    g_logit = g_opacity * opacity * (1.0 - opacity)
    along_row = lax.broadcasted_iota(I32, (1, PAIRS), 1)
    colbasis = jnp.zeros((1, PAIRS), F32)
    for k in range(16):
        colbasis = jnp.where(along_row == k, cam[0, 8 + k], colbasis)
    sent = g_centre + g_scale + g_quat + [g_logit] + g_colour + [index.astype(F32), colbasis]
    return jnp.concatenate(sent, axis=0)


def to_blocks(outgoing, incoming, send_sem, recv_sem, block, wave):
    def one(k, _):
        other = (block + k) % NBLK
        pltpu.make_async_remote_copy(
            src_ref=outgoing.at[wave, other],
            dst_ref=incoming.at[wave, block],
            send_sem=send_sem.at[wave],
            recv_sem=recv_sem.at[wave],
            device_id={"blocks": other},
            device_id_type=MESH,
        ).start()
        return 0

    lax.fori_loop(1, NBLK, one, 0)
    incoming[wave, block] = outgoing[wave, block]


def wait_blocks(outgoing, incoming, send_sem, recv_sem, block, wave):
    whole = pltpu.make_async_remote_copy(
        src_ref=outgoing.at[wave, pl.ds(0, NBLK - 1)],
        dst_ref=incoming.at[wave, pl.ds(0, NBLK - 1)],
        send_sem=send_sem.at[wave],
        recv_sem=recv_sem.at[wave],
        device_id={"blocks": block},
        device_id_type=MESH,
    )
    whole.wait_send()
    whole.wait_recv()


def to_views(piece, send_sem, recv_sem, view):
    copies = []
    for k in range(1, NVIEW):
        copy = pltpu.make_async_remote_copy(
            src_ref=piece,
            dst_ref=piece,
            send_sem=send_sem.at[k - 1],
            recv_sem=recv_sem.at[k - 1],
            device_id={"views": (view + k) % NVIEW},
            device_id_type=MESH,
        )
        copy.start()
        copies.append(copy)
    return copies


def refold(value):
    left = lax.broadcasted_iota(I32, (8, 128), 1) < CAP
    upper = lax.broadcasted_iota(I32, (8, 128), 0) < 4
    return jnp.where(left == upper, value, pltpu.roll(pltpu.roll(value, CAP, 1), 4, 0))


def pack(queue, chunks, wave):
    for j in range(NBLK // 2):
        folded = refold(queue[:, 128 * j : 128 * (j + 1)])
        chunks[wave, 2 * j] = folded[0:4]
        chunks[wave, 2 * j + 1] = folded[4:8]


def unpack(chunks, wave, j):
    return refold(jnp.concatenate([chunks[wave, 2 * j], chunks[wave, 2 * j + 1]], axis=0))


def adam(value, first, second, grad):
    first = BETA_ONE * first + (1.0 - BETA_ONE) * grad
    second = BETA_TWO * second + (1.0 - BETA_TWO) * grad * grad
    mhat = first * (1.0 / (1.0 - BETA_ONE**10))
    vhat = second * (1.0 / (1.0 - BETA_TWO**10))
    return value - LEARN * mhat / (jnp.sqrt(vhat) + EPSILON), first, second


def round_kernel(
    cam, params_in, moment1_in, moment2_in, dual_in, z_copy_in, z_table_in, rows_in, owner_in, slot_in,
    lists_in, counts_in, target_in,
    params_out, moment1_out, moment2_out, z_out, dual_out,
    params, moment1, moment2, dual, z_copy, z_table, rows, owner, slot, lists, counts, target,
    table, sheet, goal, e_all, t_all, parts, gathered,
    left, masks, masked, pen_masked, onehot, source, names, place, s_value, s_first, s_second, s_dual, s_table,
    send, got, answers, returned, z_parts, d_parts, items, queue, item_masks, item_masked, item_hot, z_new, dual_new,
    planes_in, in_sem, out_sem, s_mine, r_mine, s_send, r_send, s_back, r_back, s_z, r_z, s_d, r_d,
):
    block = lax.axis_index("blocks")
    view = lax.axis_index("views")

    pairs = [
        (lists_in, lists), (counts_in, counts), (params_in, params), (target_in, target),
        (rows_in, rows), (owner_in, owner), (slot_in, slot), (dual_in, dual), (z_copy_in, z_copy),
        (moment1_in, moment1), (moment2_in, moment2), (z_table_in, z_table),
    ]
    arriving = [pltpu.make_async_copy(there, here, in_sem.at[n]) for n, (there, here) in enumerate(pairs)]
    for copy in arriving[0:4]:
        copy.start()
    barrier = pltpu.get_barrier_semaphore()
    plane, place_in = block // PLANE, block % PLANE
    beside = [plane * PLANE + (place_in + k) % PLANE for k in range(1, PLANE)]
    across = [(block + PLANE * k) % NBLK for k in range(1, NBLK // PLANE)]
    for other in beside + across:
        pl.semaphore_signal(barrier, inc=1, device_id={"blocks": other}, device_id_type=MESH)
    for k in range(1, NVIEW):
        pl.semaphore_signal(barrier, inc=1, device_id={"views": (view + k) % NVIEW}, device_id_type=MESH)
    for copy in arriving[0:4]:
        copy.wait()
    for copy in arriving[4:]:
        copy.start()
    gathered[view] = render(cam, params, lists, counts, target, table, sheet, goal, e_all, t_all, parts)
    pl.semaphore_wait(barrier, len(beside) + len(across) + NVIEW - 1)
    view_copies = to_views(gathered.at[view], s_mine, r_mine, view)
    for other in across:
        pl.semaphore_signal(planes_in, inc=1, device_id={"blocks": other}, device_id_type=MESH)

    for copy in arriving[4:]:
        copy.wait()
    owned = lax.broadcasted_iota(I32, (NBLK, COPIES), 0) == owner[...]
    owned = jnp.where(owned, 1.0, 0.0)
    upper = lax.broadcasted_iota(I32, (128, 128), 0) < lax.broadcasted_iota(I32, (128, 128), 1)
    upper = jnp.where(upper, 1.0, 0.0).astype(BF16)
    ranks = []
    carry = jnp.zeros((NBLK, 1), F32)
    for j in range(COPIES // 128):
        part = owned[:, 128 * j : 128 * (j + 1)]
        ahead = jnp.dot(part.astype(BF16), upper, preferred_element_type=F32) + carry
        ranks.append(jnp.sum(part * ahead, axis=0, keepdims=True))
        carry = carry + jnp.sum(part, axis=1, keepdims=True)
    rank = jnp.concatenate(ranks, axis=1).astype(I32)
    place[...] = owner[...] * CAP + rank
    ident = lax.broadcasted_iota(I32, (1, COPIES), 1)
    ranked = (lax.broadcasted_iota(I32, (128, COPIES), 0) & (CAP - 1)) == rank
    coarse = jnp.where(ranked, (ident >> 5).astype(F32), 0.0).astype(BF16)
    fine = jnp.where(ranked, ((ident & 31) + 1).astype(F32), 0.0).astype(BF16)
    owned = owned.astype(BF16)
    names[...] = (
        32.0 * lax.dot_general(owned, coarse, NT, preferred_element_type=F32)
        + lax.dot_general(owned, fine, NT, preferred_element_type=F32)
    ).astype(I32)

    boundary = rows[...]
    lanes = slice(NVIEW * PAIRS, JOINT)
    left[NPAR:64, :] = jnp.zeros((64 - NPAR, JOINT), F32)
    left[0:NPAR, lanes] = dual[...] - z_copy[...]
    left[NPAR : NPAR + 1, lanes] = jnp.ones((1, COPIES), F32)

    def prepare(index, lanes):
        width = index.shape[1]
        group = jnp.broadcast_to(index >> 8, (16, width))
        for h in range(8):
            masks[16 * h : 16 * h + 16, lanes] = jnp.where(group == h, 1.0, 0.0).astype(BF16)
        hot = lax.broadcasted_iota(I32, (256, width), 0) == (index & 255)
        onehot[:, lanes] = jnp.where(hot, 1.0, 0.0).astype(BF16)

    prepare(boundary, lanes)

    s_value[...] = share_of(params, view)
    s_first[...] = share_of(moment1, view)
    s_second[...] = share_of(moment2, view)
    s_dual[...] = share_of(dual, view)
    s_table[...] = share_of(z_table, view)

    def share_masked(target, value, at):
        high, low = split(value)
        for h in range(8):
            mask = masks[16 * h : 16 * h + 16, at]
            target[32 * h : 32 * h + 16, :] = high * mask
            target[32 * h + 16 : 32 * h + 32, :] = low * mask

    spot = lax.broadcasted_iota(I32, (16, COPIES), 0)
    share_masked(pen_masked, jnp.where(spot == 7, 1.0, share_of(left.at[:, lanes], view)), lanes)
    pen_total = lax.dot_general(pen_masked[...], onehot[:, lanes], NT, preferred_element_type=F32)

    for copy in view_copies:
        copy.wait()
    pl.semaphore_wait(planes_in, len(across))
    diagonal = lax.broadcasted_iota(I32, (16, 128), 0) == lax.broadcasted_iota(I32, (16, 128), 1)
    for v in range(NVIEW):
        lanes = slice(PAIRS * v, PAIRS * (v + 1))
        left[0:11, lanes] = gathered[v, 0:11, :]
        colbasis = jnp.sum(jnp.where(diagonal, gathered[v, 15:16, 0:128], 0.0), axis=1, keepdims=True)
        for c in range(3):
            left[11 + 16 * c : 27 + 16 * c, lanes] = colbasis * gathered[v, 11 + c : 12 + c, :]
        prepare(gathered[v, 14:15, :].astype(I32), lanes)

    lanes = slice(0, NVIEW * PAIRS)
    view_masked = masked.at[0:256, lanes]
    share_masked(view_masked, share_of(left.at[:, lanes], view), lanes)
    total = pen_total + lax.dot_general(view_masked[...], onehot[:, lanes], NT, preferred_element_type=F32)
    moved = []
    for h in range(8):
        both = total[32 * h : 32 * h + 16, :] + total[32 * h + 16 : 32 * h + 32, :]
        lanes = slice(256 * h, 256 * (h + 1))
        value = s_value[:, lanes]
        grad = both + both[7:8, :] * value
        moved.append(adam(value, s_first[:, lanes], s_second[:, lanes], grad)[0])
    moved = jnp.concatenate(moved, axis=1)
    lane = lax.broadcasted_iota(I32, (8, 128), 1)
    spot = lax.broadcasted_iota(I32, (8, COPIES), 0)
    for wave in range(2):
        at = slice(8 * wave, 8 * wave + 8)
        sums = fetch(moved, 8 * wave, boundary) + s_dual[at, :]
        if wave == 0:
            sums = jnp.where(spot == 7, (slot[...] + 1).astype(F32), sums)
        source[at, :] = sums
        blocks_of = groups_of(source, 8 * wave)
        for j in range(NBLK // 2):
            name = jnp.where(lane < CAP, wide(names[2 * j : 2 * j + 1, :]), wide(names[2 * j + 1 : 2 * j + 2, :]))
            found = lane_gather(blocks_of, jnp.maximum(name - 1, 0))
            queue[:, 128 * j : 128 * (j + 1)] = jnp.where(name > 0, found, 0.0)
        pack(queue, send, wave)
        to_blocks(send, got, s_send, r_send, block, wave)

    high, low = split(left[...])
    for h in range(8):
        mask = masks[16 * h : 16 * h + 16, :]
        for n in range(4):
            masked[128 * h + 16 * n : 128 * h + 16 * n + 16, :] = high[16 * n : 16 * n + 16, :] * mask
            masked[128 * h + 64 + 16 * n : 128 * h + 80 + 16 * n, :] = low[16 * n : 16 * n + 16, :] * mask
    total = lax.dot_general(masked[...], onehot[...], NT, preferred_element_type=F32)
    for h in range(8):
        both = total[128 * h : 128 * h + 64, :] + total[128 * h + 64 : 128 * h + 128, :]
        lanes = slice(256 * h, 256 * (h + 1))
        value = params[:, lanes]
        grad = both[0:NPAR] + both[NPAR : NPAR + 1] * value
        params[:, lanes], moment1[:, lanes], moment2[:, lanes] = adam(
            value, moment1[:, lanes], moment2[:, lanes], grad
        )
    leaving = [
        pltpu.make_async_copy(here, there, out_sem.at[n])
        for n, (here, there) in enumerate(
            [(params, params_out), (moment1, moment1_out), (moment2, moment2_out), (z_new, z_out), (dual_new, dual_out)]
        )
    ]
    for copy in leaving[0:3]:
        copy.start()
    last = lax.broadcasted_iota(I32, (8, NBLK * CAP), 0) == 7
    for wave in range(2):
        at = slice(8 * wave, 8 * wave + 8)
        wait_blocks(send, got, s_send, r_send, block, wave)
        for j in range(NBLK // 2):
            items[at, 128 * j : 128 * (j + 1)] = unpack(got, wave, j)
        value = items[at, :]
        if wave == 0:
            label = items[7:8, :].astype(I32)
            index = jnp.maximum(label - 1, 0)
            group = jnp.broadcast_to(jnp.where(label > 0, index >> 8, 4), (16, NBLK * CAP))
            for h in range(4):
                item_masks[16 * h : 16 * h + 16, :] = jnp.where(group == h, 1.0, 0.0).astype(BF16)
            hot = lax.broadcasted_iota(I32, (256, NBLK * CAP), 0) == (index & 255)
            item_hot[...] = jnp.where(hot, 1.0, 0.0).astype(BF16)
            value = jnp.where(last, 1.0, value)
        high = value.astype(BF16).astype(F32)
        both = jnp.concatenate([high, value - high], axis=0).astype(BF16)
        for h in range(4):
            item_masked[16 * h : 16 * h + 16, :] = both * item_masks[16 * h : 16 * h + 16, :]
        total = lax.dot_general(item_masked[...], item_hot[...], NT, preferred_element_type=F32)
        total = jnp.concatenate([total[16 * h : 16 * h + 8, :] + total[16 * h + 8 : 16 * h + 16, :] for h in range(4)], axis=1)
        if wave == 0:
            number = 1.0 + total[7:8, :]
        fresh = (s_table[at, :] + total) / number
        z_parts[view, at, :] = fresh
        answer = groups_of(fresh, 0)
        for j in range(NBLK // 2):
            queue[:, 128 * j : 128 * (j + 1)] = lane_gather(answer, wide(index[:, 128 * j : 128 * (j + 1)]))
        pack(queue, answers, wave)
        to_blocks(answers, returned, s_back, r_back, block, wave)
    z_copies = to_views(z_parts.at[view], s_z, r_z, view)

    d_copies = []
    for wave in range(2):
        at = slice(8 * wave, 8 * wave + 8)
        wait_blocks(answers, returned, s_back, r_back, block, wave)
        for j in range(NBLK // 2):
            items[at, 128 * j : 128 * (j + 1)] = unpack(returned, wave, j)
        d_parts[wave, view] = source[at, :] - fetch(items, 8 * wave, place)
        d_copies.append(to_views(d_parts.at[wave, view], s_d.at[wave], r_d.at[wave], view))
        if wave == 0:
            for copy in z_copies:
                copy.wait()
            for v in range(NVIEW):
                for part in range(2):
                    assemble(z_new, z_parts.at[v, 8 * part : 8 * part + 8], v, part)
            leaving[3].start()
    for wave in range(2):
        for copy in d_copies[wave]:
            copy.wait()
        for v in range(NVIEW):
            assemble(dual_new, d_parts.at[wave, v], v, wave)
    leaving[4].start()
    for copy in leaving:
        copy.wait()


def finish_kernel(*refs):
    sources, targets, staged, in_sem, out_sem = refs[0:5], refs[5:10], refs[10:15], refs[15], refs[16]
    steps = []
    for n, ref in enumerate(sources):
        for piece in range(ref.shape[1] // ROWS):
            lanes = pl.ds(ROWS * piece, ROWS)
            at = len(steps)
            steps.append(
                (
                    pltpu.make_async_copy(ref.at[:, lanes], staged[n].at[:, lanes], in_sem.at[at]),
                    pltpu.make_async_copy(staged[n].at[:, lanes], targets[n].at[:, lanes], out_sem.at[at]),
                )
            )
    for arrive, _ in steps:
        arrive.start()
    for arrive, leave in steps:
        arrive.wait()
        leave.start()
    for _, leave in steps:
        leave.wait()


def anywhere():
    return pl.BlockSpec(memory_space=pl.ANY)


def local(
    params, moment1, moment2, dual, z_copy, z_table, boundary_rows, owner_block, owner_slot,
    tile_lists, tile_counts, cameras, target,
):
    shape = jax.ShapeDtypeStruct
    outs = (shape((NPAR, GAUSS), F32),) * 3 + (shape((NPAR, ROWS), F32), shape((NPAR, COPIES), F32))

    def f32(*dims):
        return pltpu.VMEM(dims, F32)

    def bf16(*dims):
        return pltpu.VMEM(dims, BF16)

    def i32(*dims):
        return pltpu.VMEM(dims, I32)

    chunks = f32(2, NBLK, 4, 128)
    dma = pltpu.SemaphoreType.DMA
    results = pl.pallas_call(
        round_kernel,
        out_shape=outs,
        in_specs=[pl.BlockSpec(memory_space=pltpu.SMEM)] + [anywhere()] * 12,
        out_specs=(anywhere(),) * 5,
        scratch_shapes=[
            f32(NPAR, GAUSS), f32(NPAR, GAUSS), f32(NPAR, GAUSS),
            f32(NPAR, COPIES), f32(NPAR, COPIES), f32(NPAR, ROWS),
            i32(1, COPIES), i32(1, COPIES), i32(1, COPIES), i32(TILES, DEPTH), i32(1, TILES), f32(3, TILES * PIXELS),
            f32(16, GAUSS), f32(PAIRS, 16), f32(48, PIXELS), f32(PAIRS, PIXELS), f32(PAIRS, PIXELS),
            bf16(10, PAIRS, PIXELS), f32(NVIEW, 16, PAIRS),
            f32(64, JOINT), bf16(128, JOINT), bf16(1024, JOINT), bf16(256, COPIES), bf16(256, JOINT),
            f32(16, COPIES), i32(NBLK, 128), i32(1, COPIES),
            f32(16, GAUSS), f32(16, GAUSS), f32(16, GAUSS), f32(16, COPIES), f32(16, ROWS),
            chunks, chunks, chunks, chunks, f32(NVIEW, 16, ROWS), f32(2, NVIEW, 8, COPIES),
            f32(16, NBLK * CAP), f32(8, NBLK * CAP), bf16(64, NBLK * CAP), bf16(64, NBLK * CAP), bf16(256, NBLK * CAP), f32(NPAR, ROWS), f32(NPAR, COPIES),
            pltpu.SemaphoreType.REGULAR, dma((12,)), dma((5,)), dma((3,)), dma((3,)), dma((2,)), dma((2,)), dma((2,)), dma((2,)),
            dma((3,)), dma((3,)), dma((2, 3)), dma((2, 3)),
        ],
        compiler_params=pltpu.CompilerParams(
            collective_id=0, has_side_effects=True, vmem_limit_bytes=56 * 1024 * 1024
        ),
        name="round",
    )(
        cameras, params, moment1, moment2, dual, z_copy, z_table,
        boundary_rows.reshape(1, COPIES), owner_block.reshape(1, COPIES), owner_slot.reshape(1, COPIES),
        tile_lists, tile_counts.reshape(1, TILES), target,
    )
    return pl.pallas_call(
        finish_kernel,
        out_shape=outs,
        in_specs=[anywhere()] * 5,
        out_specs=(anywhere(),) * 5,
        scratch_shapes=[f32(*out.shape) for out in outs] + [dma((8,)), dma((8,))],
        compiler_params=pltpu.CompilerParams(vmem_limit_bytes=56 * 1024 * 1024),
        name="finish",
    )(*results)


def solution(mesh):
    whole, both = P(None, "blocks"), ("blocks", "views")
    placed = (whole,) * 6 + (P("blocks"), P("blocks", None), P("blocks"))
    placed += (P(both, None), P(both), P(both, None), P(None, both))
    return jax.shard_map(local, mesh=mesh, in_specs=placed, out_specs=(whole,) * 5, check_vma=False)
```

```python
import functools

import jax
import jax.numpy as jnp
from jax import lax
from jax.experimental import pallas as pl
from jax.experimental.pallas import tpu as pltpu
from jax.sharding import PartitionSpec as P

LEARN = 0.05
BETA_ONE = 0.9
BETA_TWO = 0.999
EPSILON = 1e-08

NPAR = 59
GAUSS = 2048
COPIES = 1024
ROWS = 1024
TILES = 16
DEPTH = 32
PAIRS = TILES * DEPTH
PIXELS = 256
NBLK = 64
PLANE = 8
NVIEW = 4
CAP = 64
SHARE = 15
JOINT = NVIEW * PAIRS + COPIES
UNROLL = 32

F32 = jnp.float32
BF16 = jnp.bfloat16
I32 = jnp.int32
MESH = pl.DeviceIdType.MESH
NT = (((1,), (1,)), ((), ()))


def lane_gather(source, index):
    low = index & 127
    high = index >> 7
    found = jnp.take_along_axis(source[0], low, axis=1)
    for g in range(1, len(source)):
        found = jnp.where(high == g, jnp.take_along_axis(source[g], low, axis=1), found)
    return found


def groups_of(value, rows):
    return [value[rows : rows + 8, 128 * g : 128 * (g + 1)] for g in range(value.shape[1] // 128)]


def fetch(value, rows, index):
    source = groups_of(value, rows)
    found = [lane_gather(source, wide(index[:, 128 * j : 128 * (j + 1)])) for j in range(index.shape[1] // 128)]
    return jnp.concatenate(found, axis=1)


def wide(row):
    return jnp.broadcast_to(row, (8, row.shape[1]))


def split(value):
    high = value.astype(BF16)
    return high, (value - high.astype(F32)).astype(BF16)


def share_of(ref, view):
    parts = []
    for v in range(NVIEW):
        end = min(SHARE * v + SHARE, NPAR)
        rows = [ref[SHARE * v : SHARE * v + 7, :], jnp.zeros((1, ref.shape[1]), F32), ref[SHARE * v + 7 : end, :]]
        if end < SHARE * v + SHARE:
            rows.append(jnp.zeros((SHARE * v + SHARE - end, ref.shape[1]), F32))
        parts.append(jnp.concatenate(rows, axis=0))
    result = parts[3]
    for v in range(3):
        result = jnp.where(view == v, parts[v], result)
    return result


def assemble(target, part, v, wave):
    start = SHARE * v + 7 * wave
    count = min(7 + wave, NPAR - start)
    target[start : start + count, :] = part[0:count, :]


def render(cam, params, lists, counts, target, table, sheet, goal, e_all, t_all, parts):
    table[0:11, :] = params[0:11, :]
    table[14:16, :] = jnp.zeros((2, GAUSS), F32)
    for c in range(3):
        colour = cam[0, 8] * params[11 + 16 * c : 12 + 16 * c, :]
        for k in range(1, 16):
            row = 11 + 16 * c + k
            colour += cam[0, 8 + k] * params[row : row + 1, :]
        table[11 + c : 12 + c, :] = colour + 0.5
    for c in range(3):
        for t in range(TILES):
            goal[16 * c + t : 16 * c + t + 1, :] = target[c : c + 1, PIXELS * t : PIXELS * (t + 1)]

    turned = lists[...].astype(F32).T
    slots = lax.broadcasted_iota(I32, (DEPTH, TILES), 0)
    turned = jnp.where(slots < counts[...], turned, turned + GAUSS)
    turned = jnp.concatenate([turned, jnp.zeros((DEPTH, 128 - TILES), F32)], axis=1)
    turns = [turned] + [pltpu.roll(turned, TILES * m, 1) for m in range(1, 8)]
    lane = lax.broadcasted_iota(I32, (1, 128), 1)
    pieces = []
    for j in range(PAIRS // 128):
        row = turns[0][8 * j : 8 * j + 1, :]
        for m in range(1, 8):
            row = jnp.where(lane >> 4 == m, turns[m][8 * j + m : 8 * j + m + 1, :], row)
        pieces.append(row)
    coded = jnp.concatenate(pieces, axis=1).astype(I32)
    live = jnp.where(coded < GAUSS, 1.0, 0.0)
    index = coded & (GAUSS - 1)
    picked = []
    for j in range(PAIRS // 128):
        lanes = wide(index[:, 128 * j : 128 * (j + 1)])
        picked.append(jnp.concatenate([lane_gather(groups_of(table, 8 * n), lanes) for n in range(2)], axis=0))
    picked = jnp.concatenate(picked, axis=1)

    def take(row):
        return picked[row : row + 1, :]

    jac = [[cam[0, 3 * i + j] for j in range(3)] for i in range(2)]
    centre = [take(j) for j in range(3)]
    scale = [jnp.exp(take(3 + k)) for k in range(3)]
    quat = [take(6 + k) for k in range(4)]
    norm = 1.0 / jnp.sqrt(quat[0] * quat[0] + quat[1] * quat[1] + quat[2] * quat[2] + quat[3] * quat[3])
    qw, qx, qy, qz = [q * norm for q in quat]
    rot = [
        [1 - 2 * (qy * qy + qz * qz), 2 * (qx * qy - qw * qz), 2 * (qx * qz + qw * qy)],
        [2 * (qx * qy + qw * qz), 1 - 2 * (qx * qx + qz * qz), 2 * (qy * qz - qw * qx)],
        [2 * (qx * qz - qw * qy), 2 * (qy * qz + qw * qx), 1 - 2 * (qx * qx + qy * qy)],
    ]
    mixed = [
        [(jac[i][0] * rot[0][k] + jac[i][1] * rot[1][k] + jac[i][2] * rot[2][k]) * scale[k] for k in range(3)]
        for i in range(2)
    ]

    def inner(a, b):
        return a[0] * b[0] + a[1] * b[1] + a[2] * b[2]

    first = inner(mixed[0], mixed[0]) + 0.01
    second = inner(mixed[1], mixed[1]) + 0.01
    cross = inner(mixed[0], mixed[1])
    det = first * second - cross * cross
    con0, con1, con2 = second / det, -cross / det, first / det
    cu = inner(jac[0], centre) + cam[0, 6]
    cw = inner(jac[1], centre) + cam[0, 7]
    opacity = 1.0 / (1.0 + jnp.exp(-take(10)))
    shown = opacity * live

    rows = [cu, cw, con0, 2.0 * con1, con2, shown, take(11), take(12), take(13)]
    rows = jnp.concatenate(rows + [jnp.zeros((7, PAIRS), F32)], axis=0)
    sheet[...] = rows.T

    tile = lax.broadcasted_iota(I32, (TILES, PIXELS), 0)
    pixel = lax.broadcasted_iota(I32, (TILES, PIXELS), 1)
    pos_u = (((tile & 3) * 16 + (pixel & 15)).astype(F32) + 0.5) / 32.0 - 1.0
    pos_w = (((tile >> 2) * 16 + (pixel >> 4)).astype(F32) + 0.5) / 32.0 - 1.0

    def at_slot(s):
        return pl.ds(pl.multiple_of(TILES * s, TILES), TILES)

    def column(s, f):
        return jnp.broadcast_to(sheet[at_slot(s), f : f + 1], (TILES, PIXELS))

    def forward(step, state):
        image, passed = list(state[0:3]), state[3]
        for s in [UNROLL * step + n for n in range(UNROLL)]:
            du = pos_u - column(s, 0)
            dw = pos_w - column(s, 1)
            quad = (column(s, 2) * du + column(s, 3) * dw) * du + column(s, 4) * dw * dw
            bell = jnp.exp(-0.5 * quad)
            alpha = jnp.minimum(column(s, 5) * bell, 0.99)
            weight = alpha * passed
            for c in range(3):
                image[c] = image[c] + column(s, 6 + c) * weight
            e_all[at_slot(s), :] = bell
            t_all[at_slot(s), :] = passed
            passed = passed - weight
        return (*image, passed)

    zero = jnp.zeros((TILES, PIXELS), F32)
    image = lax.fori_loop(0, DEPTH // UNROLL, forward, (zero, zero, zero, zero + 1.0))
    diff = [image[c] - goal[16 * c : 16 * c + 16, :] for c in range(3)]

    def backward(step, behind):
        for s in [DEPTH - 1 - UNROLL * step - n for n in range(UNROLL)]:
            bell = e_all[at_slot(s), :]
            before = t_all[at_slot(s), :]
            raw = column(s, 5) * bell
            alpha = jnp.minimum(raw, 0.99)
            glow = diff[0] * column(s, 6) + diff[1] * column(s, 7) + diff[2] * column(s, 8)
            slope = before * (glow - behind)
            slope = jnp.where(raw < 0.99, slope, jnp.where(raw == 0.99, 0.5 * slope, 0.0))
            behind = behind + alpha * (glow - behind)
            weight = alpha * before
            sums = [-0.5 * raw * slope, bell * slope] + [diff[c] * weight for c in range(3)]
            for n, value in enumerate(sums):
                high, low = split(value)
                parts[2 * n, at_slot(s), :] = high
                parts[2 * n + 1, at_slot(s), :] = low
        return behind

    lax.fori_loop(0, DEPTH // UNROLL, backward, zero)

    which = lax.broadcasted_iota(I32, (16, PIXELS), 0)
    place = lax.broadcasted_iota(I32, (16, PIXELS), 1)
    in_u = ((place & 15).astype(F32) - 7.5) / 32.0
    in_w = ((place >> 4).astype(F32) - 7.5) / 32.0
    basis = jnp.where(which == 0, 1.0, 0.0)
    basis = jnp.where(which == 1, in_u, basis)
    basis = jnp.where(which == 2, in_w, basis)
    basis = jnp.where(which == 3, in_u * in_u, basis)
    basis = jnp.where(which == 4, in_u * in_w, basis)
    basis = jnp.where(which == 5, in_w * in_w, basis)
    basis = basis.astype(BF16)

    def over_pixels(n):
        return lax.dot_general(basis, parts[2 * n], NT, preferred_element_type=F32) + lax.dot_general(
            basis, parts[2 * n + 1], NT, preferred_element_type=F32
        )

    moments = over_pixels(0)
    m1, mu, mw, muu, muw, mww = [moments[n : n + 1, :] for n in range(6)]
    g_opacity = over_pixels(1)[0:1, :] * live
    g_colour = [over_pixels(2 + c)[0:1, :] for c in range(3)]
    at = lax.broadcasted_iota(I32, (1, PAIRS), 1) & 15
    off_u = cu - (((at & 3) * 16 + 8).astype(F32) / 32.0 - 1.0)
    off_w = cw - (((at >> 2) * 16 + 8).astype(F32) / 32.0 - 1.0)
    s_u = mu - off_u * m1
    s_w = mw - off_w * m1
    g_con0 = muu - off_u * (mu + s_u)
    g_con1 = 2.0 * (muw - off_u * mw - off_w * s_u)
    g_con2 = mww - off_w * (mw + s_w)
    g_cu = -2.0 * (con0 * s_u + con1 * s_w)
    g_cw = -2.0 * (con1 * s_u + con2 * s_w)

    g_first = -(con0 * con0 * g_con0 + con0 * con1 * g_con1 + con1 * con1 * g_con2)
    g_second = -(con1 * con1 * g_con0 + con1 * con2 * g_con1 + con2 * con2 * g_con2)
    g_cross = -(2.0 * con0 * con1 * g_con0 + (con0 * con2 + con1 * con1) * g_con1 + 2.0 * con1 * con2 * g_con2)
    g_mixed = [
        [2.0 * g_first * mixed[0][k] + g_cross * mixed[1][k] for k in range(3)],
        [2.0 * g_second * mixed[1][k] + g_cross * mixed[0][k] for k in range(3)],
    ]
    g_scale = [g_mixed[0][k] * mixed[0][k] + g_mixed[1][k] * mixed[1][k] for k in range(3)]
    r = [
        [(jac[0][j] * g_mixed[0][k] + jac[1][j] * g_mixed[1][k]) * scale[k] for k in range(3)] for j in range(3)
    ]
    h_w = 2 * (qz * (r[1][0] - r[0][1]) + qy * (r[0][2] - r[2][0]) + qx * (r[2][1] - r[1][2]))
    h_x = 2 * (
        qy * (r[0][1] + r[1][0]) + qz * (r[0][2] + r[2][0]) + qw * (r[2][1] - r[1][2]) - 2 * qx * (r[1][1] + r[2][2])
    )
    h_y = 2 * (
        qx * (r[0][1] + r[1][0]) + qz * (r[1][2] + r[2][1]) + qw * (r[0][2] - r[2][0]) - 2 * qy * (r[0][0] + r[2][2])
    )
    h_z = 2 * (
        qx * (r[0][2] + r[2][0]) + qy * (r[1][2] + r[2][1]) + qw * (r[1][0] - r[0][1]) - 2 * qz * (r[0][0] + r[1][1])
    )
    along = qw * h_w + qx * h_x + qy * h_y + qz * h_z
    g_quat = [(h - q * along) * norm for h, q in ((h_w, qw), (h_x, qx), (h_y, qy), (h_z, qz))]
    g_centre = [jac[0][j] * g_cu + jac[1][j] * g_cw for j in range(3)]
    g_logit = g_opacity * opacity * (1.0 - opacity)
    along_row = lax.broadcasted_iota(I32, (1, PAIRS), 1)
    colbasis = jnp.zeros((1, PAIRS), F32)
    for k in range(16):
        colbasis = jnp.where(along_row == k, cam[0, 8 + k], colbasis)
    sent = g_centre + g_scale + g_quat + [g_logit] + g_colour + [index.astype(F32), colbasis]
    return jnp.concatenate(sent, axis=0)


def to_blocks(outgoing, incoming, send_sem, recv_sem, block, wave):
    def one(k, _):
        other = (block + k) % NBLK
        pltpu.make_async_remote_copy(
            src_ref=outgoing.at[wave, other],
            dst_ref=incoming.at[wave, block],
            send_sem=send_sem.at[wave],
            recv_sem=recv_sem.at[wave],
            device_id={"blocks": other},
            device_id_type=MESH,
        ).start()
        return 0

    lax.fori_loop(1, NBLK, one, 0)
    incoming[wave, block] = outgoing[wave, block]


def wait_blocks(outgoing, incoming, send_sem, recv_sem, block, wave):
    whole = pltpu.make_async_remote_copy(
        src_ref=outgoing.at[wave, pl.ds(0, NBLK - 1)],
        dst_ref=incoming.at[wave, pl.ds(0, NBLK - 1)],
        send_sem=send_sem.at[wave],
        recv_sem=recv_sem.at[wave],
        device_id={"blocks": block},
        device_id_type=MESH,
    )
    whole.wait_send()
    whole.wait_recv()


def to_views(piece, send_sem, recv_sem, view):
    copies = []
    for k in range(1, NVIEW):
        copy = pltpu.make_async_remote_copy(
            src_ref=piece,
            dst_ref=piece,
            send_sem=send_sem.at[k - 1],
            recv_sem=recv_sem.at[k - 1],
            device_id={"views": (view + k) % NVIEW},
            device_id_type=MESH,
        )
        copy.start()
        copies.append(copy)
    return copies


def refold(value):
    left = lax.broadcasted_iota(I32, (8, 128), 1) < CAP
    upper = lax.broadcasted_iota(I32, (8, 128), 0) < 4
    return jnp.where(left == upper, value, pltpu.roll(pltpu.roll(value, CAP, 1), 4, 0))


def pack(queue, chunks, wave):
    for j in range(NBLK // 2):
        folded = refold(queue[:, 128 * j : 128 * (j + 1)])
        chunks[wave, 2 * j] = folded[0:4]
        chunks[wave, 2 * j + 1] = folded[4:8]


def unpack(chunks, wave, j):
    return refold(jnp.concatenate([chunks[wave, 2 * j], chunks[wave, 2 * j + 1]], axis=0))


def adam(value, first, second, grad):
    first = BETA_ONE * first + (1.0 - BETA_ONE) * grad
    second = BETA_TWO * second + (1.0 - BETA_TWO) * grad * grad
    mhat = first * (1.0 / (1.0 - BETA_ONE**10))
    vhat = second * (1.0 / (1.0 - BETA_TWO**10))
    return value - LEARN * mhat / (jnp.sqrt(vhat) + EPSILON), first, second


def round_kernel(
    cam, params_in, moment1_in, moment2_in, dual_in, z_copy_in, z_table_in, rows_in, owner_in, slot_in,
    lists_in, counts_in, target_in,
    params_out, moment1_out, moment2_out, z_out, dual_out,
    params, moment1, moment2, dual, z_copy, z_table, rows, owner, slot, lists, counts, target,
    table, sheet, goal, e_all, t_all, parts, gathered,
    left, masks, masked, pen_masked, onehot, source, names, place, s_value, s_first, s_second, s_dual, s_table,
    send, got, answers, returned, z_parts, d_parts, items, queue, item_masks, item_masked, item_hot, z_new, dual_new,
    planes_in, in_sem, out_sem, s_mine, r_mine, s_send, r_send, s_back, r_back, s_z, r_z, s_d, r_d,
):
    block = lax.axis_index("blocks")
    view = lax.axis_index("views")

    pairs = [
        (lists_in, lists), (counts_in, counts), (params_in, params), (target_in, target),
        (rows_in, rows), (owner_in, owner), (slot_in, slot), (dual_in, dual), (z_copy_in, z_copy),
        (moment1_in, moment1), (moment2_in, moment2), (z_table_in, z_table),
    ]
    arriving = [pltpu.make_async_copy(there, here, in_sem.at[n]) for n, (there, here) in enumerate(pairs)]
    for copy in arriving[0:4]:
        copy.start()
    barrier = pltpu.get_barrier_semaphore()
    plane, place_in = block // PLANE, block % PLANE
    beside = [plane * PLANE + (place_in + k) % PLANE for k in range(1, PLANE)]
    across = [(block + PLANE * k) % NBLK for k in range(1, NBLK // PLANE)]
    for other in beside + across:
        pl.semaphore_signal(barrier, inc=1, device_id={"blocks": other}, device_id_type=MESH)
    for k in range(1, NVIEW):
        pl.semaphore_signal(barrier, inc=1, device_id={"views": (view + k) % NVIEW}, device_id_type=MESH)
    for copy in arriving[0:4]:
        copy.wait()
    for copy in arriving[4:]:
        copy.start()
    gathered[view] = render(cam, params, lists, counts, target, table, sheet, goal, e_all, t_all, parts)
    pl.semaphore_wait(barrier, len(beside) + len(across) + NVIEW - 1)
    view_copies = to_views(gathered.at[view], s_mine, r_mine, view)
    for other in across:
        pl.semaphore_signal(planes_in, inc=1, device_id={"blocks": other}, device_id_type=MESH)

    for copy in arriving[4:]:
        copy.wait()
    owned = lax.broadcasted_iota(I32, (NBLK, COPIES), 0) == owner[...]
    owned = jnp.where(owned, 1.0, 0.0)
    upper = lax.broadcasted_iota(I32, (128, 128), 0) < lax.broadcasted_iota(I32, (128, 128), 1)
    upper = jnp.where(upper, 1.0, 0.0).astype(BF16)
    ranks = []
    carry = jnp.zeros((NBLK, 1), F32)
    for j in range(COPIES // 128):
        part = owned[:, 128 * j : 128 * (j + 1)]
        ahead = jnp.dot(part.astype(BF16), upper, preferred_element_type=F32) + carry
        ranks.append(jnp.sum(part * ahead, axis=0, keepdims=True))
        carry = carry + jnp.sum(part, axis=1, keepdims=True)
    rank = jnp.concatenate(ranks, axis=1).astype(I32)
    place[...] = owner[...] * CAP + rank
    ident = lax.broadcasted_iota(I32, (1, COPIES), 1)
    ranked = (lax.broadcasted_iota(I32, (128, COPIES), 0) & (CAP - 1)) == rank
    coarse = jnp.where(ranked, (ident >> 5).astype(F32), 0.0).astype(BF16)
    fine = jnp.where(ranked, ((ident & 31) + 1).astype(F32), 0.0).astype(BF16)
    owned = owned.astype(BF16)
    names[...] = (
        32.0 * lax.dot_general(owned, coarse, NT, preferred_element_type=F32)
        + lax.dot_general(owned, fine, NT, preferred_element_type=F32)
    ).astype(I32)

    boundary = rows[...]
    lanes = slice(NVIEW * PAIRS, JOINT)
    left[NPAR:64, :] = jnp.zeros((64 - NPAR, JOINT), F32)
    left[0:NPAR, lanes] = dual[...] - z_copy[...]
    left[NPAR : NPAR + 1, lanes] = jnp.ones((1, COPIES), F32)

    def prepare(index, lanes):
        width = index.shape[1]
        group = jnp.broadcast_to(index >> 8, (16, width))
        for h in range(8):
            masks[16 * h : 16 * h + 16, lanes] = jnp.where(group == h, 1.0, 0.0).astype(BF16)
        hot = lax.broadcasted_iota(I32, (256, width), 0) == (index & 255)
        onehot[:, lanes] = jnp.where(hot, 1.0, 0.0).astype(BF16)

    prepare(boundary, lanes)

    s_value[...] = share_of(params, view)
    s_first[...] = share_of(moment1, view)
    s_second[...] = share_of(moment2, view)
    s_dual[...] = share_of(dual, view)
    s_table[...] = share_of(z_table, view)

    def share_masked(target, value, at):
        high, low = split(value)
        for h in range(8):
            mask = masks[16 * h : 16 * h + 16, at]
            target[32 * h : 32 * h + 16, :] = high * mask
            target[32 * h + 16 : 32 * h + 32, :] = low * mask

    spot = lax.broadcasted_iota(I32, (16, COPIES), 0)
    share_masked(pen_masked, jnp.where(spot == 7, 1.0, share_of(left.at[:, lanes], view)), lanes)
    pen_total = lax.dot_general(pen_masked[...], onehot[:, lanes], NT, preferred_element_type=F32)

    for copy in view_copies:
        copy.wait()
    pl.semaphore_wait(planes_in, len(across))
    diagonal = lax.broadcasted_iota(I32, (16, 128), 0) == lax.broadcasted_iota(I32, (16, 128), 1)
    for v in range(NVIEW):
        lanes = slice(PAIRS * v, PAIRS * (v + 1))
        left[0:11, lanes] = gathered[v, 0:11, :]
        colbasis = jnp.sum(jnp.where(diagonal, gathered[v, 15:16, 0:128], 0.0), axis=1, keepdims=True)
        for c in range(3):
            left[11 + 16 * c : 27 + 16 * c, lanes] = colbasis * gathered[v, 11 + c : 12 + c, :]
        prepare(gathered[v, 14:15, :].astype(I32), lanes)

    lanes = slice(0, NVIEW * PAIRS)
    view_masked = masked.at[0:256, lanes]
    share_masked(view_masked, share_of(left.at[:, lanes], view), lanes)
    total = pen_total + lax.dot_general(view_masked[...], onehot[:, lanes], NT, preferred_element_type=F32)
    moved = []
    for h in range(8):
        both = total[32 * h : 32 * h + 16, :] + total[32 * h + 16 : 32 * h + 32, :]
        lanes = slice(256 * h, 256 * (h + 1))
        value = s_value[:, lanes]
        grad = both + both[7:8, :] * value
        moved.append(adam(value, s_first[:, lanes], s_second[:, lanes], grad)[0])
    moved = jnp.concatenate(moved, axis=1)
    lane = lax.broadcasted_iota(I32, (8, 128), 1)
    spot = lax.broadcasted_iota(I32, (8, COPIES), 0)
    for wave in range(2):
        at = slice(8 * wave, 8 * wave + 8)
        sums = fetch(moved, 8 * wave, boundary) + s_dual[at, :]
        if wave == 0:
            sums = jnp.where(spot == 7, (slot[...] + 1).astype(F32), sums)
        source[at, :] = sums
        blocks_of = groups_of(source, 8 * wave)
        for j in range(NBLK // 2):
            name = jnp.where(lane < CAP, wide(names[2 * j : 2 * j + 1, :]), wide(names[2 * j + 1 : 2 * j + 2, :]))
            found = lane_gather(blocks_of, jnp.maximum(name - 1, 0))
            queue[:, 128 * j : 128 * (j + 1)] = jnp.where(name > 0, found, 0.0)
        pack(queue, send, wave)
        to_blocks(send, got, s_send, r_send, block, wave)

    leaving = []

    def step_half(half):
        high, low = split(left[...])
        for n in range(4):
            mask = masks[64 * half + 16 * n : 64 * half + 16 * n + 16, :]
            for part in range(4):
                rows_at = slice(16 * part, 16 * part + 16)
                masked[128 * n + 16 * part : 128 * n + 16 * part + 16, :] = high[rows_at, :] * mask
                masked[128 * n + 64 + 16 * part : 128 * n + 80 + 16 * part, :] = low[rows_at, :] * mask
        total = lax.dot_general(masked[...], onehot[...], NT, preferred_element_type=F32)
        for n in range(4):
            both = total[128 * n : 128 * n + 64, :] + total[128 * n + 64 : 128 * n + 128, :]
            lanes = slice(1024 * half + 256 * n, 1024 * half + 256 * (n + 1))
            value = params[:, lanes]
            grad = both[0:NPAR] + both[NPAR : NPAR + 1] * value
            params[:, lanes], moment1[:, lanes], moment2[:, lanes] = adam(
                value, moment1[:, lanes], moment2[:, lanes], grad
            )
        lanes = pl.ds(1024 * half, 1024)
        for n, (here, there) in enumerate([(params, params_out), (moment1, moment1_out), (moment2, moment2_out)]):
            copy = pltpu.make_async_copy(here.at[:, lanes], there.at[:, lanes], out_sem.at[3 * half + n])
            copy.start()
            leaving.append(copy)

    step_half(0)

    last = lax.broadcasted_iota(I32, (8, NBLK * CAP), 0) == 7
    for wave in range(2):
        at = slice(8 * wave, 8 * wave + 8)
        wait_blocks(send, got, s_send, r_send, block, wave)
        for j in range(NBLK // 2):
            items[at, 128 * j : 128 * (j + 1)] = unpack(got, wave, j)
        value = items[at, :]
        if wave == 0:
            label = items[7:8, :].astype(I32)
            index = jnp.maximum(label - 1, 0)
            group = jnp.broadcast_to(jnp.where(label > 0, index >> 7, 8), (16, NBLK * CAP))
            for h in range(8):
                item_masks[16 * h : 16 * h + 16, :] = jnp.where(group == h, 1.0, 0.0).astype(BF16)
            hot = lax.broadcasted_iota(I32, (128, NBLK * CAP), 0) == (index & 127)
            item_hot[...] = jnp.where(hot, 1.0, 0.0).astype(BF16)
            value = jnp.where(last, 1.0, value)
        high = value.astype(BF16).astype(F32)
        both = jnp.concatenate([high, value - high], axis=0).astype(BF16)
        for h in range(8):
            item_masked[16 * h : 16 * h + 16, :] = both * item_masks[16 * h : 16 * h + 16, :]
        total = lax.dot_general(item_masked[...], item_hot[...], NT, preferred_element_type=F32)
        total = jnp.concatenate([total[16 * h : 16 * h + 8, :] + total[16 * h + 8 : 16 * h + 16, :] for h in range(8)], axis=1)
        if wave == 0:
            number = 1.0 + total[7:8, :]
        fresh = (s_table[at, :] + total) / number
        z_parts[view, at, :] = fresh
        answer = groups_of(fresh, 0)
        for j in range(NBLK // 2):
            queue[:, 128 * j : 128 * (j + 1)] = lane_gather(answer, wide(index[:, 128 * j : 128 * (j + 1)]))
        pack(queue, answers, wave)
        to_blocks(answers, returned, s_back, r_back, block, wave)
    z_copies = to_views(z_parts.at[view], s_z, r_z, view)
    step_half(1)

    d_copies = []
    for wave in range(2):
        at = slice(8 * wave, 8 * wave + 8)
        wait_blocks(answers, returned, s_back, r_back, block, wave)
        for j in range(NBLK // 2):
            items[at, 128 * j : 128 * (j + 1)] = unpack(returned, wave, j)
        d_parts[wave, view] = source[at, :] - fetch(items, 8 * wave, place)
        d_copies.append(to_views(d_parts.at[wave, view], s_d.at[wave], r_d.at[wave], view))
        if wave == 0:
            for copy in z_copies:
                copy.wait()
            for v in range(NVIEW):
                for part in range(2):
                    assemble(z_new, z_parts.at[v, 8 * part : 8 * part + 8], v, part)
            leaving.append(pltpu.make_async_copy(z_new, z_out, out_sem.at[6]))
            leaving[-1].start()
    for wave in range(2):
        for copy in d_copies[wave]:
            copy.wait()
        for v in range(NVIEW):
            assemble(dual_new, d_parts.at[wave, v], v, wave)
    leaving.append(pltpu.make_async_copy(dual_new, dual_out, out_sem.at[7]))
    leaving[-1].start()
    for copy in leaving:
        copy.wait()


def finish_kernel(*refs):
    sources, targets, staged, in_sem, out_sem = refs[0:5], refs[5:10], refs[10:15], refs[15], refs[16]
    steps = []
    for n, ref in enumerate(sources):
        for piece in range(ref.shape[1] // ROWS):
            lanes = pl.ds(ROWS * piece, ROWS)
            at = len(steps)
            steps.append(
                (
                    pltpu.make_async_copy(ref.at[:, lanes], staged[n].at[:, lanes], in_sem.at[at]),
                    pltpu.make_async_copy(staged[n].at[:, lanes], targets[n].at[:, lanes], out_sem.at[at]),
                )
            )
    for arrive, _ in steps:
        arrive.start()
    for arrive, leave in steps:
        arrive.wait()
        leave.start()
    for _, leave in steps:
        leave.wait()


def anywhere():
    return pl.BlockSpec(memory_space=pl.ANY)


def local(
    params, moment1, moment2, dual, z_copy, z_table, boundary_rows, owner_block, owner_slot,
    tile_lists, tile_counts, cameras, target,
):
    shape = jax.ShapeDtypeStruct
    outs = (shape((NPAR, GAUSS), F32),) * 3 + (shape((NPAR, ROWS), F32), shape((NPAR, COPIES), F32))

    def f32(*dims):
        return pltpu.VMEM(dims, F32)

    def bf16(*dims):
        return pltpu.VMEM(dims, BF16)

    def i32(*dims):
        return pltpu.VMEM(dims, I32)

    chunks = f32(2, NBLK, 4, 128)
    dma = pltpu.SemaphoreType.DMA
    results = pl.pallas_call(
        round_kernel,
        out_shape=outs,
        in_specs=[pl.BlockSpec(memory_space=pltpu.SMEM)] + [anywhere()] * 12,
        out_specs=(anywhere(),) * 5,
        scratch_shapes=[
            f32(NPAR, GAUSS), f32(NPAR, GAUSS), f32(NPAR, GAUSS),
            f32(NPAR, COPIES), f32(NPAR, COPIES), f32(NPAR, ROWS),
            i32(1, COPIES), i32(1, COPIES), i32(1, COPIES), i32(TILES, DEPTH), i32(1, TILES), f32(3, TILES * PIXELS),
            f32(16, GAUSS), f32(PAIRS, 16), f32(48, PIXELS), f32(PAIRS, PIXELS), f32(PAIRS, PIXELS),
            bf16(10, PAIRS, PIXELS), f32(NVIEW, 16, PAIRS),
            f32(64, JOINT), bf16(128, JOINT), bf16(512, JOINT), bf16(256, COPIES), bf16(256, JOINT),
            f32(16, COPIES), i32(NBLK, 128), i32(1, COPIES),
            f32(16, GAUSS), f32(16, GAUSS), f32(16, GAUSS), f32(16, COPIES), f32(16, ROWS),
            chunks, chunks, chunks, chunks, f32(NVIEW, 16, ROWS), f32(2, NVIEW, 8, COPIES),
            f32(16, NBLK * CAP), f32(8, NBLK * CAP), bf16(128, NBLK * CAP), bf16(128, NBLK * CAP), bf16(128, NBLK * CAP), f32(NPAR, ROWS), f32(NPAR, COPIES),
            pltpu.SemaphoreType.REGULAR, dma((12,)), dma((8,)), dma((3,)), dma((3,)), dma((2,)), dma((2,)), dma((2,)), dma((2,)),
            dma((3,)), dma((3,)), dma((2, 3)), dma((2, 3)),
        ],
        compiler_params=pltpu.CompilerParams(
            collective_id=0, has_side_effects=True, vmem_limit_bytes=56 * 1024 * 1024
        ),
        name="round",
    )(
        cameras, params, moment1, moment2, dual, z_copy, z_table,
        boundary_rows.reshape(1, COPIES), owner_block.reshape(1, COPIES), owner_slot.reshape(1, COPIES),
        tile_lists, tile_counts.reshape(1, TILES), target,
    )
    return pl.pallas_call(
        finish_kernel,
        out_shape=outs,
        in_specs=[anywhere()] * 5,
        out_specs=(anywhere(),) * 5,
        scratch_shapes=[f32(*out.shape) for out in outs] + [dma((8,)), dma((8,))],
        compiler_params=pltpu.CompilerParams(vmem_limit_bytes=56 * 1024 * 1024),
        name="finish",
    )(*results)


def solution(mesh):
    whole, both = P(None, "blocks"), ("blocks", "views")
    placed = (whole,) * 6 + (P("blocks"), P("blocks", None), P("blocks"))
    placed += (P(both, None), P(both), P(both, None), P(None, both))
    return jax.shard_map(local, mesh=mesh, in_specs=placed, out_specs=(whole,) * 5, check_vma=False)
```

```python
import functools

import jax
import jax.numpy as jnp
from jax import lax
from jax.experimental import pallas as pl
from jax.experimental.pallas import tpu as pltpu
from jax.sharding import PartitionSpec as P

LEARN = 0.05
BETA_ONE = 0.9
BETA_TWO = 0.999
EPSILON = 1e-08

NPAR = 59
GAUSS = 2048
COPIES = 1024
ROWS = 1024
TILES = 16
DEPTH = 32
PAIRS = TILES * DEPTH
PIXELS = 256
NBLK = 64
PLANE = 8
NVIEW = 4
CAP = 64
SHARE = 15
JOINT = NVIEW * PAIRS + COPIES
UNROLL = 32

F32 = jnp.float32
BF16 = jnp.bfloat16
I32 = jnp.int32
MESH = pl.DeviceIdType.MESH
NT = (((1,), (1,)), ((), ()))


def lane_gather(source, index):
    low = index & 127
    high = index >> 7
    found = jnp.take_along_axis(source[0], low, axis=1)
    for g in range(1, len(source)):
        found = jnp.where(high == g, jnp.take_along_axis(source[g], low, axis=1), found)
    return found


def groups_of(value, rows):
    return [value[rows : rows + 8, 128 * g : 128 * (g + 1)] for g in range(value.shape[1] // 128)]


def fetch(value, rows, index):
    source = groups_of(value, rows)
    found = [lane_gather(source, wide(index[:, 128 * j : 128 * (j + 1)])) for j in range(index.shape[1] // 128)]
    return jnp.concatenate(found, axis=1)


def wide(row):
    return jnp.broadcast_to(row, (8, row.shape[1]))


def split(value):
    high = value.astype(BF16)
    return high, (value - high.astype(F32)).astype(BF16)


def share_of(ref, view):
    parts = []
    for v in range(NVIEW):
        end = min(SHARE * v + SHARE, NPAR)
        rows = [ref[SHARE * v : SHARE * v + 7, :], jnp.zeros((1, ref.shape[1]), F32), ref[SHARE * v + 7 : end, :]]
        if end < SHARE * v + SHARE:
            rows.append(jnp.zeros((SHARE * v + SHARE - end, ref.shape[1]), F32))
        parts.append(jnp.concatenate(rows, axis=0))
    result = parts[3]
    for v in range(3):
        result = jnp.where(view == v, parts[v], result)
    return result


def assemble(target, part, v, wave):
    start = SHARE * v + 7 * wave
    count = min(7 + wave, NPAR - start)
    target[start : start + count, :] = part[0:count, :]


def render(cam, params, lists, counts, target, table, sheet, goal, e_all, t_all, parts):
    table[0:11, :] = params[0:11, :]
    table[14:16, :] = jnp.zeros((2, GAUSS), F32)
    for c in range(3):
        colour = cam[0, 8] * params[11 + 16 * c : 12 + 16 * c, :]
        for k in range(1, 16):
            row = 11 + 16 * c + k
            colour += cam[0, 8 + k] * params[row : row + 1, :]
        table[11 + c : 12 + c, :] = colour + 0.5
    for c in range(3):
        for t in range(TILES):
            goal[16 * c + t : 16 * c + t + 1, :] = target[c : c + 1, PIXELS * t : PIXELS * (t + 1)]

    turned = lists[...].astype(F32).T
    slots = lax.broadcasted_iota(I32, (DEPTH, TILES), 0)
    turned = jnp.where(slots < counts[...], turned, turned + GAUSS)
    turned = jnp.concatenate([turned, jnp.zeros((DEPTH, 128 - TILES), F32)], axis=1)
    turns = [turned] + [pltpu.roll(turned, TILES * m, 1) for m in range(1, 8)]
    lane = lax.broadcasted_iota(I32, (1, 128), 1)
    pieces = []
    for j in range(PAIRS // 128):
        row = turns[0][8 * j : 8 * j + 1, :]
        for m in range(1, 8):
            row = jnp.where(lane >> 4 == m, turns[m][8 * j + m : 8 * j + m + 1, :], row)
        pieces.append(row)
    coded = jnp.concatenate(pieces, axis=1).astype(I32)
    live = jnp.where(coded < GAUSS, 1.0, 0.0)
    index = coded & (GAUSS - 1)
    picked = []
    for j in range(PAIRS // 128):
        lanes = wide(index[:, 128 * j : 128 * (j + 1)])
        picked.append(jnp.concatenate([lane_gather(groups_of(table, 8 * n), lanes) for n in range(2)], axis=0))
    picked = jnp.concatenate(picked, axis=1)

    def take(row):
        return picked[row : row + 1, :]

    jac = [[cam[0, 3 * i + j] for j in range(3)] for i in range(2)]
    centre = [take(j) for j in range(3)]
    scale = [jnp.exp(take(3 + k)) for k in range(3)]
    quat = [take(6 + k) for k in range(4)]
    norm = 1.0 / jnp.sqrt(quat[0] * quat[0] + quat[1] * quat[1] + quat[2] * quat[2] + quat[3] * quat[3])
    qw, qx, qy, qz = [q * norm for q in quat]
    rot = [
        [1 - 2 * (qy * qy + qz * qz), 2 * (qx * qy - qw * qz), 2 * (qx * qz + qw * qy)],
        [2 * (qx * qy + qw * qz), 1 - 2 * (qx * qx + qz * qz), 2 * (qy * qz - qw * qx)],
        [2 * (qx * qz - qw * qy), 2 * (qy * qz + qw * qx), 1 - 2 * (qx * qx + qy * qy)],
    ]
    mixed = [
        [(jac[i][0] * rot[0][k] + jac[i][1] * rot[1][k] + jac[i][2] * rot[2][k]) * scale[k] for k in range(3)]
        for i in range(2)
    ]

    def inner(a, b):
        return a[0] * b[0] + a[1] * b[1] + a[2] * b[2]

    first = inner(mixed[0], mixed[0]) + 0.01
    second = inner(mixed[1], mixed[1]) + 0.01
    cross = inner(mixed[0], mixed[1])
    det = first * second - cross * cross
    con0, con1, con2 = second / det, -cross / det, first / det
    cu = inner(jac[0], centre) + cam[0, 6]
    cw = inner(jac[1], centre) + cam[0, 7]
    opacity = 1.0 / (1.0 + jnp.exp(-take(10)))
    shown = opacity * live

    rows = [cu, cw, con0, 2.0 * con1, con2, shown, take(11), take(12), take(13)]
    rows = jnp.concatenate(rows + [jnp.zeros((7, PAIRS), F32)], axis=0)
    sheet[...] = rows.T

    tile = lax.broadcasted_iota(I32, (TILES, PIXELS), 0)
    pixel = lax.broadcasted_iota(I32, (TILES, PIXELS), 1)
    pos_u = (((tile & 3) * 16 + (pixel & 15)).astype(F32) + 0.5) / 32.0 - 1.0
    pos_w = (((tile >> 2) * 16 + (pixel >> 4)).astype(F32) + 0.5) / 32.0 - 1.0

    def at_slot(s):
        return pl.ds(pl.multiple_of(TILES * s, TILES), TILES)

    def column(s, f):
        return jnp.broadcast_to(sheet[at_slot(s), f : f + 1], (TILES, PIXELS))

    def forward(step, state):
        image, passed = list(state[0:3]), state[3]
        for s in [UNROLL * step + n for n in range(UNROLL)]:
            du = pos_u - column(s, 0)
            dw = pos_w - column(s, 1)
            quad = (column(s, 2) * du + column(s, 3) * dw) * du + column(s, 4) * dw * dw
            bell = jnp.exp(-0.5 * quad)
            alpha = jnp.minimum(column(s, 5) * bell, 0.99)
            weight = alpha * passed
            for c in range(3):
                image[c] = image[c] + column(s, 6 + c) * weight
            e_all[at_slot(s), :] = bell
            t_all[at_slot(s), :] = passed
            passed = passed - weight
        return (*image, passed)

    zero = jnp.zeros((TILES, PIXELS), F32)
    image = lax.fori_loop(0, DEPTH // UNROLL, forward, (zero, zero, zero, zero + 1.0))
    diff = [image[c] - goal[16 * c : 16 * c + 16, :] for c in range(3)]

    def backward(step, behind):
        for s in [DEPTH - 1 - UNROLL * step - n for n in range(UNROLL)]:
            bell = e_all[at_slot(s), :]
            before = t_all[at_slot(s), :]
            raw = column(s, 5) * bell
            alpha = jnp.minimum(raw, 0.99)
            glow = diff[0] * column(s, 6) + diff[1] * column(s, 7) + diff[2] * column(s, 8)
            slope = before * (glow - behind)
            slope = jnp.where(raw < 0.99, slope, jnp.where(raw == 0.99, 0.5 * slope, 0.0))
            behind = behind + alpha * (glow - behind)
            weight = alpha * before
            sums = [-0.5 * raw * slope, bell * slope] + [diff[c] * weight for c in range(3)]
            for n, value in enumerate(sums):
                high, low = split(value)
                parts[2 * n, at_slot(s), :] = high
                parts[2 * n + 1, at_slot(s), :] = low
        return behind

    lax.fori_loop(0, DEPTH // UNROLL, backward, zero)

    which = lax.broadcasted_iota(I32, (16, PIXELS), 0)
    place = lax.broadcasted_iota(I32, (16, PIXELS), 1)
    in_u = ((place & 15).astype(F32) - 7.5) / 32.0
    in_w = ((place >> 4).astype(F32) - 7.5) / 32.0
    basis = jnp.where(which == 0, 1.0, 0.0)
    basis = jnp.where(which == 1, in_u, basis)
    basis = jnp.where(which == 2, in_w, basis)
    basis = jnp.where(which == 3, in_u * in_u, basis)
    basis = jnp.where(which == 4, in_u * in_w, basis)
    basis = jnp.where(which == 5, in_w * in_w, basis)
    basis = basis.astype(BF16)

    def over_pixels(n):
        return lax.dot_general(basis, parts[2 * n], NT, preferred_element_type=F32) + lax.dot_general(
            basis, parts[2 * n + 1], NT, preferred_element_type=F32
        )

    moments = over_pixels(0)
    m1, mu, mw, muu, muw, mww = [moments[n : n + 1, :] for n in range(6)]
    g_opacity = over_pixels(1)[0:1, :] * live
    g_colour = [over_pixels(2 + c)[0:1, :] for c in range(3)]
    at = lax.broadcasted_iota(I32, (1, PAIRS), 1) & 15
    off_u = cu - (((at & 3) * 16 + 8).astype(F32) / 32.0 - 1.0)
    off_w = cw - (((at >> 2) * 16 + 8).astype(F32) / 32.0 - 1.0)
    s_u = mu - off_u * m1
    s_w = mw - off_w * m1
    g_con0 = muu - off_u * (mu + s_u)
    g_con1 = 2.0 * (muw - off_u * mw - off_w * s_u)
    g_con2 = mww - off_w * (mw + s_w)
    g_cu = -2.0 * (con0 * s_u + con1 * s_w)
    g_cw = -2.0 * (con1 * s_u + con2 * s_w)

    g_first = -(con0 * con0 * g_con0 + con0 * con1 * g_con1 + con1 * con1 * g_con2)
    g_second = -(con1 * con1 * g_con0 + con1 * con2 * g_con1 + con2 * con2 * g_con2)
    g_cross = -(2.0 * con0 * con1 * g_con0 + (con0 * con2 + con1 * con1) * g_con1 + 2.0 * con1 * con2 * g_con2)
    g_mixed = [
        [2.0 * g_first * mixed[0][k] + g_cross * mixed[1][k] for k in range(3)],
        [2.0 * g_second * mixed[1][k] + g_cross * mixed[0][k] for k in range(3)],
    ]
    g_scale = [g_mixed[0][k] * mixed[0][k] + g_mixed[1][k] * mixed[1][k] for k in range(3)]
    r = [
        [(jac[0][j] * g_mixed[0][k] + jac[1][j] * g_mixed[1][k]) * scale[k] for k in range(3)] for j in range(3)
    ]
    h_w = 2 * (qz * (r[1][0] - r[0][1]) + qy * (r[0][2] - r[2][0]) + qx * (r[2][1] - r[1][2]))
    h_x = 2 * (
        qy * (r[0][1] + r[1][0]) + qz * (r[0][2] + r[2][0]) + qw * (r[2][1] - r[1][2]) - 2 * qx * (r[1][1] + r[2][2])
    )
    h_y = 2 * (
        qx * (r[0][1] + r[1][0]) + qz * (r[1][2] + r[2][1]) + qw * (r[0][2] - r[2][0]) - 2 * qy * (r[0][0] + r[2][2])
    )
    h_z = 2 * (
        qx * (r[0][2] + r[2][0]) + qy * (r[1][2] + r[2][1]) + qw * (r[1][0] - r[0][1]) - 2 * qz * (r[0][0] + r[1][1])
    )
    along = qw * h_w + qx * h_x + qy * h_y + qz * h_z
    g_quat = [(h - q * along) * norm for h, q in ((h_w, qw), (h_x, qx), (h_y, qy), (h_z, qz))]
    g_centre = [jac[0][j] * g_cu + jac[1][j] * g_cw for j in range(3)]
    g_logit = g_opacity * opacity * (1.0 - opacity)
    along_row = lax.broadcasted_iota(I32, (1, PAIRS), 1)
    colbasis = jnp.zeros((1, PAIRS), F32)
    for k in range(16):
        colbasis = jnp.where(along_row == k, cam[0, 8 + k], colbasis)
    sent = g_centre + g_scale + g_quat + [g_logit] + g_colour + [index.astype(F32), colbasis]
    return jnp.concatenate(sent, axis=0)


def to_blocks(outgoing, incoming, send_sem, recv_sem, block, wave):
    def one(k, _):
        other = (block + k) % NBLK
        pltpu.make_async_remote_copy(
            src_ref=outgoing.at[wave, other],
            dst_ref=incoming.at[wave, block],
            send_sem=send_sem.at[wave],
            recv_sem=recv_sem.at[wave],
            device_id={"blocks": other},
            device_id_type=MESH,
        ).start()
        return 0

    lax.fori_loop(1, NBLK, one, 0)
    incoming[wave, block] = outgoing[wave, block]


def wait_blocks(outgoing, incoming, send_sem, recv_sem, block, wave):
    whole = pltpu.make_async_remote_copy(
        src_ref=outgoing.at[wave, pl.ds(0, NBLK - 1)],
        dst_ref=incoming.at[wave, pl.ds(0, NBLK - 1)],
        send_sem=send_sem.at[wave],
        recv_sem=recv_sem.at[wave],
        device_id={"blocks": block},
        device_id_type=MESH,
    )
    whole.wait_send()
    whole.wait_recv()


def to_views(piece, send_sem, recv_sem, view, there=None):
    copies = []
    for k in range(1, NVIEW):
        copy = pltpu.make_async_remote_copy(
            src_ref=piece,
            dst_ref=piece if there is None else there,
            send_sem=send_sem.at[k - 1],
            recv_sem=recv_sem.at[k - 1],
            device_id={"views": (view + k) % NVIEW},
            device_id_type=MESH,
        )
        copy.start()
        copies.append(copy)
    return copies


def refold(value):
    left = lax.broadcasted_iota(I32, (8, 128), 1) < CAP
    upper = lax.broadcasted_iota(I32, (8, 128), 0) < 4
    return jnp.where(left == upper, value, pltpu.roll(pltpu.roll(value, CAP, 1), 4, 0))


def pack(queue, chunks, wave):
    for j in range(NBLK // 2):
        folded = refold(queue[:, 128 * j : 128 * (j + 1)])
        chunks[wave, 2 * j] = folded[0:4]
        chunks[wave, 2 * j + 1] = folded[4:8]


def unpack(chunks, wave, j):
    return refold(jnp.concatenate([chunks[wave, 2 * j], chunks[wave, 2 * j + 1]], axis=0))


def adam(value, first, second, grad):
    first = BETA_ONE * first + (1.0 - BETA_ONE) * grad
    second = BETA_TWO * second + (1.0 - BETA_TWO) * grad * grad
    mhat = first * (1.0 / (1.0 - BETA_ONE**10))
    vhat = second * (1.0 / (1.0 - BETA_TWO**10))
    return value - LEARN * mhat / (jnp.sqrt(vhat) + EPSILON), first, second


def round_kernel(
    cam, params_in, moment1_in, moment2_in, dual_in, z_copy_in, z_table_in, rows_in, owner_in, slot_in,
    lists_in, counts_in, target_in,
    params_out, moment1_out, moment2_out, z_out, d_out,
    params, moment1, moment2, dual, z_copy, z_table, rows, owner, slot, lists, counts, target,
    table, sheet, goal, e_all, t_all, parts, gathered,
    left, masks, masked, pen_masked, onehot, source, names, place, s_value, s_first, s_second, s_dual, s_table,
    send, got, answers, returned, z_parts, d_own, items, queue, item_masks, item_masked, item_hot, z_new,
    planes_in, in_sem, out_sem, s_mine, r_mine, s_send, r_send, s_back, r_back, s_z, r_z, s_d, r_d,
):
    block = lax.axis_index("blocks")
    view = lax.axis_index("views")

    pairs = [
        (lists_in, lists), (counts_in, counts), (params_in, params), (target_in, target),
        (rows_in, rows), (owner_in, owner), (slot_in, slot), (dual_in, dual), (z_copy_in, z_copy),
        (moment1_in, moment1), (moment2_in, moment2), (z_table_in, z_table),
    ]
    arriving = [pltpu.make_async_copy(there, here, in_sem.at[n]) for n, (there, here) in enumerate(pairs)]
    for copy in arriving[0:4]:
        copy.start()
    barrier = pltpu.get_barrier_semaphore()
    plane, place_in = block // PLANE, block % PLANE
    beside = [plane * PLANE + (place_in + k) % PLANE for k in range(1, PLANE)]
    across = [(block + PLANE * k) % NBLK for k in range(1, NBLK // PLANE)]
    for other in beside + across:
        pl.semaphore_signal(barrier, inc=1, device_id={"blocks": other}, device_id_type=MESH)
    for k in range(1, NVIEW):
        pl.semaphore_signal(barrier, inc=1, device_id={"views": (view + k) % NVIEW}, device_id_type=MESH)
    for copy in arriving[0:4]:
        copy.wait()
    for copy in arriving[4:]:
        copy.start()
    gathered[view] = render(cam, params, lists, counts, target, table, sheet, goal, e_all, t_all, parts)
    pl.semaphore_wait(barrier, len(beside) + len(across) + NVIEW - 1)
    view_copies = to_views(gathered.at[view], s_mine, r_mine, view)
    for other in across:
        pl.semaphore_signal(planes_in, inc=1, device_id={"blocks": other}, device_id_type=MESH)

    for copy in arriving[4:]:
        copy.wait()
    owned = lax.broadcasted_iota(I32, (NBLK, COPIES), 0) == owner[...]
    owned = jnp.where(owned, 1.0, 0.0)
    upper = lax.broadcasted_iota(I32, (128, 128), 0) < lax.broadcasted_iota(I32, (128, 128), 1)
    upper = jnp.where(upper, 1.0, 0.0).astype(BF16)
    ranks = []
    carry = jnp.zeros((NBLK, 1), F32)
    for j in range(COPIES // 128):
        part = owned[:, 128 * j : 128 * (j + 1)]
        ahead = jnp.dot(part.astype(BF16), upper, preferred_element_type=F32) + carry
        ranks.append(jnp.sum(part * ahead, axis=0, keepdims=True))
        carry = carry + jnp.sum(part, axis=1, keepdims=True)
    rank = jnp.concatenate(ranks, axis=1).astype(I32)
    place[...] = owner[...] * CAP + rank
    ident = lax.broadcasted_iota(I32, (1, COPIES), 1)
    ranked = (lax.broadcasted_iota(I32, (128, COPIES), 0) & (CAP - 1)) == rank
    coarse = jnp.where(ranked, (ident >> 5).astype(F32), 0.0).astype(BF16)
    fine = jnp.where(ranked, ((ident & 31) + 1).astype(F32), 0.0).astype(BF16)
    owned = owned.astype(BF16)
    names[...] = (
        32.0 * lax.dot_general(owned, coarse, NT, preferred_element_type=F32)
        + lax.dot_general(owned, fine, NT, preferred_element_type=F32)
    ).astype(I32)

    boundary = rows[...]
    lanes = slice(NVIEW * PAIRS, JOINT)
    left[NPAR:64, :] = jnp.zeros((64 - NPAR, JOINT), F32)
    left[0:NPAR, lanes] = dual[...] - z_copy[...]
    left[NPAR : NPAR + 1, lanes] = jnp.ones((1, COPIES), F32)

    def prepare(index, lanes):
        width = index.shape[1]
        group = jnp.broadcast_to(index >> 8, (16, width))
        for h in range(8):
            masks[16 * h : 16 * h + 16, lanes] = jnp.where(group == h, 1.0, 0.0).astype(BF16)
        hot = lax.broadcasted_iota(I32, (256, width), 0) == (index & 255)
        onehot[:, lanes] = jnp.where(hot, 1.0, 0.0).astype(BF16)

    prepare(boundary, lanes)

    s_value[...] = share_of(params, view)
    s_first[...] = share_of(moment1, view)
    s_second[...] = share_of(moment2, view)
    s_dual[...] = share_of(dual, view)
    s_table[...] = share_of(z_table, view)

    def share_masked(target, value, at):
        high, low = split(value)
        for h in range(8):
            mask = masks[16 * h : 16 * h + 16, at]
            target[32 * h : 32 * h + 16, :] = high * mask
            target[32 * h + 16 : 32 * h + 32, :] = low * mask

    spot = lax.broadcasted_iota(I32, (16, COPIES), 0)
    share_masked(pen_masked, jnp.where(spot == 7, 1.0, share_of(left.at[:, lanes], view)), lanes)
    pen_total = lax.dot_general(pen_masked[...], onehot[:, lanes], NT, preferred_element_type=F32)

    for copy in view_copies:
        copy.wait()
    pl.semaphore_wait(planes_in, len(across))
    diagonal = lax.broadcasted_iota(I32, (16, 128), 0) == lax.broadcasted_iota(I32, (16, 128), 1)
    for v in range(NVIEW):
        lanes = slice(PAIRS * v, PAIRS * (v + 1))
        left[0:11, lanes] = gathered[v, 0:11, :]
        colbasis = jnp.sum(jnp.where(diagonal, gathered[v, 15:16, 0:128], 0.0), axis=1, keepdims=True)
        for c in range(3):
            left[11 + 16 * c : 27 + 16 * c, lanes] = colbasis * gathered[v, 11 + c : 12 + c, :]
        prepare(gathered[v, 14:15, :].astype(I32), lanes)

    lanes = slice(0, NVIEW * PAIRS)
    view_masked = masked.at[0:256, lanes]
    share_masked(view_masked, share_of(left.at[:, lanes], view), lanes)
    total = pen_total + lax.dot_general(view_masked[...], onehot[:, lanes], NT, preferred_element_type=F32)
    moved = []
    for h in range(8):
        both = total[32 * h : 32 * h + 16, :] + total[32 * h + 16 : 32 * h + 32, :]
        lanes = slice(256 * h, 256 * (h + 1))
        value = s_value[:, lanes]
        grad = both + both[7:8, :] * value
        moved.append(adam(value, s_first[:, lanes], s_second[:, lanes], grad)[0])
    moved = jnp.concatenate(moved, axis=1)
    lane = lax.broadcasted_iota(I32, (8, 128), 1)
    spot = lax.broadcasted_iota(I32, (8, COPIES), 0)
    for wave in range(2):
        at = slice(8 * wave, 8 * wave + 8)
        sums = fetch(moved, 8 * wave, boundary) + s_dual[at, :]
        if wave == 0:
            sums = jnp.where(spot == 7, (slot[...] + 1).astype(F32), sums)
        source[at, :] = sums
        blocks_of = groups_of(source, 8 * wave)
        for j in range(NBLK // 2):
            name = jnp.where(lane < CAP, wide(names[2 * j : 2 * j + 1, :]), wide(names[2 * j + 1 : 2 * j + 2, :]))
            found = lane_gather(blocks_of, jnp.maximum(name - 1, 0))
            queue[:, 128 * j : 128 * (j + 1)] = jnp.where(name > 0, found, 0.0)
        pack(queue, send, wave)
        to_blocks(send, got, s_send, r_send, block, wave)

    leaving = []

    def step_half(half):
        high, low = split(left[...])
        for n in range(4):
            mask = masks[64 * half + 16 * n : 64 * half + 16 * n + 16, :]
            for part in range(4):
                rows_at = slice(16 * part, 16 * part + 16)
                masked[128 * n + 16 * part : 128 * n + 16 * part + 16, :] = high[rows_at, :] * mask
                masked[128 * n + 64 + 16 * part : 128 * n + 80 + 16 * part, :] = low[rows_at, :] * mask
        total = lax.dot_general(masked[...], onehot[...], NT, preferred_element_type=F32)
        for n in range(4):
            both = total[128 * n : 128 * n + 64, :] + total[128 * n + 64 : 128 * n + 128, :]
            lanes = slice(1024 * half + 256 * n, 1024 * half + 256 * (n + 1))
            value = params[:, lanes]
            grad = both[0:NPAR] + both[NPAR : NPAR + 1] * value
            params[:, lanes], moment1[:, lanes], moment2[:, lanes] = adam(
                value, moment1[:, lanes], moment2[:, lanes], grad
            )
        lanes = pl.ds(1024 * half, 1024)
        for n, (here, there) in enumerate([(params, params_out), (moment1, moment1_out), (moment2, moment2_out)]):
            copy = pltpu.make_async_copy(here.at[:, lanes], there.at[:, lanes], out_sem.at[3 * half + n])
            copy.start()
            leaving.append(copy)

    step_half(0)

    last = lax.broadcasted_iota(I32, (8, NBLK * CAP), 0) == 7
    for wave in range(2):
        at = slice(8 * wave, 8 * wave + 8)
        wait_blocks(send, got, s_send, r_send, block, wave)
        for j in range(NBLK // 2):
            items[at, 128 * j : 128 * (j + 1)] = unpack(got, wave, j)
        value = items[at, :]
        if wave == 0:
            label = items[7:8, :].astype(I32)
            index = jnp.maximum(label - 1, 0)
            group = jnp.broadcast_to(jnp.where(label > 0, index >> 7, 8), (16, NBLK * CAP))
            for h in range(8):
                item_masks[16 * h : 16 * h + 16, :] = jnp.where(group == h, 1.0, 0.0).astype(BF16)
            hot = lax.broadcasted_iota(I32, (128, NBLK * CAP), 0) == (index & 127)
            item_hot[...] = jnp.where(hot, 1.0, 0.0).astype(BF16)
            value = jnp.where(last, 1.0, value)
        high = value.astype(BF16).astype(F32)
        both = jnp.concatenate([high, value - high], axis=0).astype(BF16)
        for h in range(8):
            item_masked[16 * h : 16 * h + 16, :] = both * item_masks[16 * h : 16 * h + 16, :]
        total = lax.dot_general(item_masked[...], item_hot[...], NT, preferred_element_type=F32)
        total = jnp.concatenate([total[16 * h : 16 * h + 8, :] + total[16 * h + 8 : 16 * h + 16, :] for h in range(8)], axis=1)
        if wave == 0:
            number = 1.0 + total[7:8, :]
        fresh = (s_table[at, :] + total) / number
        z_parts[view, at, :] = fresh
        answer = groups_of(fresh, 0)
        for j in range(NBLK // 2):
            queue[:, 128 * j : 128 * (j + 1)] = lane_gather(answer, wide(index[:, 128 * j : 128 * (j + 1)]))
        pack(queue, answers, wave)
        to_blocks(answers, returned, s_back, r_back, block, wave)
    z_copies = to_views(z_parts.at[view], s_z, r_z, view)
    step_half(1)

    d_copies = []
    for wave in range(2):
        at = slice(8 * wave, 8 * wave + 8)
        wait_blocks(answers, returned, s_back, r_back, block, wave)
        for j in range(NBLK // 2):
            items[at, 128 * j : 128 * (j + 1)] = unpack(returned, wave, j)
        d_own[wave] = source[at, :] - fetch(items, 8 * wave, place)
        d_copies += to_views(d_own.at[wave], s_d.at[wave], r_d.at[wave], view, d_out.at[wave, view])
        leaving.append(pltpu.make_async_copy(d_own.at[wave], d_out.at[wave, view], out_sem.at[7 + wave]))
        leaving[-1].start()
        if wave == 0:
            for copy in z_copies:
                copy.wait()
            for v in range(NVIEW):
                for part in range(2):
                    assemble(z_new, z_parts.at[v, 8 * part : 8 * part + 8], v, part)
            leaving.append(pltpu.make_async_copy(z_new, z_out, out_sem.at[6]))
            leaving[-1].start()
    for copy in d_copies:
        copy.wait()
    for copy in leaving:
        copy.wait()


def finish_kernel(*refs):
    sources, targets, staged, dual_new, in_sem, out_sem = refs[0:5], refs[5:10], refs[10:15], refs[15], refs[16], refs[17]
    parts = pltpu.make_async_copy(sources[4], staged[4], in_sem.at[7])
    duals = pltpu.make_async_copy(dual_new, targets[4], out_sem.at[7])
    steps = []
    for n, ref in enumerate(sources[0:4]):
        for piece in range(ref.shape[1] // ROWS):
            lanes = pl.ds(ROWS * piece, ROWS)
            at = len(steps)
            steps.append(
                (
                    pltpu.make_async_copy(ref.at[:, lanes], staged[n].at[:, lanes], in_sem.at[at]),
                    pltpu.make_async_copy(staged[n].at[:, lanes], targets[n].at[:, lanes], out_sem.at[at]),
                )
            )
    parts.start()
    for arrive, _ in steps:
        arrive.start()
    for n, (arrive, leave) in enumerate(steps):
        arrive.wait()
        leave.start()
        if n == 2:
            parts.wait()
            for v in range(NVIEW):
                for wave in range(2):
                    assemble(dual_new, staged[4].at[wave, v], v, wave)
            duals.start()
    for _, leave in steps:
        leave.wait()
    duals.wait()


def anywhere():
    return pl.BlockSpec(memory_space=pl.ANY)


def local(
    params, moment1, moment2, dual, z_copy, z_table, boundary_rows, owner_block, owner_slot,
    tile_lists, tile_counts, cameras, target,
):
    shape = jax.ShapeDtypeStruct
    outs = (shape((NPAR, GAUSS), F32),) * 3 + (shape((NPAR, ROWS), F32), shape((NPAR, COPIES), F32))

    def f32(*dims):
        return pltpu.VMEM(dims, F32)

    def bf16(*dims):
        return pltpu.VMEM(dims, BF16)

    def i32(*dims):
        return pltpu.VMEM(dims, I32)

    parts = shape((2, NVIEW, 8, COPIES), F32)
    chunks = f32(2, NBLK, 4, 128)
    dma = pltpu.SemaphoreType.DMA
    results = pl.pallas_call(
        round_kernel,
        out_shape=(*outs[0:4], parts),
        in_specs=[pl.BlockSpec(memory_space=pltpu.SMEM)] + [anywhere()] * 12,
        out_specs=(anywhere(),) * 5,
        scratch_shapes=[
            f32(NPAR, GAUSS), f32(NPAR, GAUSS), f32(NPAR, GAUSS),
            f32(NPAR, COPIES), f32(NPAR, COPIES), f32(NPAR, ROWS),
            i32(1, COPIES), i32(1, COPIES), i32(1, COPIES), i32(TILES, DEPTH), i32(1, TILES), f32(3, TILES * PIXELS),
            f32(16, GAUSS), f32(PAIRS, 16), f32(48, PIXELS), f32(PAIRS, PIXELS), f32(PAIRS, PIXELS),
            bf16(10, PAIRS, PIXELS), f32(NVIEW, 16, PAIRS),
            f32(64, JOINT), bf16(128, JOINT), bf16(512, JOINT), bf16(256, COPIES), bf16(256, JOINT),
            f32(16, COPIES), i32(NBLK, 128), i32(1, COPIES),
            f32(16, GAUSS), f32(16, GAUSS), f32(16, GAUSS), f32(16, COPIES), f32(16, ROWS),
            chunks, chunks, chunks, chunks, f32(NVIEW, 16, ROWS), f32(2, 8, COPIES),
            f32(16, NBLK * CAP), f32(8, NBLK * CAP), bf16(128, NBLK * CAP), bf16(128, NBLK * CAP), bf16(128, NBLK * CAP), f32(NPAR, ROWS),
            pltpu.SemaphoreType.REGULAR, dma((12,)), dma((9,)), dma((3,)), dma((3,)), dma((2,)), dma((2,)), dma((2,)), dma((2,)),
            dma((3,)), dma((3,)), dma((2, 3)), dma((2, 3)),
        ],
        compiler_params=pltpu.CompilerParams(
            collective_id=0, has_side_effects=True, vmem_limit_bytes=56 * 1024 * 1024
        ),
        name="round",
    )(
        cameras, params, moment1, moment2, dual, z_copy, z_table,
        boundary_rows.reshape(1, COPIES), owner_block.reshape(1, COPIES), owner_slot.reshape(1, COPIES),
        tile_lists, tile_counts.reshape(1, TILES), target,
    )
    return pl.pallas_call(
        finish_kernel,
        out_shape=outs,
        in_specs=[anywhere()] * 5,
        out_specs=(anywhere(),) * 5,
        scratch_shapes=[f32(*out.shape) for out in (*outs[0:4], parts, outs[4])] + [dma((8,)), dma((8,))],
        compiler_params=pltpu.CompilerParams(vmem_limit_bytes=56 * 1024 * 1024),
        name="finish",
    )(*results)


def solution(mesh):
    whole, both = P(None, "blocks"), ("blocks", "views")
    placed = (whole,) * 6 + (P("blocks"), P("blocks", None), P("blocks"))
    placed += (P(both, None), P(both), P(both, None), P(None, both))
    return jax.shard_map(local, mesh=mesh, in_specs=placed, out_specs=(whole,) * 5, check_vma=False)
```
